32 devices in a mesh: shard: 8 (over z, y), tensor: 4 (over x, core).
Axes of the slice: x: 2, y: 2, z: 4, core: 2. Of those that a mesh axis runs over, the one named last changes fastest.
Arguments:
- gradient: float32 [384, 4, 3456], P('shard', 'tensor'), may hold values from -6 to 6
- weight: float32 [384, 4, 3456], P('shard', 'tensor'), may hold values from -0.3125 to 0.3125
- first_moment: float32 [384, 4, 3456], P('shard', 'tensor'), may hold values from -6 to 6
- second_moment: float32 [384, 4, 3456], P('shard', 'tensor'), may hold values from 0.3 to 3
- left_basis: float32 [384, 4, 960], P('shard', 'tensor')
- left_gram: float32 [384, 4, 960], P('shard', 'tensor'), as said below
- owner_table: int32 [2, 5], replicated, may hold values from 0 to 7, as said below
- bias_gradient: float32 [11520], P(('shard', 'tensor')), may hold values from -6 to 6
- bias_weight: float32 [11520], P(('shard', 'tensor')), may hold values from -3 to 3
- bias_first: float32 [11520], P(('shard', 'tensor')), may hold values from -6 to 6
- bias_second: float32 [11520], P(('shard', 'tensor')), may hold values from 0.3 to 3
Outputs:
- new_weight: float32 [384, 4, 3456], P('shard', 'tensor')
- new_first: float32 [384, 4, 3456], P('shard', 'tensor')
- new_second: float32 [384, 4, 3456], P('shard', 'tensor')
- owned_basis: float32 [8, 2, 384, 384], P('shard', None, None, 'tensor')
- owned_gram: float32 [8, 2, 384, 384], P('shard', None, None, 'tensor')
- bias_updated: float32 [11520], P(('shard', 'tensor'))
- bias_first_new: float32 [11520], P(('shard', 'tensor'))
- bias_second_new: float32 [11520], P(('shard', 'tensor'))
The draws below stay inside these ranges and needn't reach their ends.
Inputs may be any that keep to these rules, and one draw needn't show every extreme that they name: `owner_table`: every owner group that owns a matrix owns exactly 2, with at most 8 column tiles together, and some group has exactly 8; group 0 and the last group own matrices. `left_gram`: each matrix is symmetric.
All inputs are finite; a program needn't handle non-finite values.
Results may differ from the reference program's by a relative error of at most 0.0001.
Values sent between devices are 32-bit elements; how exact they have to be, the bound alone decides.
No kernel may reach another device: no remote copies, remote signals or barrier semaphores. Data moves between devices by JAX's collectives and lax.ppermute only.
A program may use at most 128 MiB of HBM per device.

```python
import math
import jax
import jax.numpy as jnp
from jax import lax

D = 384
LAYERS = 2
TILES = 36
MATS = 10
BIAS = 5760
MCAP = 2
STEP = 10
NS_STEPS = 5
N_SHARD = 8
N_TENSOR = 4


def relay_draw(tiles):
    count = tiles.shape[0]
    return tiles.reshape(count, D, N_TENSOR, D // N_TENSOR).transpose(1, 2, 0, 3).reshape(D, N_TENSOR, count * (D // N_TENSOR))


def draw_left_basis(key, part):
    noise = jax.random.normal(key, (MATS, D, D), jnp.float32)
    ident = (jnp.arange(D)[:, None] == jnp.arange(D)[None, :]).astype(jnp.float32)
    return relay_draw(ident[None] + 0.4 / math.sqrt(D) * noise)


def draw_left_gram(key, part):
    key_diag, key_off = jax.random.split(key)
    diag_vals = jnp.exp(jax.random.uniform(key_diag, (MATS, D), jnp.float32, math.log(100.0), math.log(3000.0)))
    off_vals = 30.0 * jax.random.normal(key_off, (MATS, D, D), jnp.float32)
    ident = (jnp.arange(D)[:, None] == jnp.arange(D)[None, :]).astype(jnp.float32)
    symmetric = 0.5 * (off_vals + off_vals.transpose(0, 2, 1))
    return relay_draw(symmetric * (1.0 - ident)[None] + diag_vals[:, :, None] * ident[None])


def draw_owner_table(key, part):
    used = 5 * LAYERS // 2
    key_pick, key_mix = jax.random.split(key)
    middle = jax.random.permutation(key_pick, jnp.arange(1, N_SHARD - 1, dtype=jnp.int32))[:used - 2]
    picked = jnp.concatenate([jnp.array([0, N_SHARD - 1], jnp.int32), middle])
    groups = jax.random.permutation(key_mix, picked).reshape(LAYERS // 2, 5)
    even_rows = jnp.stack([groups[:, 4], groups[:, 0], groups[:, 2], groups[:, 2], groups[:, 0]], axis=1)
    odd_rows = jnp.stack([groups[:, 4], groups[:, 1], groups[:, 3], groups[:, 3], groups[:, 1]], axis=1)
    return jnp.stack([even_rows, odd_rows], axis=1).reshape(LAYERS, 5).astype(jnp.int32)


def level_of(rng, extent, pieces, smallest, top_value):
    level, own = 1.0, jax.random.fold_in(rng, 6)
    for axis_at, shards_of in pieces:
        heights = jnp.exp(jax.random.uniform(jax.random.fold_in(own, axis_at), (shards_of,), jnp.float32, smallest / len(pieces), top_value / len(pieces)))
        level = level * jnp.repeat(heights, extent[axis_at] // shards_of).reshape([-1 if axis == axis_at else 1 for axis in range(len(extent))])
    return level


def normal_values(key, dims, width, reach, cuts=(), held_as=jnp.bfloat16):
    factor_of = level_of(key, dims, cuts, -0.22, 0.18) if cuts else 1.0
    values = jax.random.normal(key, dims, jnp.float32) * width * factor_of
    return jnp.minimum(jnp.maximum(values, -reach), reach).astype(held_as)


def setup_inputs(seed: int = 0) -> dict:
    splits = jax.random.split(jax.random.key(seed), 12)
    return {
        "gradient": normal_values(splits[0], (D, N_TENSOR, TILES * (D // N_TENSOR)), 1.0, 6.0, ((0, 8), (1, 4)), jnp.float32),
        "weight": normal_values(splits[1], (D, N_TENSOR, TILES * (D // N_TENSOR)), D ** -0.5, 0.3125, ((0, 8), (1, 4)), jnp.float32),
        "first_moment": normal_values(splits[2], (D, N_TENSOR, TILES * (D // N_TENSOR)), 1.0, 6.0, ((0, 8), (1, 4)), jnp.float32),
        "second_moment": jnp.clip(jnp.exp(math.log(3.0) - 2.3025851 * jax.random.uniform(splits[3], (D, N_TENSOR, TILES * (D // N_TENSOR)), jnp.float32) ** level_of(splits[3], (D, N_TENSOR, TILES * (D // N_TENSOR)), ((0, 8), (1, 4)), -0.2, 0.2)), 0.3, 3.0),
        "left_basis": draw_left_basis(jax.random.fold_in(splits[11], 71), 0),
        "left_gram": draw_left_gram(jax.random.fold_in(splits[11], 71), 0),
        "owner_table": draw_owner_table(jax.random.fold_in(splits[11], 71), 0),
        "bias_gradient": normal_values(splits[7], (LAYERS * BIAS,), 1.0, 6.0, ((0, 32),), jnp.float32),
        "bias_weight": normal_values(splits[8], (LAYERS * BIAS,), 0.5, 3.0, ((0, 32),), jnp.float32),
        "bias_first": normal_values(splits[9], (LAYERS * BIAS,), 1.0, 6.0, ((0, 32),), jnp.float32),
        "bias_second": jnp.clip(jnp.exp(math.log(3.0) - 2.3025851 * jax.random.uniform(splits[10], (LAYERS * BIAS,), jnp.float32) ** level_of(splits[10], (LAYERS * BIAS,), ((0, 32),), -0.2, 0.2)), 0.3, 3.0),
    }


TYPE_TILES = (3, 1, 4, 4, 6)
TYPE_START = (0, 3, 4, 8, 12)
HIGH = lax.Precision.HIGHEST

def adam_direction(moment_hat, second_new):
    corr_one = 1.0 - 0.9 ** STEP
    corr_two = 1.0 - 0.95 ** STEP
    return moment_hat / corr_one / (jnp.sqrt(second_new / corr_two) + 1e-08)

def unlay(packed):
    count = packed.shape[2] // (D // N_TENSOR)
    return packed.reshape(D, N_TENSOR, count, D // N_TENSOR).transpose(2, 0, 1, 3).reshape(count, D, D)

def relay(tiles):
    count = tiles.shape[0]
    return tiles.reshape(count, D, N_TENSOR, D // N_TENSOR).transpose(1, 2, 0, 3).reshape(D, N_TENSOR, count * (D // N_TENSOR))

def join_tiles(tiles):
    return tiles.transpose(1, 0, 2).reshape(tiles.shape[1], tiles.shape[0] * tiles.shape[2])

def split_tiles(matrix, tile_count):
    return matrix.reshape(matrix.shape[0], tile_count, matrix.shape[0]).transpose(1, 0, 2)

def refresh_basis(gram_new, basis):
    power = jnp.dot(gram_new, basis, precision=HIGH, preferred_element_type=jnp.float32)
    frame = power / jnp.sqrt(jnp.sum(power * power) + 1e-06)
    for sweep in range(NS_STEPS):
        square = jnp.dot(frame, frame.T, precision=HIGH, preferred_element_type=jnp.float32)
        frame = 1.5 * frame - 0.5 * jnp.dot(square, frame, precision=HIGH, preferred_element_type=jnp.float32)
    return frame

def slot_ranks(owner_table):
    owners = owner_table.reshape(-1).astype(jnp.int32)
    matrix_ids = jnp.arange(owners.shape[0], dtype=jnp.int32)
    earlier = (owners[:, None] == owners[None, :]) & (matrix_ids[None, :] < matrix_ids[:, None])
    return (owners, lax.optimization_barrier(jnp.sum(earlier.astype(jnp.int32), axis=1)).astype(jnp.int32))

def reference(gradient, weight, first_moment, second_moment, left_basis, left_gram, owner_table, bias_gradient, bias_weight, bias_first, bias_second):
    gradient = unlay(gradient)
    weight = unlay(weight)
    first_moment = unlay(first_moment)
    second_moment = unlay(second_moment)
    left_basis = unlay(left_basis)
    left_gram = unlay(left_gram)
    weight_list, first_list, second_list, basis_list, gram_list = ([], [], [], [], [])
    for layer_id in range(LAYERS):
        for kind_id in range(5):
            tile_count = TYPE_TILES[kind_id]
            first_tile = 18 * layer_id + TYPE_START[kind_id]
            matrix_id = 5 * layer_id + kind_id
            grad_mat = join_tiles(gradient[first_tile:first_tile + tile_count])
            weight_mat = join_tiles(weight[first_tile:first_tile + tile_count])
            first_mat = join_tiles(first_moment[first_tile:first_tile + tile_count])
            second_mat = join_tiles(second_moment[first_tile:first_tile + tile_count])
            basis = left_basis[matrix_id]
            gram = left_gram[matrix_id]
            moment_new = 0.9 * first_mat + 0.1 * grad_mat
            grad_hat = jnp.dot(basis.T, grad_mat, precision=HIGH, preferred_element_type=jnp.float32)
            moment_hat = jnp.dot(basis.T, moment_new, precision=HIGH, preferred_element_type=jnp.float32)
            second_new = 0.95 * second_mat + 0.05 * grad_hat * grad_hat
            direction = jnp.dot(basis, adam_direction(moment_hat, second_new), precision=HIGH, preferred_element_type=jnp.float32)
            weight_new = weight_mat - 0.01 * (direction + 0.1 * weight_mat)
            gram_new = 0.95 * gram + 0.05 * jnp.dot(grad_mat, grad_mat.T, precision=HIGH, preferred_element_type=jnp.float32)
            weight_list.append(split_tiles(weight_new, tile_count))
            first_list.append(split_tiles(moment_new, tile_count))
            second_list.append(split_tiles(second_new, tile_count))
            basis_list.append(refresh_basis(gram_new, basis))
            gram_list.append(gram_new)
    owners, ranks = slot_ranks(owner_table)
    owned_basis = jnp.zeros((N_SHARD, MCAP, D, D), jnp.float32).at[owners, ranks].set(jnp.stack(basis_list))
    owned_gram = jnp.zeros((N_SHARD, MCAP, D, D), jnp.float32).at[owners, ranks].set(jnp.stack(gram_list))
    bias_first_new = 0.9 * bias_first + 0.1 * bias_gradient
    bias_second_new = 0.95 * bias_second + 0.05 * bias_gradient * bias_gradient
    bias_updated = bias_weight - 0.01 * adam_direction(bias_first_new, bias_second_new)
    return (relay(jnp.concatenate(weight_list, axis=0)), relay(jnp.concatenate(first_list, axis=0)), relay(jnp.concatenate(second_list, axis=0)), owned_basis, owned_gram, bias_updated, bias_first_new, bias_second_new)
```

```python
import functools

import jax
import jax.numpy as jnp
import numpy as np
from jax import lax
from jax.experimental import pallas as pl
from jax.experimental.pallas import tpu as pltpu
from jax.sharding import PartitionSpec as P

MCAP = 2
STEP = 10
NS_STEPS = 5
TYPE_TILES = (3, 1, 4, 4, 6)
LANES = 128
F32 = jnp.float32
BF16 = jnp.bfloat16
CORR_ONE = 1.0 - 0.9**STEP
CORR_TWO = 1.0 - 0.95**STEP


def adam_direction(moment_hat, second_new):
    return moment_hat / CORR_ONE / (jnp.sqrt(second_new / CORR_TWO) + 1e-08)


def place_columns(layer_total, shards, columns):
    sizes = [tiles * columns for tiles in TYPE_TILES] * layer_total
    starts = np.concatenate([[0], np.cumsum(sizes)]).tolist()
    share = starts[-1] // shards
    assert share * shards == starts[-1]
    small = [i for i, size in enumerate(sizes) if size <= share]
    groups = [[] for _ in range(shards)]
    room = [share] * shards
    if len(small) <= shards:
        for group, i in enumerate(small):
            groups[group].append((i, starts[i], sizes[i]))
            room[group] -= sizes[i]
        rest = [i for i in range(len(sizes)) if i not in small]
    else:
        rest = list(range(len(sizes)))
    group = 0
    for i in rest:
        at, left = starts[i], sizes[i]
        while left:
            while not room[group]:
                group += 1
            take = min(left, room[group])
            groups[group].append((i, at, take))
            room[group] -= take
            at += take
            left -= take
    return groups, share


def block_form(rows, width):
    full, rest = divmod(width, LANES)
    padded = -(-rows // 8) * 8
    halved = 0 < rest <= LANES // 2 and rows % 16 == 0
    total = full * padded + (0 if not rest else rows // 2 if halved else padded)
    return full, rest, padded, halved, total


def store_block(ref, index, base, value, rows, width):
    full, rest, padded, halved, _ = block_form(rows, width)
    for j in range(full):
        at = base + j * padded
        ref[index, at : at + rows, :] = value[:, j * LANES : (j + 1) * LANES]
    if rest:
        at = base + full * padded
        tail = value[:, full * LANES : width]
        if halved:
            half = rows // 2
            ref[index, at : at + half, 0:rest] = tail[:half]
            ref[index, at : at + half, LANES // 2 : LANES // 2 + rest] = tail[half:]
        else:
            ref[index, at : at + rows, 0:rest] = tail


def load_pieces(ref, index, base, rows, width):
    full, rest, padded, halved, _ = block_form(rows, width)
    pieces = []
    for j in range(full):
        at = base + j * padded
        pieces.append(ref[index, at : at + rows, :])
    if rest:
        at = base + full * padded
        if halved:
            half = rows // 2
            block = ref[index, at : at + half, :]
            pieces.append(
                jnp.concatenate(
                    [block[:, 0:rest], block[:, LANES // 2 : LANES // 2 + rest]], axis=0
                )
            )
        else:
            pieces.append(ref[index, at : at + rows, 0:rest])
    return pieces


def load_block(ref, index, base, rows, width):
    pieces = load_pieces(ref, index, base, rows, width)
    return pieces[0] if len(pieces) == 1 else jnp.concatenate(pieces, axis=1)


def unpack_columns(ref, base, out_ref, shards, rows, width):
    if width % LANES:
        tail = width // LANES * LANES
        out_ref[:, tail:] = jnp.zeros((out_ref.shape[0], LANES), F32)
    for source in range(shards):
        for j, piece in enumerate(load_pieces(ref, source, base, rows, width)):
            lanes = piece.shape[1]
            out_ref[source * rows : (source + 1) * rows, j * LANES : j * LANES + lanes] = piece


def pack_columns(value_ref, ref, base, shards, rows, width):
    for dest in range(shards):
        block = value_ref[dest * rows : (dest + 1) * rows, 0:width]
        store_block(ref, dest, base, block, rows, width)


def parts_of(value):
    high = value.astype(BF16)
    return high, (value - high.astype(F32)).astype(BF16)


def product(left, right, contract=(1, 0)):
    dims = (((contract[0],), (contract[1],)), ((), ()))
    dot = functools.partial(lax.dot_general, dimension_numbers=dims, preferred_element_type=F32)
    return dot(left[0], right[0]) + (dot(left[0], right[1]) + dot(left[1], right[0]))


def call(kernel, outs, args, specs=None, out_specs=None, scratch=(), aliases=None, grid=()):
    single = isinstance(outs, tuple)
    shapes = [outs] if single else list(outs)
    shapes = [s if isinstance(s, jax.ShapeDtypeStruct) else jax.ShapeDtypeStruct(s, F32) for s in shapes]
    vmem = pl.BlockSpec(memory_space=pltpu.VMEM)
    specs = specs or [None] * len(args)
    result = pl.pallas_call(
        kernel,
        out_shape=shapes,
        grid=grid,
        in_specs=[s or vmem for s in specs],
        out_specs=out_specs or [vmem] * len(shapes),
        scratch_shapes=list(scratch),
        input_output_aliases=aliases or {},
        compiler_params=pltpu.CompilerParams(vmem_limit_bytes=40 * 2**20),
    )(*args)
    return result[0] if single else result


SMEM = pl.BlockSpec(memory_space=pltpu.SMEM)
ANY = pl.BlockSpec(memory_space=pl.ANY)


def body(
    gradient,
    weight,
    first_moment,
    second_moment,
    left_basis,
    left_gram,
    owner_table,
    bias_gradient,
    bias_weight,
    bias_first,
    bias_second,
):
    shards = lax.axis_size("shard")
    ranks = lax.axis_size("tensor")
    assert ranks == 4 and MCAP == 2
    layer_total = owner_table.shape[0]
    matrix_total = 5 * layer_total
    rows = gradient.shape[0]
    line = gradient.shape[2]
    columns = line // (sum(TYPE_TILES) * layer_total)
    width = rows * shards
    assert columns * ranks == width and columns <= LANES
    groups, share = place_columns(layer_total, shards, columns)
    slots = max(len(group) for group in groups)
    wide = -(-share // LANES) * LANES
    strip = slots * columns
    owned = MCAP * columns
    tile_rows = block_form(rows, share)[4]
    strip_rows = block_form(rows, strip)[4]
    owned_rows = block_form(rows, owned)[4]
    slot_matrix = [[piece[0] for piece in group] for group in groups]
    edges = np.full((shards, slots + 1), share, np.int32)
    for group, pieces in enumerate(groups):
        edges[group, 0] = 0
        edges[group, 1 : len(pieces) + 1] = np.cumsum([piece[2] for piece in pieces])

    my_group = lax.axis_index("shard")
    my_rank = lax.axis_index("tensor").astype(jnp.int32)
    my_edges = jnp.asarray(edges)[my_group]
    rank_arg = my_rank.reshape(1)
    owners = owner_table.reshape(-1)
    core_pairs = [(r, r ^ 1) for r in range(ranks)]
    chip_pairs = [(r, r ^ 2) for r in range(ranks)]

    def over_core(value):
        return lax.ppermute(value, "tensor", core_pairs)

    def over_chip(value):
        return lax.ppermute(value, "tensor", chip_pairs)

    def exchange(value):
        return lax.all_to_all(value, "shard", split_axis=0, concat_axis=0, tiled=True)

    together = lax.optimization_barrier


    line_tiles = line // LANES
    assert line_tiles * LANES == line
    dense = (rows * line_tiles, LANES)
    line_scratch = pltpu.VMEM((rows, line), F32)

    def open_line(ref, line_ref):
        for j in range(line_tiles):
            line_ref[:, j * LANES : (j + 1) * LANES] = ref[pl.ds(j, rows, stride=line_tiles), :]

    def close_line(line_ref, ref):
        for j in range(line_tiles):
            ref[pl.ds(j, rows, stride=line_tiles), :] = line_ref[:, j * LANES : (j + 1) * LANES]

    def gather_line(ref, group):
        pieces = [ref[:, at : at + length] for _, at, length in groups[group]]
        return pieces[0] if len(pieces) == 1 else jnp.concatenate(pieces, axis=1)

    def send_tiles(ref, line_ref, out_ref, base):
        open_line(ref, line_ref)
        for group in range(shards):
            store_block(out_ref, group, base, gather_line(line_ref, group), rows, share)

    def fill_owned_table(owner_ref, table_ref, count_ref):
        for group in range(shards):
            count_ref[group] = 0
            for m in range(MCAP):
                table_ref[group * MCAP + m] = -1

        def take(i, carry):
            owner = owner_ref[i]
            rank = count_ref[owner]
            table_ref[owner * MCAP + rank] = i
            count_ref[owner] = rank + 1
            return carry

        lax.fori_loop(0, matrix_total, take, 0)

    def send_owned(stage_ref, table_ref, out_ref, base):
        for group in range(shards):
            held = []
            for m in range(MCAP):
                matrix = table_ref[group * MCAP + m]
                block = stage_ref[jnp.maximum(matrix, 0)]
                held.append(jnp.where(matrix >= 0, block, 0.0))
            store_block(out_ref, group, base, jnp.concatenate(held, axis=1), rows, owned)

    table_scratch = [pltpu.SMEM((shards * MCAP,), jnp.int32), pltpu.SMEM((shards,), jnp.int32)]
    stage_scratch = pltpu.VMEM((matrix_total, rows, columns), F32)

    def slot_masks(edges_ref):
        lane = lax.broadcasted_iota(jnp.int32, (1, wide), 1)
        return [(lane >= edges_ref[k]) & (lane < edges_ref[k + 1]) for k in range(slots)]


    def pack_gradient(grad_ref, basis_ref, out_ref, line_ref):
        send_tiles(grad_ref, line_ref, out_ref, strip_rows)
        for group in range(shards):
            held = [
                basis_ref[:, matrix * columns : (matrix + 1) * columns]
                for matrix in slot_matrix[group]
            ]
            held += [jnp.zeros((rows, columns), F32)] * (slots - len(held))
            store_block(out_ref, group, 0, jnp.concatenate(held, axis=1), rows, strip)

    grad_dense = gradient.reshape(dense)
    basis_line = left_basis.reshape(rows, matrix_total * columns)
    send_one = call(
        pack_gradient,
        (shards, strip_rows + tile_rows, LANES),
        (grad_dense, basis_line),
        scratch=[line_scratch],
    )
    came_one = exchange(send_one)


    def pack_second(
        owner_ref, second_ref, basis_ref, out_ref, table_ref, count_ref, stage_ref, line_ref
    ):
        fill_owned_table(owner_ref, table_ref, count_ref)
        for matrix in range(matrix_total):
            stage_ref[matrix] = basis_ref[:, matrix * columns : (matrix + 1) * columns]
        send_tiles(second_ref, line_ref, out_ref, owned_rows)
        send_owned(stage_ref, table_ref, out_ref, 0)

    send_two = call(
        pack_second,
        (shards, owned_rows + tile_rows, LANES),
        (owners, second_moment.reshape(dense), basis_line),
        specs=[SMEM, None, None],
        scratch=table_scratch + [stage_scratch, line_scratch],
    )
    came_one, send_two = together((came_one, send_two))
    came_two = exchange(send_two)


    def gram_partials(edges_ref, came_ref, grad_ref, strips_ref, gram_ref, turned_ref):
        unpack_columns(came_ref, strip_rows, grad_ref, shards, rows, share)
        for source in range(shards):
            strips_ref[source] = came_ref[source, 0:strip_rows, :]
        turned_ref[...] = jnp.zeros_like(turned_ref)
        for rank in range(ranks):
            turned_ref[rank * LANES : rank * LANES + columns, :] = grad_ref[
                rank * columns : (rank + 1) * columns, :
            ]
        right = parts_of(turned_ref[...])
        grams = []
        for mask in slot_masks(edges_ref):
            left = parts_of(jnp.where(mask, grad_ref[...], 0.0))
            grams.append(product(left, right, (1, 1)))
        for rank in range(ranks):
            for group in range(shards):
                at = slice(group * rows, (group + 1) * rows)
                held = [g[at, rank * LANES : rank * LANES + columns] for g in grams]
                store_block(
                    gram_ref.at[rank],
                    group,
                    0,
                    jnp.concatenate(held, axis=1),
                    rows,
                    strip,
                )

    strip_shape = (shards, strip_rows, LANES)
    grad_full, strips_own, gram_parts = call(
        gram_partials,
        [(width, wide), strip_shape, (ranks,) + strip_shape],
        (my_edges, came_one),
        specs=[SMEM, None],
        scratch=[pltpu.VMEM((ranks * LANES, wide), F32)],
    )

    parts = gram_parts.reshape((2, 2) + strip_shape)
    my_chip, my_core = my_rank // 2, my_rank % 2
    for_core = lax.dynamic_index_in_dim(parts, 1 - my_core, 1, False)
    kept = lax.dynamic_index_in_dim(parts, my_core, 1, False) + over_core(for_core)
    for_chip = lax.dynamic_index_in_dim(kept, 1 - my_chip, 0, False)
    gram_strips = lax.dynamic_index_in_dim(kept, my_chip, 0, False) + over_chip(for_chip)

    strips_chip = over_chip(strips_own)
    pair = over_core(jnp.stack([strips_own, strips_chip]))


    def pack_first(first_ref, grad_ref, out_ref, new_ref, line_ref):
        send_tiles(first_ref, line_ref, out_ref, strip_rows)
        new_ref[...] = 0.9 * first_ref[...] + 0.1 * grad_ref[...]

    send_three, first_out = call(
        pack_first,
        [(shards, strip_rows + tile_rows, LANES), dense],
        (first_moment.reshape(dense), grad_dense),
        scratch=[line_scratch],
    )

    def add_strips(base_ref, strips_ref, out_ref):
        del base_ref
        out_ref[...] = strips_ref[...]

    def fill_head(kernel, base, head_rows, args, specs, scratch=()):
        return call(
            kernel,
            base.shape,
            (base,) + args,
            specs=[ANY] + specs,
            out_specs=[pl.BlockSpec((shards, head_rows, LANES), lambda i: (0, 0, 0))],
            grid=(1,),
            scratch=scratch,
            aliases={0: 0},
        )

    send_three = fill_head(add_strips, send_three, strip_rows, (gram_strips,), [None])
    came_two, send_three = together((came_two, send_three))
    came_three = exchange(send_three)


    half_shape = jax.ShapeDtypeStruct((slots, width, width), BF16)

    def rotate_gradient(
        rank_ref,
        edges_ref,
        own_ref,
        chip_ref,
        pair_ref,
        grad_ref,
        came_ref,
        high_ref,
        low_ref,
        high_turned_ref,
        low_turned_ref,
        second_ref,
        basis_ref,
    ):
        rank = rank_ref[0]
        for group in range(shards):
            blocks = [
                load_block(ref, group, 0, rows, strip)
                for ref in (own_ref, pair_ref.at[0], chip_ref, pair_ref.at[1])
            ]
            at = slice(group * rows, (group + 1) * rows)
            for k in range(slots):
                cut = [block[:, k * columns : (k + 1) * columns] for block in blocks]
                low = [jnp.where(rank % 2 == 0, cut[0 + h], cut[1 + h]) for h in (0, 2)]
                odd = [jnp.where(rank % 2 == 0, cut[1 + h], cut[0 + h]) for h in (0, 2)]
                first = rank < 2
                ordered = [
                    jnp.where(first, low[0], low[1]),
                    jnp.where(first, odd[0], odd[1]),
                    jnp.where(first, low[1], low[0]),
                    jnp.where(first, odd[1], odd[0]),
                ]
                basis_ref[k, at, :] = jnp.concatenate(ordered, axis=1)
        unpack_columns(came_ref, owned_rows, second_ref, shards, rows, share)
        grad = parts_of(grad_ref[...])
        hat = jnp.zeros((width, wide), F32)
        for k, mask in enumerate(slot_masks(edges_ref)):
            basis = basis_ref[k]
            high_ref[k], low_ref[k] = parts_of(basis)
            turned = parts_of(basis.T)
            high_turned_ref[k], low_turned_ref[k] = turned
            hat = jnp.where(mask, product(turned, grad), hat)
        second_ref[...] = 0.95 * second_ref[...] + 0.05 * hat * hat

    high, low, high_turned, low_turned, second_full = call(
        rotate_gradient,
        [half_shape] * 4 + [(width, wide)],
        (rank_arg, my_edges, strips_own, strips_chip, pair, grad_full, came_two),
        specs=[SMEM, SMEM] + [None] * 5,
        scratch=[pltpu.VMEM((slots, width, width), F32)],
    )


    def new_grams(owner_ref, came_ref, gram_ref, out_ref, table_ref, count_ref, stage_ref):
        fill_owned_table(owner_ref, table_ref, count_ref)
        total = [None] * matrix_total
        for group in range(shards):
            block = load_block(came_ref, group, 0, rows, strip)
            for k, matrix in enumerate(slot_matrix[group]):
                part = block[:, k * columns : (k + 1) * columns]
                total[matrix] = part if total[matrix] is None else total[matrix] + part
        for matrix in range(matrix_total):
            gram = gram_ref[:, matrix * columns : (matrix + 1) * columns]
            stage_ref[matrix] = 0.95 * gram + 0.05 * total[matrix]
        send_owned(stage_ref, table_ref, out_ref, 0)

    send_four = call(
        new_grams,
        (shards, owned_rows, LANES),
        (owners, came_three, left_gram.reshape(rows, matrix_total * columns)),
        specs=[SMEM, None, None],
        scratch=table_scratch + [stage_scratch],
    )
    came_three, send_four = together((came_three, send_four))
    came_four = exchange(send_four)


    def directions(
        edges_ref,
        came_ref,
        grad_ref,
        second_ref,
        high_ref,
        low_ref,
        high_turned_ref,
        low_turned_ref,
        send_ref,
        moment_ref,
    ):
        unpack_columns(came_ref, strip_rows, moment_ref, shards, rows, share)
        masks = slot_masks(edges_ref)
        moment = parts_of(0.9 * moment_ref[...] + 0.1 * grad_ref[...])
        hat = jnp.zeros((width, wide), F32)
        for k, mask in enumerate(masks):
            hat = jnp.where(mask, product((high_turned_ref[k], low_turned_ref[k]), moment), hat)
        step = parts_of(adam_direction(hat, second_ref[...]))
        turned = jnp.zeros((width, wide), F32)
        for k, mask in enumerate(masks):
            turned = jnp.where(mask, product((high_ref[k], low_ref[k]), step), turned)
        moment_ref[...] = turned
        pack_columns(moment_ref, send_ref, 0, shards, rows, share)
        pack_columns(second_ref, send_ref, tile_rows, shards, rows, share)

    send_five = call(
        directions,
        (shards, 2 * tile_rows, LANES),
        (my_edges, came_three, grad_full, second_full, high, low, high_turned, low_turned),
        specs=[SMEM] + [None] * 7,
        scratch=[pltpu.VMEM((width, wide), F32)],
    )
    came_four, send_five = together((came_four, send_five))
    came_five = exchange(send_five)


    def split_owned(rank_ref, came_ref, strips_ref, mine_ref, other_ref, whole_ref):
        odd = rank_ref[0] % 2 == 1
        for source in range(shards):
            at = slice(source * rows, (source + 1) * rows)
            block = load_block(came_ref, source, 0, rows, owned)
            zero, one = block[:, 0:columns], block[:, columns:owned]
            whole_ref[0, at, 0:columns] = zero
            whole_ref[1, at, 0:columns] = one
            mine_ref[at, 0:columns] = jnp.where(odd, one, zero)
            other_ref[at, 0:columns] = jnp.where(odd, zero, one)
        for m in range(MCAP):
            strips_ref[m] = whole_ref[m].T[0:columns]

    def join_half(rank_ref, mine_ref, other_ref, half_ref):
        odd = rank_ref[0] % 2 == 1
        for group in range(shards):
            at = slice(group * rows, (group + 1) * rows)
            mine, other = mine_ref[at, 0:columns], other_ref[at, 0:columns]
            both = [jnp.where(odd, other, mine), jnp.where(odd, mine, other)]
            store_block(half_ref, group, 0, jnp.concatenate(both, axis=1), rows, owned)

    def collect(came):
        strips, mine, other = call(
            split_owned,
            [(MCAP, columns, width), (width, LANES), (width, LANES)],
            (rank_arg, came),
            specs=[SMEM, None],
            scratch=[pltpu.VMEM((MCAP, width, LANES), F32)],
        )
        half = call(
            join_half,
            (shards, owned_rows, LANES),
            (rank_arg, mine, over_core(other)),
            specs=[SMEM, None, None],
        )
        return strips, half, over_chip(half)

    _, basis_half, basis_far = collect(came_two)
    gram_out, gram_half, gram_far = collect(came_four)

    def refresh(
        rank_ref,
        basis_half_ref,
        basis_far_ref,
        gram_half_ref,
        gram_far_ref,
        mine_ref,
        other_ref,
        basis_ref,
        gram_ref,
    ):
        rank = rank_ref[0]
        first = rank < 2
        for out, half_ref, far_ref in (
            (basis_ref, basis_half_ref, basis_far_ref),
            (gram_ref, gram_half_ref, gram_far_ref),
        ):
            for group in range(shards):
                half = load_block(half_ref, group, 0, rows, owned)
                far = load_block(far_ref, group, 0, rows, owned)
                both = [jnp.where(first, half, far), jnp.where(first, far, half)]
                out[group * rows : (group + 1) * rows, :] = jnp.concatenate(both, axis=1)
        power = product(parts_of(basis_ref[...].T), parts_of(gram_ref[...]))
        frame = power / jnp.sqrt(jnp.sum(power * power) + 1e-06)
        for _ in range(NS_STEPS):
            pieces = parts_of(frame)
            square = product(pieces, pieces, (1, 1))
            frame = 1.5 * frame - 0.5 * product(parts_of(square), pieces)
        strips = [frame[r * columns : (r + 1) * columns] for r in range(ranks)]
        low = jnp.where(first, strips[0], strips[2])
        odd = jnp.where(first, strips[1], strips[3])
        even_core = rank % 2 == 0
        mine_ref[...] = jnp.where(even_core, low, odd)
        other_ref[...] = jnp.where(even_core, odd, low)

    frame_mine, frame_other = call(
        refresh,
        [(columns, width), (columns, width)],
        (rank_arg, basis_half, basis_far, gram_half, gram_far),
        specs=[SMEM] + [None] * 4,
        scratch=[pltpu.VMEM((width, width), F32)] * 2,
    )
    frame_came = over_core(frame_other)
    pair_out = jnp.where(
        my_core == 0,
        jnp.stack([frame_mine, frame_came]),
        jnp.stack([frame_came, frame_mine]),
    )
    came_five, pair_out, gram_out, first_out = together((came_five, pair_out, gram_out, first_out))


    def line_from(came_ref, base, line_ref):
        for group in range(shards):
            block = load_block(came_ref, group, base, rows, share)
            offset = 0
            for _, at, length in groups[group]:
                line_ref[:, at : at + length] = block[:, offset : offset + length]
                offset += length

    def take_back(came_ref, weight_ref, weight_out_ref, second_out_ref, line_ref):
        line_from(came_ref, 0, line_ref)
        close_line(line_ref, weight_out_ref)
        old = weight_ref[...]
        weight_out_ref[...] = old - 0.01 * (weight_out_ref[...] + 0.1 * old)
        line_from(came_ref, tile_rows, line_ref)
        close_line(line_ref, second_out_ref)

    weight_out, second_out = call(
        take_back, [dense, dense], (came_five, weight.reshape(dense)), scratch=[line_scratch]
    )

    bias_first_new = 0.9 * bias_first + 0.1 * bias_gradient
    bias_second_new = 0.95 * bias_second + 0.05 * bias_gradient * bias_gradient
    bias_updated = bias_weight - 0.01 * adam_direction(bias_first_new, bias_second_new)
    flat = (rows, 1, line)
    return (
        weight_out.reshape(flat),
        first_out.reshape(flat),
        second_out.reshape(flat),
        pair_out.transpose(0, 2, 1)[None],
        gram_out.transpose(0, 2, 1)[None],
        bias_updated,
        bias_first_new,
        bias_second_new,
    )


def solution(mesh):
    tiles = P("shard", "tensor", None)
    bias = P(("shard", "tensor"))
    owned = P("shard", None, None, "tensor")
    in_specs = (tiles,) * 6 + (P(),) + (bias,) * 4
    out_specs = (tiles,) * 3 + (owned,) * 2 + (bias,) * 3
    return jax.shard_map(body, mesh=mesh, in_specs=in_specs, out_specs=out_specs, check_vma=False)
```

```python
import functools

import jax
import jax.numpy as jnp
import numpy as np
from jax import lax
from jax.experimental import pallas as pl
from jax.experimental.pallas import tpu as pltpu
from jax.sharding import PartitionSpec as P

MCAP = 2
STEP = 10
NS_STEPS = 5
TYPE_TILES = (3, 1, 4, 4, 6)
LANES = 128
F32 = jnp.float32
BF16 = jnp.bfloat16
CORR_ONE = 1.0 - 0.9**STEP
CORR_TWO = 1.0 - 0.95**STEP


def adam_direction(moment_hat, second_new):
    return moment_hat / CORR_ONE / (jnp.sqrt(second_new / CORR_TWO) + 1e-08)


def place_columns(layer_total, shards, columns):
    sizes = [tiles * columns for tiles in TYPE_TILES] * layer_total
    starts = np.concatenate([[0], np.cumsum(sizes)]).tolist()
    share = starts[-1] // shards
    assert share * shards == starts[-1]
    small = [i for i, size in enumerate(sizes) if size <= share]
    groups = [[] for _ in range(shards)]
    room = [share] * shards
    if len(small) <= shards:
        for group, i in enumerate(small):
            groups[group].append((i, starts[i], sizes[i]))
            room[group] -= sizes[i]
        rest = [i for i in range(len(sizes)) if i not in small]
    else:
        rest = list(range(len(sizes)))
    group = 0
    for i in rest:
        at, left = starts[i], sizes[i]
        while left:
            while not room[group]:
                group += 1
            take = min(left, room[group])
            groups[group].append((i, at, take))
            room[group] -= take
            at += take
            left -= take
    return groups, share


def block_form(rows, width):
    full, rest = divmod(width, LANES)
    padded = -(-rows // 8) * 8
    halved = 0 < rest <= LANES // 2 and rows % 16 == 0
    total = full * padded + (0 if not rest else rows // 2 if halved else padded)
    return full, rest, padded, halved, total


def store_block(ref, index, base, value, rows, width):
    full, rest, padded, halved, _ = block_form(rows, width)
    for j in range(full):
        at = base + j * padded
        ref[index, at : at + rows, :] = value[:, j * LANES : (j + 1) * LANES]
    if rest:
        at = base + full * padded
        tail = value[:, full * LANES : width]
        if halved:
            half = rows // 2
            ref[index, at : at + half, 0:rest] = tail[:half]
            ref[index, at : at + half, LANES // 2 : LANES // 2 + rest] = tail[half:]
        else:
            ref[index, at : at + rows, 0:rest] = tail


def load_pieces(ref, index, base, rows, width):
    full, rest, padded, halved, _ = block_form(rows, width)
    pieces = []
    for j in range(full):
        at = base + j * padded
        pieces.append(ref[index, at : at + rows, :])
    if rest:
        at = base + full * padded
        if halved:
            half = rows // 2
            block = ref[index, at : at + half, :]
            pieces.append(
                jnp.concatenate(
                    [block[:, 0:rest], block[:, LANES // 2 : LANES // 2 + rest]], axis=0
                )
            )
        else:
            pieces.append(ref[index, at : at + rows, 0:rest])
    return pieces


def load_block(ref, index, base, rows, width):
    pieces = load_pieces(ref, index, base, rows, width)
    return pieces[0] if len(pieces) == 1 else jnp.concatenate(pieces, axis=1)


def unpack_columns(ref, base, out_ref, shards, rows, width):
    if width % LANES:
        tail = width // LANES * LANES
        out_ref[:, tail:] = jnp.zeros((out_ref.shape[0], LANES), F32)
    for source in range(shards):
        for j, piece in enumerate(load_pieces(ref, source, base, rows, width)):
            lanes = piece.shape[1]
            out_ref[source * rows : (source + 1) * rows, j * LANES : j * LANES + lanes] = piece


def pack_columns(value_ref, ref, base, shards, rows, width):
    for dest in range(shards):
        block = value_ref[dest * rows : (dest + 1) * rows, 0:width]
        store_block(ref, dest, base, block, rows, width)


def parts_of(value):
    high = value.astype(BF16)
    return high, (value - high.astype(F32)).astype(BF16)


def product(left, right, contract=(1, 0)):
    dims = (((contract[0],), (contract[1],)), ((), ()))
    dot = functools.partial(lax.dot_general, dimension_numbers=dims, preferred_element_type=F32)
    return dot(left[0], right[0]) + (dot(left[0], right[1]) + dot(left[1], right[0]))


def call(kernel, outs, args, specs=None, out_specs=None, scratch=(), aliases=None, grid=()):
    single = isinstance(outs, tuple)
    shapes = [outs] if single else list(outs)
    shapes = [s if isinstance(s, jax.ShapeDtypeStruct) else jax.ShapeDtypeStruct(s, F32) for s in shapes]
    vmem = pl.BlockSpec(memory_space=pltpu.VMEM)
    specs = specs or [None] * len(args)
    result = pl.pallas_call(
        kernel,
        out_shape=shapes,
        grid=grid,
        in_specs=[s or vmem for s in specs],
        out_specs=out_specs or [vmem] * len(shapes),
        scratch_shapes=list(scratch),
        input_output_aliases=aliases or {},
        compiler_params=pltpu.CompilerParams(vmem_limit_bytes=32 * 2**20),
    )(*args)
    return result[0] if single else result


SMEM = pl.BlockSpec(memory_space=pltpu.SMEM)
ANY = pl.BlockSpec(memory_space=pl.ANY)
HBM = pl.BlockSpec(memory_space=pltpu.HBM)


def body(
    gradient,
    weight,
    first_moment,
    second_moment,
    left_basis,
    left_gram,
    owner_table,
    bias_gradient,
    bias_weight,
    bias_first,
    bias_second,
):
    shards = lax.axis_size("shard")
    ranks = lax.axis_size("tensor")
    assert ranks == 4 and MCAP == 2
    layer_total = owner_table.shape[0]
    matrix_total = 5 * layer_total
    rows = gradient.shape[0]
    line = gradient.shape[2]
    columns = line // (sum(TYPE_TILES) * layer_total)
    width = rows * shards
    assert columns * ranks == width and columns <= LANES
    groups, share = place_columns(layer_total, shards, columns)
    slots = max(len(group) for group in groups)
    wide = -(-share // LANES) * LANES
    strip = slots * columns
    owned = MCAP * columns
    tile_rows = block_form(rows, share)[4]
    strip_rows = block_form(rows, strip)[4]
    owned_rows = block_form(rows, owned)[4]
    slot_matrix = [[piece[0] for piece in group] for group in groups]
    edges = np.full((shards, slots + 1), share, np.int32)
    for group, pieces in enumerate(groups):
        edges[group, 0] = 0
        edges[group, 1 : len(pieces) + 1] = np.cumsum([piece[2] for piece in pieces])

    my_group = lax.axis_index("shard")
    my_rank = lax.axis_index("tensor").astype(jnp.int32)
    my_edges = jnp.asarray(edges)[my_group]
    rank_arg = my_rank.reshape(1)
    owners = owner_table.reshape(-1)
    core_pairs = [(r, r ^ 1) for r in range(ranks)]
    chip_pairs = [(r, r ^ 2) for r in range(ranks)]

    def over_core(value):
        return lax.ppermute(value, "tensor", core_pairs)

    def over_chip(value):
        return lax.ppermute(value, "tensor", chip_pairs)

    def exchange(value):
        return lax.all_to_all(value, "shard", split_axis=0, concat_axis=0, tiled=True)

    together = lax.optimization_barrier


    line_tiles = line // LANES
    assert line_tiles * LANES == line
    dense = (rows * line_tiles, LANES)
    line_scratch = pltpu.VMEM((rows, line), F32)

    def open_line(ref, line_ref):
        for j in range(line_tiles):
            line_ref[:, j * LANES : (j + 1) * LANES] = ref[pl.ds(j, rows, stride=line_tiles), :]

    def close_line(line_ref, ref):
        for j in range(line_tiles):
            ref[pl.ds(j, rows, stride=line_tiles), :] = line_ref[:, j * LANES : (j + 1) * LANES]

    def gather_line(ref, group):
        pieces = [ref[:, at : at + length] for _, at, length in groups[group]]
        return pieces[0] if len(pieces) == 1 else jnp.concatenate(pieces, axis=1)

    def send_tiles(ref, line_ref, out_ref, base):
        open_line(ref, line_ref)
        for group in range(shards):
            store_block(out_ref, group, base, gather_line(line_ref, group), rows, share)

    def fill_owned_table(owner_ref, table_ref, count_ref):
        for group in range(shards):
            count_ref[group] = 0
            for m in range(MCAP):
                table_ref[group * MCAP + m] = -1

        def take(i, carry):
            owner = owner_ref[i]
            rank = count_ref[owner]
            table_ref[owner * MCAP + rank] = i
            count_ref[owner] = rank + 1
            return carry

        lax.fori_loop(0, matrix_total, take, 0)

    def send_owned(stage_ref, table_ref, out_ref, base):
        for group in range(shards):
            held = []
            for m in range(MCAP):
                matrix = table_ref[group * MCAP + m]
                block = stage_ref[jnp.maximum(matrix, 0)]
                held.append(jnp.where(matrix >= 0, block, 0.0))
            store_block(out_ref, group, base, jnp.concatenate(held, axis=1), rows, owned)

    count_scratch = pltpu.SMEM((shards,), jnp.int32)
    stage_scratch = pltpu.VMEM((matrix_total, rows, columns), F32)

    def slot_masks(edges_ref):
        lane = lax.broadcasted_iota(jnp.int32, (1, wide), 1)
        return [(lane >= edges_ref[k]) & (lane < edges_ref[k + 1]) for k in range(slots)]


    def pack_gradient(grad_ref, out_ref, line_ref, dense_ref, send_ref, in_sems, out_sems):
        parts = 2 if rows % 16 == 0 else 1
        part_rows = rows // parts
        size = part_rows * line_tiles
        fetches = [
            pltpu.make_async_copy(
                grad_ref.at[pl.ds(p * size, size)], dense_ref.at[pl.ds(p * size, size)], in_sems.at[p]
            )
            for p in range(parts)
        ]
        for fetch in fetches:
            fetch.start()
        for p, fetch in enumerate(fetches):
            fetch.wait()
            for j in range(line_tiles):
                line_ref[p * part_rows : (p + 1) * part_rows, j * LANES : (j + 1) * LANES] = dense_ref[
                    pl.ds(p * size + j, part_rows, stride=line_tiles), :
                ]
        puts = []
        for group in range(shards):
            store_block(send_ref, group, 0, gather_line(line_ref, group), rows, share)
            puts.append(
                pltpu.make_async_copy(send_ref.at[group], out_ref.at[group], out_sems.at[group])
            )
            puts[-1].start()
        for put in puts:
            put.wait()

    grad_dense = gradient.reshape(dense)
    basis_line = left_basis.reshape(rows, matrix_total * columns)
    send_one = call(
        pack_gradient,
        (shards, tile_rows, LANES),
        (pltpu.with_memory_space_constraint(grad_dense, pltpu.HBM),),
        specs=[HBM],
        out_specs=[HBM],
        scratch=[
            line_scratch,
            pltpu.VMEM(dense, F32),
            pltpu.VMEM((shards, tile_rows, LANES), F32),
            pltpu.SemaphoreType.DMA((2,)),
            pltpu.SemaphoreType.DMA((shards,)),
        ],
    )
    came_one = exchange(send_one)


    def pack_second(
        owner_ref, second_ref, basis_ref, out_ref, table_ref, count_ref, stage_ref, line_ref
    ):
        fill_owned_table(owner_ref, table_ref, count_ref)
        for matrix in range(matrix_total):
            stage_ref[matrix] = basis_ref[:, matrix * columns : (matrix + 1) * columns]
        send_tiles(second_ref, line_ref, out_ref, head_rows)
        send_owned(stage_ref, table_ref, out_ref, 0)
        for group in range(shards):
            held = [stage_ref[matrix] for matrix in slot_matrix[group]]
            held += [jnp.zeros((rows, columns), F32)] * (slots - len(held))
            store_block(out_ref, group, owned_rows, jnp.concatenate(held, axis=1), rows, strip)

    head_rows = owned_rows + strip_rows
    send_two, owned_table = call(
        pack_second,
        [
            (shards, head_rows + tile_rows, LANES),
            jax.ShapeDtypeStruct((shards * MCAP,), jnp.int32),
        ],
        (owners, second_moment.reshape(dense), basis_line),
        specs=[SMEM, None, None],
        out_specs=[pl.BlockSpec(memory_space=pltpu.VMEM), SMEM],
        scratch=[count_scratch, stage_scratch, line_scratch],
    )
    came_one, send_two = together((came_one, send_two))
    came_two = exchange(send_two)


    def gram_partials(edges_ref, came_ref, grad_ref, gram_ref, turned_ref):
        unpack_columns(came_ref, 0, grad_ref, shards, rows, share)
        turned_ref[...] = jnp.zeros_like(turned_ref)
        for rank in range(ranks):
            turned_ref[rank * LANES : rank * LANES + columns, :] = grad_ref[
                rank * columns : (rank + 1) * columns, :
            ]
        right = parts_of(turned_ref[...])
        grams = []
        for mask in slot_masks(edges_ref):
            left = parts_of(jnp.where(mask, grad_ref[...], 0.0))
            grams.append(product(left, right, (1, 1)))
        for rank in range(ranks):
            for group in range(shards):
                at = slice(group * rows, (group + 1) * rows)
                held = [g[at, rank * LANES : rank * LANES + columns] for g in grams]
                store_block(
                    gram_ref.at[rank],
                    group,
                    0,
                    jnp.concatenate(held, axis=1),
                    rows,
                    strip,
                )

    strip_shape = (shards, strip_rows, LANES)
    grad_full, gram_parts = call(
        gram_partials,
        [(width, wide), (ranks,) + strip_shape],
        (my_edges, came_one),
        specs=[SMEM, None],
        scratch=[pltpu.VMEM((ranks * LANES, wide), F32)],
    )

    parts = gram_parts.reshape((2, 2) + strip_shape)
    my_chip, my_core = my_rank // 2, my_rank % 2
    for_core = lax.dynamic_index_in_dim(parts, 1 - my_core, 1, False)
    kept = lax.dynamic_index_in_dim(parts, my_core, 1, False) + over_core(for_core)
    for_chip = lax.dynamic_index_in_dim(kept, 1 - my_chip, 0, False)
    gram_strips = lax.dynamic_index_in_dim(kept, my_chip, 0, False) + over_chip(for_chip)


    def pack_first(first_ref, grad_ref, out_ref, new_ref, line_ref):
        send_tiles(first_ref, line_ref, out_ref, strip_rows)
        new_ref[...] = 0.9 * first_ref[...] + 0.1 * grad_ref[...]

    send_three, first_out = call(
        pack_first,
        [(shards, strip_rows + tile_rows, LANES), dense],
        (first_moment.reshape(dense), grad_dense),
        scratch=[line_scratch],
    )

    def add_strips(base_ref, strips_ref, out_ref):
        del base_ref
        out_ref[...] = strips_ref[...]

    def fill_head(kernel, base, head_rows, args, specs, scratch=()):
        return call(
            kernel,
            base.shape,
            (base,) + args,
            specs=[ANY] + specs,
            out_specs=[pl.BlockSpec((shards, head_rows, LANES), lambda i: (0, 0, 0))],
            grid=(1,),
            scratch=scratch,
            aliases={0: 0},
        )

    send_three = fill_head(add_strips, send_three, strip_rows, (gram_strips,), [None])
    came_two, send_three = together((came_two, send_three))
    came_three = exchange(send_three)


    strips_own = came_two[:, owned_rows:head_rows]
    strips_chip = over_chip(strips_own)
    pair = over_core(jnp.stack([strips_own, strips_chip]))


    def rotate_gradient(
        rank_ref,
        edges_ref,
        own_ref,
        chip_ref,
        pair_ref,
        grad_ref,
        came_ref,
        basis_ref,
        second_ref,
    ):
        rank = rank_ref[0]
        for group in range(shards):
            blocks = [
                load_block(ref, group, 0, rows, strip)
                for ref in (own_ref, pair_ref.at[0], chip_ref, pair_ref.at[1])
            ]
            at = slice(group * rows, (group + 1) * rows)
            for k in range(slots):
                cut = [block[:, k * columns : (k + 1) * columns] for block in blocks]
                low = [jnp.where(rank % 2 == 0, cut[0 + h], cut[1 + h]) for h in (0, 2)]
                odd = [jnp.where(rank % 2 == 0, cut[1 + h], cut[0 + h]) for h in (0, 2)]
                first = rank < 2
                ordered = [
                    jnp.where(first, low[0], low[1]),
                    jnp.where(first, odd[0], odd[1]),
                    jnp.where(first, low[1], low[0]),
                    jnp.where(first, odd[1], odd[0]),
                ]
                basis_ref[k, at, :] = jnp.concatenate(ordered, axis=1)
        unpack_columns(came_ref, head_rows, second_ref, shards, rows, share)
        grad = parts_of(grad_ref[...])
        hat = jnp.zeros((width, wide), F32)
        for k, mask in enumerate(slot_masks(edges_ref)):
            hat = jnp.where(mask, product(parts_of(basis_ref[k].T), grad), hat)
        second_ref[...] = 0.95 * second_ref[...] + 0.05 * hat * hat

    basis_full, second_full = call(
        rotate_gradient,
        [(slots, width, width), (width, wide)],
        (rank_arg, my_edges, strips_own, strips_chip, pair, grad_full, came_two),
        specs=[SMEM, SMEM] + [None] * 5,
    )


    def split_owned(rank_ref, came_ref, strips_ref, mine_ref, other_ref, whole_ref):
        odd = rank_ref[0] % 2 == 1
        for source in range(shards):
            at = slice(source * rows, (source + 1) * rows)
            block = load_block(came_ref, source, 0, rows, owned)
            zero, one = block[:, 0:columns], block[:, columns:owned]
            whole_ref[0, at, 0:columns] = zero
            whole_ref[1, at, 0:columns] = one
            mine_ref[at, 0:columns] = jnp.where(odd, one, zero)
            other_ref[at, 0:columns] = jnp.where(odd, zero, one)
        for m in range(MCAP):
            strips_ref[m] = whole_ref[m].T[0:columns]

    def join_half(rank_ref, mine_ref, other_ref, half_ref):
        odd = rank_ref[0] % 2 == 1
        for group in range(shards):
            at = slice(group * rows, (group + 1) * rows)
            mine, other = mine_ref[at, 0:columns], other_ref[at, 0:columns]
            both = [jnp.where(odd, other, mine), jnp.where(odd, mine, other)]
            store_block(half_ref, group, 0, jnp.concatenate(both, axis=1), rows, owned)

    def collect(came):
        strips, mine, other = call(
            split_owned,
            [(MCAP, columns, width), (width, LANES), (width, LANES)],
            (rank_arg, came),
            specs=[SMEM, None],
            scratch=[pltpu.VMEM((MCAP, width, LANES), F32)],
        )
        half = call(
            join_half,
            (shards, owned_rows, LANES),
            (rank_arg, mine, over_core(other)),
            specs=[SMEM, None, None],
        )
        return strips, half, over_chip(half)

    _, basis_half, basis_far = collect(came_two)


    def new_grams(table_ref, came_ref, gram_ref, out_ref, stage_ref):
        total = [None] * matrix_total
        for group in range(shards):
            block = load_block(came_ref, group, 0, rows, strip)
            for k, matrix in enumerate(slot_matrix[group]):
                part = block[:, k * columns : (k + 1) * columns]
                total[matrix] = part if total[matrix] is None else total[matrix] + part
        for matrix in range(matrix_total):
            gram = gram_ref[:, matrix * columns : (matrix + 1) * columns]
            stage_ref[matrix] = 0.95 * gram + 0.05 * total[matrix]
        send_owned(stage_ref, table_ref, out_ref, 0)

    send_four = call(
        new_grams,
        (shards, owned_rows, LANES),
        (owned_table, came_three, left_gram.reshape(rows, matrix_total * columns)),
        specs=[SMEM, None, None],
        scratch=[stage_scratch],
    )
    came_three, send_four, second_full, basis_half, basis_far = together(
        (came_three, send_four, second_full, basis_half, basis_far)
    )
    came_four = exchange(send_four)


    def directions(
        edges_ref,
        came_ref,
        grad_ref,
        second_ref,
        basis_ref,
        send_ref,
        moment_ref,
    ):
        unpack_columns(came_ref, strip_rows, moment_ref, shards, rows, share)
        masks = slot_masks(edges_ref)
        moment = parts_of(0.9 * moment_ref[...] + 0.1 * grad_ref[...])
        hat = jnp.zeros((width, wide), F32)
        for k, mask in enumerate(masks):
            hat = jnp.where(mask, product(parts_of(basis_ref[k].T), moment), hat)
        step = parts_of(adam_direction(hat, second_ref[...]))
        turned = jnp.zeros((width, wide), F32)
        for k, mask in enumerate(masks):
            turned = jnp.where(mask, product(parts_of(basis_ref[k]), step), turned)
        moment_ref[...] = turned
        pack_columns(moment_ref, send_ref, 0, shards, rows, share)
        pack_columns(second_ref, send_ref, tile_rows, shards, rows, share)

    send_five = call(
        directions,
        (shards, 2 * tile_rows, LANES),
        (my_edges, came_three, grad_full, second_full, basis_full),
        specs=[SMEM] + [None] * 4,
        scratch=[pltpu.VMEM((width, wide), F32)],
    )
    came_four, send_five = together((came_four, send_five))
    came_five = exchange(send_five)


    gram_out, gram_half, gram_far = collect(came_four)

    def refresh(
        rank_ref,
        basis_half_ref,
        basis_far_ref,
        gram_half_ref,
        gram_far_ref,
        weight_ref,
        mine_ref,
        other_ref,
        weight_out_ref,
        basis_ref,
        gram_ref,
        sem,
    ):
        fetch = pltpu.make_async_copy(weight_ref, weight_out_ref, sem)
        fetch.start()
        rank = rank_ref[0]
        first = rank < 2
        for out, half_ref, far_ref in (
            (basis_ref, basis_half_ref, basis_far_ref),
            (gram_ref, gram_half_ref, gram_far_ref),
        ):
            for group in range(shards):
                half = load_block(half_ref, group, 0, rows, owned)
                far = load_block(far_ref, group, 0, rows, owned)
                both = [jnp.where(first, half, far), jnp.where(first, far, half)]
                out[group * rows : (group + 1) * rows, :] = jnp.concatenate(both, axis=1)
        power = product(parts_of(basis_ref[...].T), parts_of(gram_ref[...]))
        frame = power / jnp.sqrt(jnp.sum(power * power) + 1e-06)
        for _ in range(NS_STEPS):
            pieces = parts_of(frame)
            square = product(pieces, pieces, (1, 1))
            frame = 1.5 * frame - 0.5 * product(parts_of(square), pieces)
        strips = [frame[r * columns : (r + 1) * columns] for r in range(ranks)]
        low = jnp.where(first, strips[0], strips[2])
        odd = jnp.where(first, strips[1], strips[3])
        even_core = rank % 2 == 0
        mine_ref[...] = jnp.where(even_core, low, odd)
        other_ref[...] = jnp.where(even_core, odd, low)
        fetch.wait()

    weight_dense = pltpu.with_memory_space_constraint(weight.reshape(dense), pltpu.HBM)
    frame_mine, frame_other, weight_near = call(
        refresh,
        [(columns, width), (columns, width), dense],
        (rank_arg, basis_half, basis_far, gram_half, gram_far, weight_dense),
        specs=[SMEM] + [None] * 4 + [HBM],
        scratch=[pltpu.VMEM((width, width), F32)] * 2 + [pltpu.SemaphoreType.DMA(())],
    )
    frame_came = over_core(frame_other)
    pair_out = jnp.where(
        my_core == 0,
        jnp.stack([frame_mine, frame_came]),
        jnp.stack([frame_came, frame_mine]),
    )
    came_five, pair_out, gram_out, first_out = together((came_five, pair_out, gram_out, first_out))


    def line_from(came_ref, base, line_ref):
        for group in range(shards):
            block = load_block(came_ref, group, base, rows, share)
            offset = 0
            for _, at, length in groups[group]:
                line_ref[:, at : at + length] = block[:, offset : offset + length]
                offset += length

    def take_back(came_ref, weight_ref, weight_out_ref, second_out_ref, line_ref):
        line_from(came_ref, 0, line_ref)
        close_line(line_ref, weight_out_ref)
        old = weight_ref[...]
        weight_out_ref[...] = old - 0.01 * (weight_out_ref[...] + 0.1 * old)
        line_from(came_ref, tile_rows, line_ref)
        close_line(line_ref, second_out_ref)

    weight_out, second_out = call(
        take_back, [dense, dense], (came_five, weight_near), scratch=[line_scratch]
    )

    bias_first_new = 0.9 * bias_first + 0.1 * bias_gradient
    bias_second_new = 0.95 * bias_second + 0.05 * bias_gradient * bias_gradient
    bias_updated = bias_weight - 0.01 * adam_direction(bias_first_new, bias_second_new)
    flat = (rows, 1, line)
    return (
        weight_out.reshape(flat),
        first_out.reshape(flat),
        second_out.reshape(flat),
        pair_out.transpose(0, 2, 1)[None],
        gram_out.transpose(0, 2, 1)[None],
        bias_updated,
        bias_first_new,
        bias_second_new,
    )


def solution(mesh):
    tiles = P("shard", "tensor", None)
    bias = P(("shard", "tensor"))
    owned = P("shard", None, None, "tensor")
    in_specs = (tiles,) * 6 + (P(),) + (bias,) * 4
    out_specs = (tiles,) * 3 + (owned,) * 2 + (bias,) * 3
    return jax.shard_map(body, mesh=mesh, in_specs=in_specs, out_specs=out_specs, check_vma=False)
```

```python
import functools

import jax
import jax.numpy as jnp
import numpy as np
from jax import lax
from jax.experimental import pallas as pl
from jax.experimental.pallas import tpu as pltpu
from jax.sharding import PartitionSpec as P

MCAP = 2
STEP = 10
NS_STEPS = 5
TYPE_TILES = (3, 1, 4, 4, 6)
LANES = 128
F32 = jnp.float32
BF16 = jnp.bfloat16
CORR_ONE = 1.0 - 0.9**STEP
CORR_TWO = 1.0 - 0.95**STEP


def adam_direction(moment_hat, second_new):
    return moment_hat / CORR_ONE / (jnp.sqrt(second_new / CORR_TWO) + 1e-08)


def place_columns(layer_total, shards, columns):
    sizes = [tiles * columns for tiles in TYPE_TILES] * layer_total
    starts = np.concatenate([[0], np.cumsum(sizes)]).tolist()
    share = starts[-1] // shards
    assert share * shards == starts[-1]
    small = [i for i, size in enumerate(sizes) if size <= share]
    groups = [[] for _ in range(shards)]
    room = [share] * shards
    if len(small) <= shards:
        for group, i in enumerate(small):
            groups[group].append((i, starts[i], sizes[i]))
            room[group] -= sizes[i]
        rest = [i for i in range(len(sizes)) if i not in small]
    else:
        rest = list(range(len(sizes)))
    group = 0
    for i in rest:
        at, left = starts[i], sizes[i]
        while left:
            while not room[group]:
                group += 1
            take = min(left, room[group])
            groups[group].append((i, at, take))
            room[group] -= take
            at += take
            left -= take
    return groups, share


def block_form(rows, width):
    full, rest = divmod(width, LANES)
    padded = -(-rows // 8) * 8
    halved = 0 < rest <= LANES // 2 and rows % 16 == 0
    total = full * padded + (0 if not rest else rows // 2 if halved else padded)
    return full, rest, padded, halved, total


def store_block(ref, index, base, value, rows, width):
    full, rest, padded, halved, _ = block_form(rows, width)
    for j in range(full):
        at = base + j * padded
        ref[index, at : at + rows, :] = value[:, j * LANES : (j + 1) * LANES]
    if rest:
        at = base + full * padded
        tail = value[:, full * LANES : width]
        if halved:
            half = rows // 2
            ref[index, at : at + half, 0:rest] = tail[:half]
            ref[index, at : at + half, LANES // 2 : LANES // 2 + rest] = tail[half:]
        else:
            ref[index, at : at + rows, 0:rest] = tail


def load_pieces(ref, index, base, rows, width):
    full, rest, padded, halved, _ = block_form(rows, width)
    pieces = []
    for j in range(full):
        at = base + j * padded
        pieces.append(ref[index, at : at + rows, :])
    if rest:
        at = base + full * padded
        if halved:
            half = rows // 2
            block = ref[index, at : at + half, :]
            pieces.append(
                jnp.concatenate(
                    [block[:, 0:rest], block[:, LANES // 2 : LANES // 2 + rest]], axis=0
                )
            )
        else:
            pieces.append(ref[index, at : at + rows, 0:rest])
    return pieces


def load_block(ref, index, base, rows, width):
    pieces = load_pieces(ref, index, base, rows, width)
    return pieces[0] if len(pieces) == 1 else jnp.concatenate(pieces, axis=1)


def unpack_columns(ref, base, out_ref, shards, rows, width):
    if width % LANES:
        tail = width // LANES * LANES
        out_ref[:, tail:] = jnp.zeros((out_ref.shape[0], LANES), F32)
    for source in range(shards):
        for j, piece in enumerate(load_pieces(ref, source, base, rows, width)):
            lanes = piece.shape[1]
            out_ref[source * rows : (source + 1) * rows, j * LANES : j * LANES + lanes] = piece


def pack_columns(value_ref, ref, base, shards, rows, width):
    for dest in range(shards):
        block = value_ref[dest * rows : (dest + 1) * rows, 0:width]
        store_block(ref, dest, base, block, rows, width)


def parts_of(value):
    high = value.astype(BF16)
    return high, (value - high.astype(F32)).astype(BF16)


def product(left, right, contract=(1, 0)):
    dims = (((contract[0],), (contract[1],)), ((), ()))
    dot = functools.partial(lax.dot_general, dimension_numbers=dims, preferred_element_type=F32)
    return dot(left[0], right[0]) + (dot(left[0], right[1]) + dot(left[1], right[0]))


def call(kernel, outs, args, specs=None, out_specs=None, scratch=(), aliases=None, grid=()):
    single = isinstance(outs, tuple)
    shapes = [outs] if single else list(outs)
    shapes = [s if isinstance(s, jax.ShapeDtypeStruct) else jax.ShapeDtypeStruct(s, F32) for s in shapes]
    vmem = pl.BlockSpec(memory_space=pltpu.VMEM)
    specs = specs or [None] * len(args)
    result = pl.pallas_call(
        kernel,
        out_shape=shapes,
        grid=grid,
        in_specs=[s or vmem for s in specs],
        out_specs=out_specs or [vmem] * len(shapes),
        scratch_shapes=list(scratch),
        input_output_aliases=aliases or {},
        compiler_params=pltpu.CompilerParams(vmem_limit_bytes=32 * 2**20),
    )(*args)
    return result[0] if single else result


SMEM = pl.BlockSpec(memory_space=pltpu.SMEM)
ANY = pl.BlockSpec(memory_space=pl.ANY)
HBM = pl.BlockSpec(memory_space=pltpu.HBM)


def body(
    gradient,
    weight,
    first_moment,
    second_moment,
    left_basis,
    left_gram,
    owner_table,
    bias_gradient,
    bias_weight,
    bias_first,
    bias_second,
):
    shards = lax.axis_size("shard")
    ranks = lax.axis_size("tensor")
    assert ranks == 4 and MCAP == 2
    layer_total = owner_table.shape[0]
    matrix_total = 5 * layer_total
    rows = gradient.shape[0]
    line = gradient.shape[2]
    columns = line // (sum(TYPE_TILES) * layer_total)
    width = rows * shards
    assert columns * ranks == width and columns <= LANES
    groups, share = place_columns(layer_total, shards, columns)
    slots = max(len(group) for group in groups)
    wide = -(-share // LANES) * LANES
    strip = slots * columns
    owned = MCAP * columns
    tile_rows = block_form(rows, share)[4]
    strip_rows = block_form(rows, strip)[4]
    owned_rows = block_form(rows, owned)[4]
    slot_matrix = [[piece[0] for piece in group] for group in groups]
    edges = np.full((shards, slots + 1), share, np.int32)
    for group, pieces in enumerate(groups):
        edges[group, 0] = 0
        edges[group, 1 : len(pieces) + 1] = np.cumsum([piece[2] for piece in pieces])

    my_group = lax.axis_index("shard")
    my_rank = lax.axis_index("tensor").astype(jnp.int32)
    my_edges = jnp.asarray(edges)[my_group]
    rank_arg = my_rank.reshape(1)
    owners = owner_table.reshape(-1)
    core_pairs = [(r, r ^ 1) for r in range(ranks)]
    chip_pairs = [(r, r ^ 2) for r in range(ranks)]

    def over_core(value):
        return lax.ppermute(value, "tensor", core_pairs)

    def over_chip(value):
        return lax.ppermute(value, "tensor", chip_pairs)

    def exchange(value):
        return lax.all_to_all(value, "shard", split_axis=0, concat_axis=0, tiled=True)

    together = lax.optimization_barrier


    line_tiles = line // LANES
    assert line_tiles * LANES == line
    dense = (rows * line_tiles, LANES)
    line_scratch = pltpu.VMEM((rows, line), F32)

    def open_line(ref, line_ref):
        for j in range(line_tiles):
            line_ref[:, j * LANES : (j + 1) * LANES] = ref[pl.ds(j, rows, stride=line_tiles), :]

    def close_line(line_ref, ref):
        for j in range(line_tiles):
            ref[pl.ds(j, rows, stride=line_tiles), :] = line_ref[:, j * LANES : (j + 1) * LANES]

    def gather_line(ref, group):
        pieces = [ref[:, at : at + length] for _, at, length in groups[group]]
        return pieces[0] if len(pieces) == 1 else jnp.concatenate(pieces, axis=1)

    def send_tiles(ref, line_ref, out_ref, base):
        open_line(ref, line_ref)
        for group in range(shards):
            store_block(out_ref, group, base, gather_line(line_ref, group), rows, share)

    def fill_owned_table(owner_ref, table_ref, count_ref):
        for group in range(shards):
            count_ref[group] = 0
            for m in range(MCAP):
                table_ref[group * MCAP + m] = -1

        def take(i, carry):
            owner = owner_ref[i]
            rank = count_ref[owner]
            table_ref[owner * MCAP + rank] = i
            count_ref[owner] = rank + 1
            return carry

        lax.fori_loop(0, matrix_total, take, 0)

    def send_owned(stage_ref, table_ref, out_ref, base):
        for group in range(shards):
            held = []
            for m in range(MCAP):
                matrix = table_ref[group * MCAP + m]
                block = stage_ref[jnp.maximum(matrix, 0)]
                held.append(jnp.where(matrix >= 0, block, 0.0))
            store_block(out_ref, group, base, jnp.concatenate(held, axis=1), rows, owned)

    count_scratch = pltpu.SMEM((shards,), jnp.int32)
    stage_scratch = pltpu.VMEM((matrix_total, rows, columns), F32)

    def slot_masks(edges_ref):
        lane = lax.broadcasted_iota(jnp.int32, (1, wide), 1)
        return [(lane >= edges_ref[k]) & (lane < edges_ref[k + 1]) for k in range(slots)]


    def pack_gradient(grad_ref, basis_ref, out_ref, line_ref, dense_ref, sem):
        fetch = pltpu.make_async_copy(grad_ref, dense_ref, sem)
        fetch.start()
        for group in range(shards):
            held = [
                basis_ref[:, matrix * columns : (matrix + 1) * columns]
                for matrix in slot_matrix[group]
            ]
            held += [jnp.zeros((rows, columns), F32)] * (slots - len(held))
            store_block(out_ref, group, 0, jnp.concatenate(held, axis=1), rows, strip)
        fetch.wait()
        send_tiles(dense_ref, line_ref, out_ref, strip_rows)

    grad_dense = gradient.reshape(dense)
    basis_line = left_basis.reshape(rows, matrix_total * columns)
    send_one = call(
        pack_gradient,
        (shards, strip_rows + tile_rows, LANES),
        (pltpu.with_memory_space_constraint(grad_dense, pltpu.HBM), basis_line),
        specs=[HBM, None],
        scratch=[line_scratch, pltpu.VMEM(dense, F32), pltpu.SemaphoreType.DMA(())],
    )
    came_one = exchange(send_one)


    half_groups = shards // 2
    half_total = matrix_total // 2
    assert half_groups * 2 == shards and shards & (shards - 1) == 0
    assert all(
        (matrix >= half_total) == (group >= half_groups)
        for group in range(shards)
        for matrix in slot_matrix[group]
    )
    group_arg = my_group.astype(jnp.int32).reshape(1)
    slot_table = np.full((shards, slots), -1, np.int32)
    for group in range(shards):
        slot_table[group, : len(slot_matrix[group])] = slot_matrix[group]
    slot_table = jnp.asarray(slot_table.reshape(-1))


    def pack_moments(
        owner_ref,
        second_ref,
        first_ref,
        grad_ref,
        basis_ref,
        out_ref,
        new_ref,
        table_ref,
        count_ref,
        stage_ref,
        line_ref,
    ):
        fill_owned_table(owner_ref, table_ref, count_ref)
        for matrix in range(matrix_total):
            stage_ref[matrix] = basis_ref[:, matrix * columns : (matrix + 1) * columns]
        send_owned(stage_ref, table_ref, out_ref, 0)
        send_tiles(second_ref, line_ref, out_ref, owned_rows)
        send_tiles(first_ref, line_ref, out_ref, owned_rows + tile_rows)
        new_ref[...] = 0.9 * first_ref[...] + 0.1 * grad_ref[...]

    vmem = pl.BlockSpec(memory_space=pltpu.VMEM)
    send_two, first_out, owned_table = call(
        pack_moments,
        [
            (shards, owned_rows + 2 * tile_rows, LANES),
            dense,
            jax.ShapeDtypeStruct((shards * MCAP,), jnp.int32),
        ],
        (
            owners,
            second_moment.reshape(dense),
            first_moment.reshape(dense),
            grad_dense,
            basis_line,
        ),
        specs=[SMEM, None, None, None, None],
        out_specs=[vmem, vmem, SMEM],
        scratch=[count_scratch, stage_scratch, line_scratch],
    )
    came_one, send_two = together((came_one, send_two))
    came_two = exchange(send_two)


    def gram_partials(edges_ref, came_ref, grad_ref, strips_ref, gram_ref, turned_ref):
        unpack_columns(came_ref, strip_rows, grad_ref, shards, rows, share)
        for source in range(shards):
            strips_ref[source] = came_ref[source, 0:strip_rows, :]
        turned_ref[...] = jnp.zeros_like(turned_ref)
        for rank in range(ranks):
            turned_ref[rank * LANES : rank * LANES + columns, :] = grad_ref[
                rank * columns : (rank + 1) * columns, :
            ]
        right = parts_of(turned_ref[...])
        grams = []
        for mask in slot_masks(edges_ref):
            left = parts_of(jnp.where(mask, grad_ref[...], 0.0))
            grams.append(product(left, right, (1, 1)))
        for rank in range(ranks):
            for group in range(shards):
                at = slice(group * rows, (group + 1) * rows)
                held = [g[at, rank * LANES : rank * LANES + columns] for g in grams]
                store_block(
                    gram_ref.at[rank],
                    group,
                    0,
                    jnp.concatenate(held, axis=1),
                    rows,
                    strip,
                )

    strip_shape = (shards, strip_rows, LANES)
    grad_full, strips_own, gram_parts = call(
        gram_partials,
        [(width, wide), strip_shape, (ranks,) + strip_shape],
        (my_edges, came_one),
        specs=[SMEM, None],
        scratch=[pltpu.VMEM((ranks * LANES, wide), F32)],
    )

    parts = gram_parts.reshape((2, 2) + strip_shape)
    my_chip, my_core = my_rank // 2, my_rank % 2
    for_core = lax.dynamic_index_in_dim(parts, 1 - my_core, 1, False)
    kept = lax.dynamic_index_in_dim(parts, my_core, 1, False) + over_core(for_core)
    for_chip = lax.dynamic_index_in_dim(kept, 1 - my_chip, 0, False)
    came_chip = over_chip(for_chip)


    def sum_strips(group_ref, chip_ref, kept_ref, came_ref, *out_refs):
        place = group_ref[0] % half_groups
        for k, out_ref in enumerate(out_refs):
            for j in range(2):
                at = (place ^ k) + j * half_groups
                out_ref[j] = kept_ref[chip_ref[0], at] + came_ref[at]

    gram_blocks = call(
        sum_strips,
        [(2, strip_rows, LANES)] * half_groups,
        (group_arg, my_chip.astype(jnp.int32).reshape(1), kept, came_chip),
        specs=[SMEM, SMEM, None, None],
    )
    gram_blocks = [gram_blocks[0]] + [
        lax.ppermute(gram_blocks[k], "shard", [(s, s ^ k) for s in range(shards)])
        for k in range(1, half_groups)
    ]


    *gram_blocks, strips_own = together((*gram_blocks, strips_own))
    strips_chip = over_chip(strips_own)


    def split_owned(rank_ref, came_ref, *refs):
        spread = len(refs) == 4
        mine_ref, other_ref = refs[-3:-1] if spread else refs
        odd = rank_ref[0] % 2 == 1
        for block_at in range(shards):
            at = slice(block_at * rows, (block_at + 1) * rows)
            if spread:
                place, base = block_at % half_groups, block_at // half_groups * owned_rows
                block = load_block(came_ref, place, base, rows, owned) + load_block(
                    came_ref, half_groups + place, base, rows, owned
                )
            else:
                block = load_block(came_ref, block_at, 0, rows, owned)
            strips = [block[:, m * columns : (m + 1) * columns] for m in range(MCAP)]
            mine_ref[at, 0:columns] = jnp.where(odd, strips[1], strips[0])
            other_ref[at, 0:columns] = jnp.where(odd, strips[0], strips[1])
            if spread:
                for m in range(MCAP):
                    refs[-1][m, at, 0:columns] = strips[m]
        if spread:
            for m in range(MCAP):
                refs[0][m] = refs[-1][m].T[0:columns]

    def join_half(rank_ref, mine_ref, other_ref, half_ref):
        odd = rank_ref[0] % 2 == 1
        for group in range(shards):
            at = slice(group * rows, (group + 1) * rows)
            mine, other = mine_ref[at, 0:columns], other_ref[at, 0:columns]
            both = [jnp.where(odd, other, mine), jnp.where(odd, mine, other)]
            store_block(half_ref, group, 0, jnp.concatenate(both, axis=1), rows, owned)

    def collect(came, spread):
        *strips, mine, other = call(
            split_owned,
            [(MCAP, columns, width)] * spread + [(width, LANES), (width, LANES)],
            (rank_arg, came),
            specs=[SMEM, None],
            scratch=[pltpu.VMEM((MCAP, width, LANES), F32)] * spread,
        )
        half = call(
            join_half,
            (shards, owned_rows, LANES),
            (rank_arg, mine, over_core(other)),
            specs=[SMEM, None, None],
        )
        return *strips, half, over_chip(half)


    def new_grams(group_ref, table_ref, slot_ref, gram_ref, *refs):
        came, (out_ref, stage_ref) = refs[:half_groups], refs[half_groups:]
        group = group_ref[0]
        half = group // half_groups
        for matrix in range(matrix_total):
            old = 0.95 * gram_ref[:, matrix * columns : (matrix + 1) * columns]
            stage_ref[0, matrix] = jnp.where(half == 0, old, 0.0)
            stage_ref[1, matrix] = jnp.where(half == 0, 0.0, old)
        for k, came_ref in enumerate(came):
            for j in range(2):
                block = load_block(came_ref, j, 0, rows, strip)
                for m in range(slots):
                    matrix = slot_ref[(group ^ k) * slots + m]
                    at = jnp.where(matrix >= 0, matrix, matrix_total)
                    part = block[:, m * columns : (m + 1) * columns]
                    stage_ref[j, at] = stage_ref[j, at] + 0.05 * part
        for dest in range(shards):
            for j in range(2):
                held = []
                for m in range(MCAP):
                    matrix = table_ref[dest * MCAP + m]
                    block = stage_ref[j, jnp.maximum(matrix, 0)]
                    held.append(jnp.where(matrix >= 0, block, 0.0))
                block = jnp.concatenate(held, axis=1)
                store_block(out_ref, dest, j * owned_rows, block, rows, owned)

    send_four = call(
        new_grams,
        (shards, 2 * owned_rows, LANES),
        (
            group_arg,
            owned_table,
            slot_table,
            left_gram.reshape(rows, matrix_total * columns),
            *gram_blocks,
        ),
        specs=[SMEM, SMEM, SMEM] + [None] * (1 + half_groups),
        scratch=[pltpu.VMEM((2, matrix_total + 1, rows, columns), F32)],
    )
    came_two, send_four, strips_chip = together((came_two, send_four, strips_chip))
    came_four = exchange(send_four)
    pair = over_core(jnp.stack([strips_own, strips_chip]))


    def rotate_gradient(
        rank_ref,
        edges_ref,
        own_ref,
        chip_ref,
        pair_ref,
        grad_ref,
        basis_ref,
        hat_ref,
    ):
        rank = rank_ref[0]
        for group in range(shards):
            blocks = [
                load_block(ref, group, 0, rows, strip)
                for ref in (own_ref, pair_ref.at[0], chip_ref, pair_ref.at[1])
            ]
            at = slice(group * rows, (group + 1) * rows)
            for k in range(slots):
                cut = [block[:, k * columns : (k + 1) * columns] for block in blocks]
                low = [jnp.where(rank % 2 == 0, cut[0 + h], cut[1 + h]) for h in (0, 2)]
                odd = [jnp.where(rank % 2 == 0, cut[1 + h], cut[0 + h]) for h in (0, 2)]
                first = rank < 2
                ordered = [
                    jnp.where(first, low[0], low[1]),
                    jnp.where(first, odd[0], odd[1]),
                    jnp.where(first, low[1], low[0]),
                    jnp.where(first, odd[1], odd[0]),
                ]
                basis_ref[k, at, :] = jnp.concatenate(ordered, axis=1)
        grad = parts_of(grad_ref[...])
        hat = jnp.zeros((width, wide), F32)
        for k, mask in enumerate(slot_masks(edges_ref)):
            hat = jnp.where(mask, product(parts_of(basis_ref[k].T), grad), hat)
        hat_ref[...] = hat

    basis_full, hat_full = call(
        rotate_gradient,
        [(slots, width, width), (width, wide)],
        (rank_arg, my_edges, strips_own, strips_chip, pair, grad_full),
        specs=[SMEM, SMEM] + [None] * 4,
    )

    basis_half, basis_far = collect(came_two, 0)


    def directions(
        edges_ref,
        came_ref,
        grad_ref,
        hat_ref,
        basis_ref,
        send_ref,
        moment_ref,
        second_ref,
    ):
        unpack_columns(came_ref, owned_rows, second_ref, shards, rows, share)
        second_ref[...] = 0.95 * second_ref[...] + 0.05 * hat_ref[...] * hat_ref[...]
        unpack_columns(came_ref, owned_rows + tile_rows, moment_ref, shards, rows, share)
        masks = slot_masks(edges_ref)
        moment = parts_of(0.9 * moment_ref[...] + 0.1 * grad_ref[...])
        hat = jnp.zeros((width, wide), F32)
        for k, mask in enumerate(masks):
            hat = jnp.where(mask, product(parts_of(basis_ref[k].T), moment), hat)
        step = parts_of(adam_direction(hat, second_ref[...]))
        turned = jnp.zeros((width, wide), F32)
        for k, mask in enumerate(masks):
            turned = jnp.where(mask, product(parts_of(basis_ref[k]), step), turned)
        moment_ref[...] = turned
        pack_columns(moment_ref, send_ref, 0, shards, rows, share)
        pack_columns(second_ref, send_ref, tile_rows, shards, rows, share)

    send_five = call(
        directions,
        (shards, 2 * tile_rows, LANES),
        (my_edges, came_two, grad_full, hat_full, basis_full),
        specs=[SMEM] + [None] * 4,
        scratch=[pltpu.VMEM((width, wide), F32)] * 2,
    )
    came_four, send_five = together((came_four, send_five))
    came_five = exchange(send_five)


    gram_out, gram_half, gram_far = collect(came_four, 1)

    def refresh(
        rank_ref,
        basis_half_ref,
        basis_far_ref,
        gram_half_ref,
        gram_far_ref,
        weight_ref,
        mine_ref,
        other_ref,
        weight_out_ref,
        basis_ref,
        gram_ref,
        sem,
    ):
        fetch = pltpu.make_async_copy(weight_ref, weight_out_ref, sem)
        fetch.start()
        rank = rank_ref[0]
        first = rank < 2
        for out, half_ref, far_ref in (
            (basis_ref, basis_half_ref, basis_far_ref),
            (gram_ref, gram_half_ref, gram_far_ref),
        ):
            for group in range(shards):
                half = load_block(half_ref, group, 0, rows, owned)
                far = load_block(far_ref, group, 0, rows, owned)
                both = [jnp.where(first, half, far), jnp.where(first, far, half)]
                out[group * rows : (group + 1) * rows, :] = jnp.concatenate(both, axis=1)
        power = product(parts_of(basis_ref[...].T), parts_of(gram_ref[...]))
        frame = power / jnp.sqrt(jnp.sum(power * power) + 1e-06)
        for _ in range(NS_STEPS):
            pieces = parts_of(frame)
            square = product(pieces, pieces, (1, 1))
            frame = 1.5 * frame - 0.5 * product(parts_of(square), pieces)
        strips = [frame[r * columns : (r + 1) * columns] for r in range(ranks)]
        low = jnp.where(first, strips[0], strips[2])
        odd = jnp.where(first, strips[1], strips[3])
        even_core = rank % 2 == 0
        mine_ref[...] = jnp.where(even_core, low, odd)
        other_ref[...] = jnp.where(even_core, odd, low)
        fetch.wait()

    weight_dense = pltpu.with_memory_space_constraint(weight.reshape(dense), pltpu.HBM)
    frame_mine, frame_other, weight_near = call(
        refresh,
        [(columns, width), (columns, width), dense],
        (rank_arg, basis_half, basis_far, gram_half, gram_far, weight_dense),
        specs=[SMEM] + [None] * 4 + [HBM],
        scratch=[pltpu.VMEM((width, width), F32)] * 2 + [pltpu.SemaphoreType.DMA(())],
    )
    frame_came = over_core(frame_other)
    pair_out = jnp.where(
        my_core == 0,
        jnp.stack([frame_mine, frame_came]),
        jnp.stack([frame_came, frame_mine]),
    )
    came_five, pair_out, gram_out, first_out = together((came_five, pair_out, gram_out, first_out))


    def line_from(came_ref, base, line_ref):
        for group in range(shards):
            block = load_block(came_ref, group, base, rows, share)
            offset = 0
            for _, at, length in groups[group]:
                line_ref[:, at : at + length] = block[:, offset : offset + length]
                offset += length

    def take_back(came_ref, weight_ref, weight_out_ref, second_out_ref, line_ref):
        line_from(came_ref, 0, line_ref)
        close_line(line_ref, weight_out_ref)
        old = weight_ref[...]
        weight_out_ref[...] = old - 0.01 * (weight_out_ref[...] + 0.1 * old)
        line_from(came_ref, tile_rows, line_ref)
        close_line(line_ref, second_out_ref)

    weight_out, second_out = call(
        take_back, [dense, dense], (came_five, weight_near), scratch=[line_scratch]
    )

    bias_first_new = 0.9 * bias_first + 0.1 * bias_gradient
    bias_second_new = 0.95 * bias_second + 0.05 * bias_gradient * bias_gradient
    bias_updated = bias_weight - 0.01 * adam_direction(bias_first_new, bias_second_new)
    flat = (rows, 1, line)
    return (
        weight_out.reshape(flat),
        first_out.reshape(flat),
        second_out.reshape(flat),
        pair_out.transpose(0, 2, 1)[None],
        gram_out.transpose(0, 2, 1)[None],
        bias_updated,
        bias_first_new,
        bias_second_new,
    )


def solution(mesh):
    tiles = P("shard", "tensor", None)
    bias = P(("shard", "tensor"))
    owned = P("shard", None, None, "tensor")
    in_specs = (tiles,) * 6 + (P(),) + (bias,) * 4
    out_specs = (tiles,) * 3 + (owned,) * 2 + (bias,) * 3
    return jax.shard_map(body, mesh=mesh, in_specs=in_specs, out_specs=out_specs, check_vma=False)
```

```python
import functools

import jax
import jax.numpy as jnp
import numpy as np
from jax import lax
from jax.experimental import pallas as pl
from jax.experimental.pallas import tpu as pltpu
from jax.sharding import PartitionSpec as P

MCAP = 2
STEP = 10
NS_STEPS = 5
TYPE_TILES = (3, 1, 4, 4, 6)
LANES = 128
F32 = jnp.float32
BF16 = jnp.bfloat16
CORR_ONE = 1.0 - 0.9**STEP
CORR_TWO = 1.0 - 0.95**STEP


def adam_direction(moment_hat, second_new):
    return moment_hat / CORR_ONE / (jnp.sqrt(second_new / CORR_TWO) + 1e-08)


def place_columns(layer_total, shards, columns):
    sizes = [tiles * columns for tiles in TYPE_TILES] * layer_total
    starts = np.concatenate([[0], np.cumsum(sizes)]).tolist()
    share = starts[-1] // shards
    assert share * shards == starts[-1]
    small = [i for i, size in enumerate(sizes) if size <= share]
    groups = [[] for _ in range(shards)]
    room = [share] * shards
    if len(small) <= shards:
        for group, i in enumerate(small):
            groups[group].append((i, starts[i], sizes[i]))
            room[group] -= sizes[i]
        rest = [i for i in range(len(sizes)) if i not in small]
    else:
        rest = list(range(len(sizes)))
    group = 0
    for i in rest:
        at, left = starts[i], sizes[i]
        while left:
            while not room[group]:
                group += 1
            take = min(left, room[group])
            groups[group].append((i, at, take))
            room[group] -= take
            at += take
            left -= take
    return groups, share


def block_form(rows, width):
    full, rest = divmod(width, LANES)
    padded = -(-rows // 8) * 8
    halved = 0 < rest <= LANES // 2 and rows % 16 == 0
    total = full * padded + (0 if not rest else rows // 2 if halved else padded)
    return full, rest, padded, halved, total


def store_block(ref, index, base, value, rows, width):
    full, rest, padded, halved, _ = block_form(rows, width)
    for j in range(full):
        at = base + j * padded
        ref[index, at : at + rows, :] = value[:, j * LANES : (j + 1) * LANES]
    if rest:
        at = base + full * padded
        tail = value[:, full * LANES : width]
        if halved:
            half = rows // 2
            ref[index, at : at + half, 0:rest] = tail[:half]
            ref[index, at : at + half, LANES // 2 : LANES // 2 + rest] = tail[half:]
        else:
            ref[index, at : at + rows, 0:rest] = tail


def load_pieces(ref, index, base, rows, width):
    full, rest, padded, halved, _ = block_form(rows, width)
    pieces = []
    for j in range(full):
        at = base + j * padded
        pieces.append(ref[index, at : at + rows, :])
    if rest:
        at = base + full * padded
        if halved:
            half = rows // 2
            block = ref[index, at : at + half, :]
            pieces.append(
                jnp.concatenate(
                    [block[:, 0:rest], block[:, LANES // 2 : LANES // 2 + rest]], axis=0
                )
            )
        else:
            pieces.append(ref[index, at : at + rows, 0:rest])
    return pieces


def load_block(ref, index, base, rows, width):
    pieces = load_pieces(ref, index, base, rows, width)
    return pieces[0] if len(pieces) == 1 else jnp.concatenate(pieces, axis=1)


def unpack_columns(ref, base, out_ref, shards, rows, width):
    if width % LANES:
        tail = width // LANES * LANES
        out_ref[:, tail:] = jnp.zeros((out_ref.shape[0], LANES), F32)
    for source in range(shards):
        for j, piece in enumerate(load_pieces(ref, source, base, rows, width)):
            lanes = piece.shape[1]
            out_ref[source * rows : (source + 1) * rows, j * LANES : j * LANES + lanes] = piece


def pack_columns(value_ref, ref, base, shards, rows, width):
    for dest in range(shards):
        block = value_ref[dest * rows : (dest + 1) * rows, 0:width]
        store_block(ref, dest, base, block, rows, width)


def parts_of(value):
    high = value.astype(BF16)
    return high, (value - high.astype(F32)).astype(BF16)


def product(left, right, contract=(1, 0)):
    dims = (((contract[0],), (contract[1],)), ((), ()))
    dot = functools.partial(lax.dot_general, dimension_numbers=dims, preferred_element_type=F32)
    return dot(left[0], right[0]) + (dot(left[0], right[1]) + dot(left[1], right[0]))


def call(kernel, outs, args, specs=None, out_specs=None, scratch=(), aliases=None, grid=()):
    single = isinstance(outs, tuple)
    shapes = [outs] if single else list(outs)
    shapes = [s if isinstance(s, jax.ShapeDtypeStruct) else jax.ShapeDtypeStruct(s, F32) for s in shapes]
    vmem = pl.BlockSpec(memory_space=pltpu.VMEM)
    specs = specs or [None] * len(args)
    result = pl.pallas_call(
        kernel,
        out_shape=shapes,
        grid=grid,
        in_specs=[s or vmem for s in specs],
        out_specs=out_specs or [vmem] * len(shapes),
        scratch_shapes=list(scratch),
        input_output_aliases=aliases or {},
        compiler_params=pltpu.CompilerParams(vmem_limit_bytes=32 * 2**20),
    )(*args)
    return result[0] if single else result


SMEM = pl.BlockSpec(memory_space=pltpu.SMEM)
ANY = pl.BlockSpec(memory_space=pl.ANY)
HBM = pl.BlockSpec(memory_space=pltpu.HBM)


def body(
    gradient,
    weight,
    first_moment,
    second_moment,
    left_basis,
    left_gram,
    owner_table,
    bias_gradient,
    bias_weight,
    bias_first,
    bias_second,
):
    shards = lax.axis_size("shard")
    ranks = lax.axis_size("tensor")
    assert ranks == 4 and MCAP == 2
    layer_total = owner_table.shape[0]
    matrix_total = 5 * layer_total
    rows = gradient.shape[0]
    line = gradient.shape[2]
    columns = line // (sum(TYPE_TILES) * layer_total)
    width = rows * shards
    assert columns * ranks == width and columns <= LANES
    groups, share = place_columns(layer_total, shards, columns)
    slots = max(len(group) for group in groups)
    wide = -(-share // LANES) * LANES
    strip = slots * columns
    owned = MCAP * columns
    tile_rows = block_form(rows, share)[4]
    strip_rows = block_form(rows, strip)[4]
    owned_rows = block_form(rows, owned)[4]
    slot_matrix = [[piece[0] for piece in group] for group in groups]
    edges = np.full((shards, slots + 1), share, np.int32)
    for group, pieces in enumerate(groups):
        edges[group, 0] = 0
        edges[group, 1 : len(pieces) + 1] = np.cumsum([piece[2] for piece in pieces])

    my_group = lax.axis_index("shard")
    my_rank = lax.axis_index("tensor").astype(jnp.int32)
    edge_table = jnp.asarray(edges.reshape(-1))
    group_arg = my_group.astype(jnp.int32).reshape(1)
    rank_arg = my_rank.reshape(1)
    owners = owner_table.reshape(-1)
    core_pairs = [(r, r ^ 1) for r in range(ranks)]
    chip_pairs = [(r, r ^ 2) for r in range(ranks)]

    def over_core(value):
        return lax.ppermute(value, "tensor", core_pairs)

    def over_chip(value):
        return lax.ppermute(value, "tensor", chip_pairs)

    def exchange(value):
        return lax.all_to_all(value, "shard", split_axis=0, concat_axis=0, tiled=True)

    together = lax.optimization_barrier

    def in_hbm(value):
        return pltpu.with_memory_space_constraint(value, pltpu.HBM)


    line_tiles = line // LANES
    assert line_tiles * LANES == line
    dense = (rows * line_tiles, LANES)
    line_scratch = pltpu.VMEM((rows, line), F32)

    def open_line(ref, line_ref):
        for j in range(line_tiles):
            line_ref[:, j * LANES : (j + 1) * LANES] = ref[pl.ds(j, rows, stride=line_tiles), :]

    def close_line(line_ref, ref):
        for j in range(line_tiles):
            ref[pl.ds(j, rows, stride=line_tiles), :] = line_ref[:, j * LANES : (j + 1) * LANES]

    def gather_line(ref, group):
        pieces = [ref[:, at : at + length] for _, at, length in groups[group]]
        return pieces[0] if len(pieces) == 1 else jnp.concatenate(pieces, axis=1)

    def send_tiles(ref, line_ref, out_ref, base):
        open_line(ref, line_ref)
        for group in range(shards):
            store_block(out_ref, group, base, gather_line(line_ref, group), rows, share)

    def fill_owned_table(owner_ref, table_ref, count_ref):
        for group in range(shards):
            count_ref[group] = 0
            for m in range(MCAP):
                table_ref[group * MCAP + m] = -1

        def take(i, carry):
            owner = owner_ref[i]
            rank = count_ref[owner]
            table_ref[owner * MCAP + rank] = i
            count_ref[owner] = rank + 1
            return carry

        lax.fori_loop(0, matrix_total, take, 0)

    def send_owned(stage_ref, table_ref, out_ref, base):
        for group in range(shards):
            held = []
            for m in range(MCAP):
                matrix = table_ref[group * MCAP + m]
                block = stage_ref[jnp.maximum(matrix, 0)]
                held.append(jnp.where(matrix >= 0, block, 0.0))
            store_block(out_ref, group, base, jnp.concatenate(held, axis=1), rows, owned)

    count_scratch = pltpu.SMEM((shards,), jnp.int32)
    stage_scratch = pltpu.VMEM((matrix_total, rows, columns), F32)

    def slot_masks(group_ref, edges_ref):
        lane = lax.broadcasted_iota(jnp.int32, (1, wide), 1)
        at = group_ref[0] * (slots + 1)
        return [(lane >= edges_ref[at + k]) & (lane < edges_ref[at + k + 1]) for k in range(slots)]


    def pack_gradient(grad_ref, basis_ref, out_ref, line_ref, dense_ref, near_ref, sems):
        fetch_basis = pltpu.make_async_copy(basis_ref, near_ref, sems.at[0])
        fetch_basis.start()
        fetch = pltpu.make_async_copy(grad_ref, dense_ref, sems.at[1])
        fetch.start()
        fetch_basis.wait()
        basis = near_ref[:, 0, :]
        for group in range(shards):
            held = [
                basis[:, matrix * columns : (matrix + 1) * columns]
                for matrix in slot_matrix[group]
            ]
            held += [jnp.zeros((rows, columns), F32)] * (slots - len(held))
            store_block(out_ref, group, 0, jnp.concatenate(held, axis=1), rows, strip)
        fetch.wait()
        send_tiles(dense_ref, line_ref, out_ref, strip_rows)

    grad_dense = gradient.reshape(dense)
    basis_hbm = in_hbm(left_basis)
    send_one = call(
        pack_gradient,
        (shards, strip_rows + tile_rows, LANES),
        (in_hbm(grad_dense), basis_hbm),
        specs=[HBM, HBM],
        scratch=[
            line_scratch,
            pltpu.VMEM(dense, F32),
            pltpu.VMEM(left_basis.shape, F32),
            pltpu.SemaphoreType.DMA((2,)),
        ],
    )
    came_one = exchange(send_one)


    half_groups = shards // 2
    half_total = matrix_total // 2
    assert half_groups * 2 == shards and shards & (shards - 1) == 0
    assert all(
        (matrix >= half_total) == (group >= half_groups)
        for group in range(shards)
        for matrix in slot_matrix[group]
    )
    slot_table = np.full((shards, slots), -1, np.int32)
    for group in range(shards):
        slot_table[group, : len(slot_matrix[group])] = slot_matrix[group]
    slot_table = jnp.asarray(slot_table.reshape(-1))


    def pack_moments(
        owner_ref,
        second_ref,
        first_ref,
        grad_ref,
        basis_ref,
        out_ref,
        new_ref,
        table_ref,
        count_ref,
        stage_ref,
        line_ref,
    ):
        fill_owned_table(owner_ref, table_ref, count_ref)
        basis = basis_ref[:, 0, :]
        for matrix in range(matrix_total):
            stage_ref[matrix] = basis[:, matrix * columns : (matrix + 1) * columns]
        send_owned(stage_ref, table_ref, out_ref, 0)
        send_tiles(second_ref, line_ref, out_ref, owned_rows)
        send_tiles(first_ref, line_ref, out_ref, owned_rows + tile_rows)
        new_ref[...] = 0.9 * first_ref[...] + 0.1 * grad_ref[...]

    vmem = pl.BlockSpec(memory_space=pltpu.VMEM)
    send_two, first_out, owned_table = call(
        pack_moments,
        [
            (shards, owned_rows + 2 * tile_rows, LANES),
            dense,
            jax.ShapeDtypeStruct((shards * MCAP,), jnp.int32),
        ],
        (
            owners,
            second_moment.reshape(dense),
            first_moment.reshape(dense),
            grad_dense,
            left_basis,
        ),
        specs=[SMEM, None, None, None, None],
        out_specs=[vmem, vmem, SMEM],
        scratch=[count_scratch, stage_scratch, line_scratch],
    )
    came_one, send_two = together((came_one, send_two))
    came_two = exchange(send_two)


    def gram_partials(
        group_ref, rank_ref, edges_ref, came_ref, grad_ref, strips_ref, kept_ref, core_ref, turned_ref
    ):
        unpack_columns(came_ref, strip_rows, grad_ref, shards, rows, share)
        for source in range(shards):
            strips_ref[source] = came_ref[source, 0:strip_rows, :]
        turned_ref[...] = jnp.zeros_like(turned_ref)
        for rank in range(ranks):
            turned_ref[rank * LANES : rank * LANES + columns, :] = grad_ref[
                rank * columns : (rank + 1) * columns, :
            ]
        right = parts_of(turned_ref[...])
        grams = []
        for mask in slot_masks(group_ref, edges_ref):
            left = parts_of(jnp.where(mask, grad_ref[...], 0.0))
            grams.append(product(left, right, (1, 1)))
        odd = rank_ref[0] % 2 == 1
        for chip in range(2):
            for group in range(shards):
                at = slice(group * rows, (group + 1) * rows)
                low = [g[at, 2 * chip * LANES : 2 * chip * LANES + columns] for g in grams]
                high = [g[at, (2 * chip + 1) * LANES : (2 * chip + 1) * LANES + columns] for g in grams]
                low, high = jnp.concatenate(low, axis=1), jnp.concatenate(high, axis=1)
                mine, other = jnp.where(odd, high, low), jnp.where(odd, low, high)
                store_block(kept_ref.at[chip], group, 0, mine, rows, strip)
                store_block(core_ref.at[chip], group, 0, other, rows, strip)

    strip_shape = (shards, strip_rows, LANES)
    grad_full, strips_own, kept, for_core = call(
        gram_partials,
        [(width, wide), strip_shape, (2,) + strip_shape, (2,) + strip_shape],
        (group_arg, rank_arg, edge_table, came_one),
        specs=[SMEM, SMEM, SMEM, None],
        scratch=[pltpu.VMEM((ranks * LANES, wide), F32)],
    )


    def add_core(rank_ref, kept_ref, came_ref, mine_ref, far_ref):
        chip = rank_ref[0] // 2
        mine_ref[...] = kept_ref[chip] + came_ref[chip]
        far_ref[...] = kept_ref[1 - chip] + came_ref[1 - chip]

    gram_mine, for_chip = call(
        add_core,
        [strip_shape, strip_shape],
        (rank_arg, kept, over_core(for_core)),
        specs=[SMEM, None, None],
    )
    came_chip = over_chip(for_chip)


    def sum_strips(group_ref, mine_ref, came_ref, *out_refs):
        place = group_ref[0] % half_groups
        for k, out_ref in enumerate(out_refs):
            for j in range(2):
                at = (place ^ k) + j * half_groups
                out_ref[j] = mine_ref[at] + came_ref[at]

    gram_blocks = call(
        sum_strips,
        [(2, strip_rows, LANES)] * half_groups,
        (group_arg, gram_mine, came_chip),
        specs=[SMEM, None, None],
    )
    *gram_blocks, strips_own = together((*gram_blocks, strips_own))
    gram_blocks = [gram_blocks[0]] + [
        lax.ppermute(gram_blocks[k], "shard", [(s, s ^ k) for s in range(shards)])
        for k in range(1, half_groups)
    ]


    strips_chip = over_chip(strips_own)
    *gram_blocks, strips_chip = together((*gram_blocks, strips_chip))


    def split_owned(rank_ref, came_ref, *refs):
        spread = len(refs) == 4
        mine_ref, other_ref = refs[-3:-1] if spread else refs
        odd = rank_ref[0] % 2 == 1
        for block_at in range(shards):
            at = slice(block_at * rows, (block_at + 1) * rows)
            if spread:
                place, base = block_at % half_groups, block_at // half_groups * owned_rows
                block = load_block(came_ref, place, base, rows, owned) + load_block(
                    came_ref, half_groups + place, base, rows, owned
                )
            else:
                block = load_block(came_ref, block_at, 0, rows, owned)
            strips = [block[:, m * columns : (m + 1) * columns] for m in range(MCAP)]
            mine_ref[at, 0:columns] = jnp.where(odd, strips[1], strips[0])
            other_ref[at, 0:columns] = jnp.where(odd, strips[0], strips[1])
            if spread:
                for m in range(MCAP):
                    refs[-1][m, at, 0:columns] = strips[m]
        if spread:
            for m in range(MCAP):
                refs[0][m] = refs[-1][m].T[0:columns]

    def join_half(rank_ref, mine_ref, other_ref, half_ref):
        odd = rank_ref[0] % 2 == 1
        for group in range(shards):
            at = slice(group * rows, (group + 1) * rows)
            mine, other = mine_ref[at, 0:columns], other_ref[at, 0:columns]
            both = [jnp.where(odd, other, mine), jnp.where(odd, mine, other)]
            store_block(half_ref, group, 0, jnp.concatenate(both, axis=1), rows, owned)

    def collect(came, spread):
        *strips, mine, other = call(
            split_owned,
            [(MCAP, columns, width)] * spread + [(width, LANES), (width, LANES)],
            (rank_arg, came),
            specs=[SMEM, None],
            scratch=[pltpu.VMEM((MCAP, width, LANES), F32)] * spread,
        )
        half = call(
            join_half,
            (shards, owned_rows, LANES),
            (rank_arg, mine, over_core(other)),
            specs=[SMEM, None, None],
        )
        return *strips, half, over_chip(half)


    def new_grams(group_ref, table_ref, slot_ref, gram_ref, *refs):
        came, (out_ref, stage_ref, near_ref, sem) = refs[:half_groups], refs[half_groups:]
        fetch = pltpu.make_async_copy(gram_ref, near_ref, sem)
        fetch.start()
        group = group_ref[0]
        half = group // half_groups
        stage_ref[...] = jnp.zeros_like(stage_ref)
        for k, came_ref in enumerate(came):
            for j in range(2):
                block = load_block(came_ref, j, 0, rows, strip)
                for m in range(slots):
                    matrix = slot_ref[(group ^ k) * slots + m]
                    at = jnp.where(matrix >= 0, matrix, matrix_total)
                    part = block[:, m * columns : (m + 1) * columns]
                    stage_ref[j, at] = stage_ref[j, at] + 0.05 * part
        fetch.wait()
        old = 0.95 * near_ref[:, 0, :]
        for matrix in range(matrix_total):
            own = old[:, matrix * columns : (matrix + 1) * columns]
            stage_ref[half, matrix] = stage_ref[half, matrix] + own
        for dest in range(shards):
            for j in range(2):
                held = []
                for m in range(MCAP):
                    matrix = table_ref[dest * MCAP + m]
                    block = stage_ref[j, jnp.maximum(matrix, 0)]
                    held.append(jnp.where(matrix >= 0, block, 0.0))
                block = jnp.concatenate(held, axis=1)
                store_block(out_ref, dest, j * owned_rows, block, rows, owned)

    send_four = call(
        new_grams,
        (shards, 2 * owned_rows, LANES),
        (
            group_arg,
            owned_table,
            slot_table,
            in_hbm(left_gram),
            *gram_blocks,
        ),
        specs=[SMEM, SMEM, SMEM, HBM] + [None] * half_groups,
        scratch=[
            pltpu.VMEM((2, matrix_total + 1, rows, columns), F32),
            pltpu.VMEM(left_gram.shape, F32),
            pltpu.SemaphoreType.DMA(()),
        ],
    )
    send_four = in_hbm(send_four)
    came_two, send_four = together((came_two, send_four))
    came_four = in_hbm(exchange(send_four))
    pair = over_core(jnp.stack([strips_own, strips_chip]))


    def rotate_gradient(
        group_ref,
        rank_ref,
        edges_ref,
        own_ref,
        chip_ref,
        pair_ref,
        grad_ref,
        basis_ref,
        hat_ref,
    ):
        rank = rank_ref[0]
        for group in range(shards):
            blocks = [
                load_block(ref, group, 0, rows, strip)
                for ref in (own_ref, pair_ref.at[0], chip_ref, pair_ref.at[1])
            ]
            at = slice(group * rows, (group + 1) * rows)
            for k in range(slots):
                cut = [block[:, k * columns : (k + 1) * columns] for block in blocks]
                low = [jnp.where(rank % 2 == 0, cut[0 + h], cut[1 + h]) for h in (0, 2)]
                odd = [jnp.where(rank % 2 == 0, cut[1 + h], cut[0 + h]) for h in (0, 2)]
                first = rank < 2
                ordered = [
                    jnp.where(first, low[0], low[1]),
                    jnp.where(first, odd[0], odd[1]),
                    jnp.where(first, low[1], low[0]),
                    jnp.where(first, odd[1], odd[0]),
                ]
                basis_ref[k, at, :] = jnp.concatenate(ordered, axis=1)
        grad = parts_of(grad_ref[...])
        hat = jnp.zeros((width, wide), F32)
        for k, mask in enumerate(slot_masks(group_ref, edges_ref)):
            hat = jnp.where(mask, product(parts_of(basis_ref[k].T), grad), hat)
        hat_ref[...] = hat

    basis_full, hat_full = call(
        rotate_gradient,
        [(slots, width, width), (width, wide)],
        (group_arg, rank_arg, edge_table, strips_own, strips_chip, pair, grad_full),
        specs=[SMEM, SMEM, SMEM] + [None] * 4,
    )

    basis_half, basis_far = collect(came_two, 0)


    def directions(
        group_ref,
        edges_ref,
        came_ref,
        grad_ref,
        hat_ref,
        basis_ref,
        send_ref,
        moment_ref,
        second_ref,
    ):
        unpack_columns(came_ref, owned_rows, second_ref, shards, rows, share)
        second_ref[...] = 0.95 * second_ref[...] + 0.05 * hat_ref[...] * hat_ref[...]
        unpack_columns(came_ref, owned_rows + tile_rows, moment_ref, shards, rows, share)
        masks = slot_masks(group_ref, edges_ref)
        moment = parts_of(0.9 * moment_ref[...] + 0.1 * grad_ref[...])
        hat = jnp.zeros((width, wide), F32)
        for k, mask in enumerate(masks):
            hat = jnp.where(mask, product(parts_of(basis_ref[k].T), moment), hat)
        step = parts_of(adam_direction(hat, second_ref[...]))
        turned = jnp.zeros((width, wide), F32)
        for k, mask in enumerate(masks):
            turned = jnp.where(mask, product(parts_of(basis_ref[k]), step), turned)
        moment_ref[...] = turned
        pack_columns(moment_ref, send_ref, 0, shards, rows, share)
        pack_columns(second_ref, send_ref, tile_rows, shards, rows, share)

    send_five = call(
        directions,
        (shards, 2 * tile_rows, LANES),
        (group_arg, edge_table, came_two, grad_full, hat_full, basis_full),
        specs=[SMEM, SMEM] + [None] * 4,
        scratch=[pltpu.VMEM((width, wide), F32)] * 2,
    )
    came_four, send_five = together((came_four, send_five))
    came_five = exchange(send_five)


    gram_out, gram_half, gram_far = collect(came_four, 1)

    def refresh(
        rank_ref,
        basis_half_ref,
        basis_far_ref,
        gram_half_ref,
        gram_far_ref,
        weight_ref,
        mine_ref,
        other_ref,
        weight_out_ref,
        basis_ref,
        gram_ref,
        sem,
    ):
        fetch = pltpu.make_async_copy(weight_ref, weight_out_ref, sem)
        fetch.start()
        rank = rank_ref[0]
        first = rank < 2
        for out, half_ref, far_ref in (
            (basis_ref, basis_half_ref, basis_far_ref),
            (gram_ref, gram_half_ref, gram_far_ref),
        ):
            for group in range(shards):
                half = load_block(half_ref, group, 0, rows, owned)
                far = load_block(far_ref, group, 0, rows, owned)
                both = [jnp.where(first, half, far), jnp.where(first, far, half)]
                out[group * rows : (group + 1) * rows, :] = jnp.concatenate(both, axis=1)
        power = product(parts_of(basis_ref[...].T), parts_of(gram_ref[...]))
        frame = power / jnp.sqrt(jnp.sum(power * power) + 1e-06)
        for _ in range(NS_STEPS):
            pieces = parts_of(frame)
            square = product(pieces, pieces, (1, 1))
            frame = 1.5 * frame - 0.5 * product(parts_of(square), pieces)
        strips = [frame[r * columns : (r + 1) * columns] for r in range(ranks)]
        low = jnp.where(first, strips[0], strips[2])
        odd = jnp.where(first, strips[1], strips[3])
        even_core = rank % 2 == 0
        mine_ref[...] = jnp.where(even_core, low, odd)
        other_ref[...] = jnp.where(even_core, odd, low)
        fetch.wait()

    weight_dense = in_hbm(weight.reshape(dense))
    frame_mine, frame_other, weight_near = call(
        refresh,
        [(columns, width), (columns, width), dense],
        (rank_arg, basis_half, basis_far, gram_half, gram_far, weight_dense),
        specs=[SMEM] + [None] * 4 + [HBM],
        scratch=[pltpu.VMEM((width, width), F32)] * 2 + [pltpu.SemaphoreType.DMA(())],
    )
    frame_came = over_core(frame_other)
    pair_out = jnp.where(
        my_rank % 2 == 0,
        jnp.stack([frame_mine, frame_came]),
        jnp.stack([frame_came, frame_mine]),
    )
    came_five, pair_out, gram_out, first_out = together((came_five, pair_out, gram_out, first_out))


    def line_from(came_ref, base, line_ref):
        for group in range(shards):
            block = load_block(came_ref, group, base, rows, share)
            offset = 0
            for _, at, length in groups[group]:
                line_ref[:, at : at + length] = block[:, offset : offset + length]
                offset += length

    def take_back(came_ref, weight_ref, weight_out_ref, second_out_ref, line_ref):
        line_from(came_ref, 0, line_ref)
        close_line(line_ref, weight_out_ref)
        old = weight_ref[...]
        weight_out_ref[...] = old - 0.01 * (weight_out_ref[...] + 0.1 * old)
        line_from(came_ref, tile_rows, line_ref)
        close_line(line_ref, second_out_ref)

    weight_out, second_out = call(
        take_back, [dense, dense], (came_five, weight_near), scratch=[line_scratch]
    )

    bias_first_new = 0.9 * bias_first + 0.1 * bias_gradient
    bias_second_new = 0.95 * bias_second + 0.05 * bias_gradient * bias_gradient
    bias_updated = bias_weight - 0.01 * adam_direction(bias_first_new, bias_second_new)
    flat = (rows, 1, line)
    return (
        weight_out.reshape(flat),
        first_out.reshape(flat),
        second_out.reshape(flat),
        pair_out.transpose(0, 2, 1)[None],
        gram_out.transpose(0, 2, 1)[None],
        bias_updated,
        bias_first_new,
        bias_second_new,
    )


def solution(mesh):
    tiles = P("shard", "tensor", None)
    bias = P(("shard", "tensor"))
    owned = P("shard", None, None, "tensor")
    in_specs = (tiles,) * 6 + (P(),) + (bias,) * 4
    out_specs = (tiles,) * 3 + (owned,) * 2 + (bias,) * 3
    return jax.shard_map(body, mesh=mesh, in_specs=in_specs, out_specs=out_specs, check_vma=False)
```

```python
import functools

import jax
import jax.numpy as jnp
import numpy as np
from jax import lax
from jax.experimental import pallas as pl
from jax.experimental.pallas import tpu as pltpu
from jax.sharding import PartitionSpec as P

MCAP = 2
STEP = 10
NS_STEPS = 5
TYPE_TILES = (3, 1, 4, 4, 6)
LANES = 128
F32 = jnp.float32
BF16 = jnp.bfloat16
CORR_ONE = 1.0 - 0.9**STEP
CORR_TWO = 1.0 - 0.95**STEP


def adam_direction(moment_hat, second_new):
    return moment_hat / CORR_ONE / (jnp.sqrt(second_new / CORR_TWO) + 1e-08)


def place_columns(layer_total, shards, columns):
    sizes = [tiles * columns for tiles in TYPE_TILES] * layer_total
    starts = np.concatenate([[0], np.cumsum(sizes)]).tolist()
    share = starts[-1] // shards
    assert share * shards == starts[-1]
    small = [i for i, size in enumerate(sizes) if size <= share]
    groups = [[] for _ in range(shards)]
    room = [share] * shards
    if len(small) <= shards:
        for group, i in enumerate(small):
            groups[group].append((i, starts[i], sizes[i]))
            room[group] -= sizes[i]
        rest = [i for i in range(len(sizes)) if i not in small]
    else:
        rest = list(range(len(sizes)))
    group = 0
    for i in rest:
        at, left = starts[i], sizes[i]
        while left:
            while not room[group]:
                group += 1
            take = min(left, room[group])
            groups[group].append((i, at, take))
            room[group] -= take
            at += take
            left -= take
    return groups, share


def block_form(rows, width):
    full, rest = divmod(width, LANES)
    padded = -(-rows // 8) * 8
    halved = 0 < rest <= LANES // 2 and rows % 16 == 0
    total = full * padded + (0 if not rest else rows // 2 if halved else padded)
    return full, rest, padded, halved, total


def store_block(ref, index, base, value, rows, width):
    full, rest, padded, halved, _ = block_form(rows, width)
    for j in range(full):
        at = base + j * padded
        ref[index, at : at + rows, :] = value[:, j * LANES : (j + 1) * LANES]
    if rest:
        at = base + full * padded
        tail = value[:, full * LANES : width]
        if halved:
            half = rows // 2
            ref[index, at : at + half, 0:rest] = tail[:half]
            ref[index, at : at + half, LANES // 2 : LANES // 2 + rest] = tail[half:]
        else:
            ref[index, at : at + rows, 0:rest] = tail


def load_pieces(ref, index, base, rows, width):
    full, rest, padded, halved, _ = block_form(rows, width)
    pieces = []
    for j in range(full):
        at = base + j * padded
        pieces.append(ref[index, at : at + rows, :])
    if rest:
        at = base + full * padded
        if halved:
            half = rows // 2
            block = ref[index, at : at + half, :]
            pieces.append(
                jnp.concatenate(
                    [block[:, 0:rest], block[:, LANES // 2 : LANES // 2 + rest]], axis=0
                )
            )
        else:
            pieces.append(ref[index, at : at + rows, 0:rest])
    return pieces


def load_block(ref, index, base, rows, width):
    pieces = load_pieces(ref, index, base, rows, width)
    return pieces[0] if len(pieces) == 1 else jnp.concatenate(pieces, axis=1)


def unpack_columns(ref, base, out_ref, shards, rows, width):
    if width % LANES:
        tail = width // LANES * LANES
        out_ref[:, tail:] = jnp.zeros((out_ref.shape[0], LANES), F32)
    for source in range(shards):
        for j, piece in enumerate(load_pieces(ref, source, base, rows, width)):
            lanes = piece.shape[1]
            out_ref[source * rows : (source + 1) * rows, j * LANES : j * LANES + lanes] = piece


def pack_columns(value_ref, ref, base, shards, rows, width):
    for dest in range(shards):
        block = value_ref[dest * rows : (dest + 1) * rows, 0:width]
        store_block(ref, dest, base, block, rows, width)


def parts_of(value):
    high = value.astype(BF16)
    return high, (value - high.astype(F32)).astype(BF16)


def product(left, right, contract=(1, 0)):
    dims = (((contract[0],), (contract[1],)), ((), ()))
    dot = functools.partial(lax.dot_general, dimension_numbers=dims, preferred_element_type=F32)
    return dot(left[0], right[0]) + (dot(left[0], right[1]) + dot(left[1], right[0]))


def thirds_of(value):
    high = value.astype(BF16)
    rest = value - high.astype(F32)
    middle = rest.astype(BF16)
    return high, middle, (rest - middle.astype(F32)).astype(BF16)


def fine_product(left, right):
    dims = (((1,), (0,)), ((), ()))
    dot = functools.partial(lax.dot_general, dimension_numbers=dims, preferred_element_type=F32)
    small = dot(left[0], right[2]) + dot(left[1], right[1]) + dot(left[2], right[0])
    return dot(left[0], right[0]) + (dot(left[0], right[1]) + dot(left[1], right[0]) + small)


def call(kernel, outs, args, specs=None, out_specs=None, scratch=(), aliases=None, grid=()):
    single = isinstance(outs, tuple)
    shapes = [outs] if single else list(outs)
    shapes = [s if isinstance(s, jax.ShapeDtypeStruct) else jax.ShapeDtypeStruct(s, F32) for s in shapes]
    vmem = pl.BlockSpec(memory_space=pltpu.VMEM)
    specs = specs or [None] * len(args)
    result = pl.pallas_call(
        kernel,
        out_shape=shapes,
        grid=grid,
        in_specs=[s or vmem for s in specs],
        out_specs=out_specs or [vmem] * len(shapes),
        scratch_shapes=list(scratch),
        input_output_aliases=aliases or {},
        compiler_params=pltpu.CompilerParams(vmem_limit_bytes=32 * 2**20),
    )(*args)
    return result[0] if single else result


SMEM = pl.BlockSpec(memory_space=pltpu.SMEM)
ANY = pl.BlockSpec(memory_space=pl.ANY)
HBM = pl.BlockSpec(memory_space=pltpu.HBM)


def body(
    gradient,
    weight,
    first_moment,
    second_moment,
    left_basis,
    left_gram,
    owner_table,
    bias_gradient,
    bias_weight,
    bias_first,
    bias_second,
):
    shards = lax.axis_size("shard")
    ranks = lax.axis_size("tensor")
    assert ranks == 4 and MCAP == 2
    layer_total = owner_table.shape[0]
    matrix_total = 5 * layer_total
    rows = gradient.shape[0]
    line = gradient.shape[2]
    columns = line // (sum(TYPE_TILES) * layer_total)
    width = rows * shards
    assert columns * ranks == width and columns <= LANES
    groups, share = place_columns(layer_total, shards, columns)
    slots = max(len(group) for group in groups)
    wide = -(-share // LANES) * LANES
    strip = slots * columns
    owned = MCAP * columns
    tile_rows = block_form(rows, share)[4]
    strip_rows = block_form(rows, strip)[4]
    owned_rows = block_form(rows, owned)[4]
    slot_matrix = [[piece[0] for piece in group] for group in groups]
    edges = np.full((shards, slots + 1), share, np.int32)
    for group, pieces in enumerate(groups):
        edges[group, 0] = 0
        edges[group, 1 : len(pieces) + 1] = np.cumsum([piece[2] for piece in pieces])

    my_group = lax.axis_index("shard")
    my_rank = lax.axis_index("tensor").astype(jnp.int32)
    edge_table = jnp.asarray(edges.reshape(-1))
    group_arg = my_group.astype(jnp.int32).reshape(1)
    rank_arg = my_rank.reshape(1)
    owners = owner_table.reshape(-1)
    core_pairs = [(r, r ^ 1) for r in range(ranks)]
    chip_pairs = [(r, r ^ 2) for r in range(ranks)]

    def over_core(value):
        return lax.ppermute(value, "tensor", core_pairs)

    def over_chip(value):
        return lax.ppermute(value, "tensor", chip_pairs)

    def exchange(value):
        return lax.all_to_all(value, "shard", split_axis=0, concat_axis=0, tiled=True)

    together = lax.optimization_barrier

    def in_hbm(value):
        return pltpu.with_memory_space_constraint(value, pltpu.HBM)


    line_tiles = line // LANES
    assert line_tiles * LANES == line
    dense = (rows * line_tiles, LANES)
    line_scratch = pltpu.VMEM((rows, line), F32)

    def open_line(ref, line_ref):
        for j in range(line_tiles):
            line_ref[:, j * LANES : (j + 1) * LANES] = ref[pl.ds(j, rows, stride=line_tiles), :]

    def close_line(line_ref, ref):
        for j in range(line_tiles):
            ref[pl.ds(j, rows, stride=line_tiles), :] = line_ref[:, j * LANES : (j + 1) * LANES]

    def gather_line(ref, group):
        pieces = [ref[:, at : at + length] for _, at, length in groups[group]]
        return pieces[0] if len(pieces) == 1 else jnp.concatenate(pieces, axis=1)

    def send_tiles(ref, line_ref, out_ref, base):
        open_line(ref, line_ref)
        for group in range(shards):
            store_block(out_ref, group, base, gather_line(line_ref, group), rows, share)

    def fill_owned_table(owner_ref, table_ref, count_ref):
        for group in range(shards):
            count_ref[group] = 0
            for m in range(MCAP):
                table_ref[group * MCAP + m] = -1

        def take(i, carry):
            owner = owner_ref[i]
            rank = count_ref[owner]
            table_ref[owner * MCAP + rank] = i
            count_ref[owner] = rank + 1
            return carry

        lax.fori_loop(0, matrix_total, take, 0)

    def send_owned(stage_ref, table_ref, out_ref, base):
        for group in range(shards):
            held = []
            for m in range(MCAP):
                matrix = table_ref[group * MCAP + m]
                block = stage_ref[jnp.maximum(matrix, 0)]
                held.append(jnp.where(matrix >= 0, block, 0.0))
            store_block(out_ref, group, base, jnp.concatenate(held, axis=1), rows, owned)

    count_scratch = pltpu.SMEM((shards,), jnp.int32)
    stage_scratch = pltpu.VMEM((matrix_total, rows, columns), F32)

    def slot_masks(group_ref, edges_ref):
        lane = lax.broadcasted_iota(jnp.int32, (1, wide), 1)
        at = group_ref[0] * (slots + 1)
        return [(lane >= edges_ref[at + k]) & (lane < edges_ref[at + k + 1]) for k in range(slots)]


    def pack_gradient(grad_ref, basis_ref, out_ref, line_ref, dense_ref, near_ref, sems):
        fetch_basis = pltpu.make_async_copy(basis_ref, near_ref, sems.at[0])
        fetch_basis.start()
        fetch = pltpu.make_async_copy(grad_ref, dense_ref, sems.at[1])
        fetch.start()
        fetch_basis.wait()
        basis = near_ref[:, 0, :]
        for group in range(shards):
            held = [
                basis[:, matrix * columns : (matrix + 1) * columns]
                for matrix in slot_matrix[group]
            ]
            held += [jnp.zeros((rows, columns), F32)] * (slots - len(held))
            store_block(out_ref, group, 0, jnp.concatenate(held, axis=1), rows, strip)
        fetch.wait()
        send_tiles(dense_ref, line_ref, out_ref, strip_rows)

    grad_dense = gradient.reshape(dense)
    basis_hbm = in_hbm(left_basis)
    send_one = call(
        pack_gradient,
        (shards, strip_rows + tile_rows, LANES),
        (in_hbm(grad_dense), basis_hbm),
        specs=[HBM, HBM],
        scratch=[
            line_scratch,
            pltpu.VMEM(dense, F32),
            pltpu.VMEM(left_basis.shape, F32),
            pltpu.SemaphoreType.DMA((2,)),
        ],
    )
    came_one = exchange(send_one)


    half_groups = shards // 2
    half_total = matrix_total // 2
    assert half_groups * 2 == shards and shards & (shards - 1) == 0
    assert all(
        (matrix >= half_total) == (group >= half_groups)
        for group in range(shards)
        for matrix in slot_matrix[group]
    )
    slot_table = np.full((shards, slots), -1, np.int32)
    for group in range(shards):
        slot_table[group, : len(slot_matrix[group])] = slot_matrix[group]
    slot_table = jnp.asarray(slot_table.reshape(-1))


    def pack_moments(
        owner_ref,
        second_ref,
        first_ref,
        grad_ref,
        basis_ref,
        out_ref,
        new_ref,
        table_ref,
        count_ref,
        stage_ref,
        line_ref,
    ):
        fill_owned_table(owner_ref, table_ref, count_ref)
        basis = basis_ref[:, 0, :]
        for matrix in range(matrix_total):
            stage_ref[matrix] = basis[:, matrix * columns : (matrix + 1) * columns]
        send_owned(stage_ref, table_ref, out_ref, 0)
        send_tiles(second_ref, line_ref, out_ref, owned_rows)
        send_tiles(first_ref, line_ref, out_ref, owned_rows + tile_rows)
        new_ref[...] = 0.9 * first_ref[...] + 0.1 * grad_ref[...]

    vmem = pl.BlockSpec(memory_space=pltpu.VMEM)
    send_two, first_out, owned_table = call(
        pack_moments,
        [
            (shards, owned_rows + 2 * tile_rows, LANES),
            dense,
            jax.ShapeDtypeStruct((shards * MCAP,), jnp.int32),
        ],
        (
            owners,
            second_moment.reshape(dense),
            first_moment.reshape(dense),
            grad_dense,
            left_basis,
        ),
        specs=[SMEM, None, None, None, None],
        out_specs=[vmem, vmem, SMEM],
        scratch=[count_scratch, stage_scratch, line_scratch],
    )
    came_one, send_two = together((came_one, send_two))
    came_two = exchange(send_two)


    def gram_partials(
        group_ref, rank_ref, edges_ref, came_ref, grad_ref, strips_ref, kept_ref, core_ref, turned_ref
    ):
        unpack_columns(came_ref, strip_rows, grad_ref, shards, rows, share)
        for source in range(shards):
            strips_ref[source] = came_ref[source, 0:strip_rows, :]
        turned_ref[...] = jnp.zeros_like(turned_ref)
        for rank in range(ranks):
            turned_ref[rank * LANES : rank * LANES + columns, :] = grad_ref[
                rank * columns : (rank + 1) * columns, :
            ]
        right = parts_of(turned_ref[...])
        grams = []
        for mask in slot_masks(group_ref, edges_ref):
            left = parts_of(jnp.where(mask, grad_ref[...], 0.0))
            grams.append(product(left, right, (1, 1)))
        odd = rank_ref[0] % 2 == 1
        for chip in range(2):
            for group in range(shards):
                at = slice(group * rows, (group + 1) * rows)
                low = [g[at, 2 * chip * LANES : 2 * chip * LANES + columns] for g in grams]
                high = [g[at, (2 * chip + 1) * LANES : (2 * chip + 1) * LANES + columns] for g in grams]
                low, high = jnp.concatenate(low, axis=1), jnp.concatenate(high, axis=1)
                mine, other = jnp.where(odd, high, low), jnp.where(odd, low, high)
                store_block(kept_ref.at[chip], group, 0, mine, rows, strip)
                store_block(core_ref.at[chip], group, 0, other, rows, strip)

    strip_shape = (shards, strip_rows, LANES)
    grad_full, strips_own, kept, for_core = call(
        gram_partials,
        [(width, wide), strip_shape, (2,) + strip_shape, (2,) + strip_shape],
        (group_arg, rank_arg, edge_table, came_one),
        specs=[SMEM, SMEM, SMEM, None],
        scratch=[pltpu.VMEM((ranks * LANES, wide), F32)],
    )


    def add_core(rank_ref, kept_ref, came_ref, mine_ref, far_ref):
        chip = rank_ref[0] // 2
        mine_ref[...] = kept_ref[chip] + came_ref[chip]
        far_ref[...] = kept_ref[1 - chip] + came_ref[1 - chip]

    gram_mine, for_chip = call(
        add_core,
        [strip_shape, strip_shape],
        (rank_arg, kept, over_core(for_core)),
        specs=[SMEM, None, None],
    )
    came_chip = over_chip(for_chip)


    def sum_strips(group_ref, mine_ref, came_ref, *out_refs):
        place = group_ref[0] % half_groups
        for k, out_ref in enumerate(out_refs):
            for j in range(2):
                at = (place ^ k) + j * half_groups
                out_ref[j] = mine_ref[at] + came_ref[at]

    gram_blocks = call(
        sum_strips,
        [(2, strip_rows, LANES)] * half_groups,
        (group_arg, gram_mine, came_chip),
        specs=[SMEM, None, None],
    )
    *gram_blocks, strips_own = together((*gram_blocks, strips_own))
    gram_blocks = [gram_blocks[0]] + [
        lax.ppermute(gram_blocks[k], "shard", [(s, s ^ k) for s in range(shards)])
        for k in range(1, half_groups)
    ]


    strips_chip = over_chip(strips_own)
    *gram_blocks, strips_chip = together((*gram_blocks, strips_chip))


    def split_owned(rank_ref, came_ref, *refs):
        spread = len(refs) == 4
        mine_ref, other_ref = refs[-3:-1] if spread else refs
        odd = rank_ref[0] % 2 == 1
        for block_at in range(shards):
            at = slice(block_at * rows, (block_at + 1) * rows)
            if spread:
                place, base = block_at % half_groups, block_at // half_groups * owned_rows
                block = load_block(came_ref, place, base, rows, owned) + load_block(
                    came_ref, half_groups + place, base, rows, owned
                )
            else:
                block = load_block(came_ref, block_at, 0, rows, owned)
            strips = [block[:, m * columns : (m + 1) * columns] for m in range(MCAP)]
            mine_ref[at, 0:columns] = jnp.where(odd, strips[1], strips[0])
            other_ref[at, 0:columns] = jnp.where(odd, strips[0], strips[1])
            if spread:
                for m in range(MCAP):
                    refs[-1][m, at, 0:columns] = strips[m]
        if spread:
            for m in range(MCAP):
                refs[0][m] = refs[-1][m].T[0:columns]

    def join_half(rank_ref, mine_ref, other_ref, half_ref):
        odd = rank_ref[0] % 2 == 1
        for group in range(shards):
            at = slice(group * rows, (group + 1) * rows)
            mine, other = mine_ref[at, 0:columns], other_ref[at, 0:columns]
            both = [jnp.where(odd, other, mine), jnp.where(odd, mine, other)]
            store_block(half_ref, group, 0, jnp.concatenate(both, axis=1), rows, owned)

    def collect(came, spread):
        *strips, mine, other = call(
            split_owned,
            [(MCAP, columns, width)] * spread + [(width, LANES), (width, LANES)],
            (rank_arg, came),
            specs=[SMEM, None],
            scratch=[pltpu.VMEM((MCAP, width, LANES), F32)] * spread,
        )
        half = call(
            join_half,
            (shards, owned_rows, LANES),
            (rank_arg, mine, over_core(other)),
            specs=[SMEM, None, None],
        )
        return *strips, half, over_chip(half)


    def new_grams(group_ref, table_ref, slot_ref, gram_ref, *refs):
        came, (out_ref, stage_ref, near_ref, sem) = refs[:half_groups], refs[half_groups:]
        fetch = pltpu.make_async_copy(gram_ref, near_ref, sem)
        fetch.start()
        group = group_ref[0]
        half = group // half_groups
        stage_ref[...] = jnp.zeros_like(stage_ref)
        for k, came_ref in enumerate(came):
            for j in range(2):
                block = load_block(came_ref, j, 0, rows, strip)
                for m in range(slots):
                    matrix = slot_ref[(group ^ k) * slots + m]
                    at = jnp.where(matrix >= 0, matrix, matrix_total)
                    part = block[:, m * columns : (m + 1) * columns]
                    stage_ref[j, at] = stage_ref[j, at] + 0.05 * part
        fetch.wait()
        old = 0.95 * near_ref[:, 0, :]
        for matrix in range(matrix_total):
            own = old[:, matrix * columns : (matrix + 1) * columns]
            stage_ref[half, matrix] = stage_ref[half, matrix] + own
        for dest in range(shards):
            for j in range(2):
                held = []
                for m in range(MCAP):
                    matrix = table_ref[dest * MCAP + m]
                    block = stage_ref[j, jnp.maximum(matrix, 0)]
                    held.append(jnp.where(matrix >= 0, block, 0.0))
                block = jnp.concatenate(held, axis=1)
                store_block(out_ref, dest, j * owned_rows, block, rows, owned)

    send_four = call(
        new_grams,
        (shards, 2 * owned_rows, LANES),
        (
            group_arg,
            owned_table,
            slot_table,
            in_hbm(left_gram),
            *gram_blocks,
        ),
        specs=[SMEM, SMEM, SMEM, HBM] + [None] * half_groups,
        scratch=[
            pltpu.VMEM((2, matrix_total + 1, rows, columns), F32),
            pltpu.VMEM(left_gram.shape, F32),
            pltpu.SemaphoreType.DMA(()),
        ],
    )
    send_four = in_hbm(send_four)
    came_two, send_four = together((came_two, send_four))
    came_four = in_hbm(exchange(send_four))
    pair = over_core(jnp.stack([strips_own, strips_chip]))


    def rotate_gradient(
        group_ref,
        rank_ref,
        edges_ref,
        own_ref,
        chip_ref,
        pair_ref,
        grad_ref,
        basis_ref,
        hat_ref,
    ):
        rank = rank_ref[0]
        for group in range(shards):
            blocks = [
                load_block(ref, group, 0, rows, strip)
                for ref in (own_ref, pair_ref.at[0], chip_ref, pair_ref.at[1])
            ]
            at = slice(group * rows, (group + 1) * rows)
            for k in range(slots):
                cut = [block[:, k * columns : (k + 1) * columns] for block in blocks]
                low = [jnp.where(rank % 2 == 0, cut[0 + h], cut[1 + h]) for h in (0, 2)]
                odd = [jnp.where(rank % 2 == 0, cut[1 + h], cut[0 + h]) for h in (0, 2)]
                first = rank < 2
                ordered = [
                    jnp.where(first, low[0], low[1]),
                    jnp.where(first, odd[0], odd[1]),
                    jnp.where(first, low[1], low[0]),
                    jnp.where(first, odd[1], odd[0]),
                ]
                basis_ref[k, at, :] = jnp.concatenate(ordered, axis=1)
        grad = thirds_of(grad_ref[...])
        hat = jnp.zeros((width, wide), F32)
        for k, mask in enumerate(slot_masks(group_ref, edges_ref)):
            hat = jnp.where(mask, fine_product(thirds_of(basis_ref[k].T), grad), hat)
        hat_ref[...] = hat

    basis_full, hat_full = call(
        rotate_gradient,
        [(slots, width, width), (width, wide)],
        (group_arg, rank_arg, edge_table, strips_own, strips_chip, pair, grad_full),
        specs=[SMEM, SMEM, SMEM] + [None] * 4,
    )

    basis_half, basis_far = collect(came_two, 0)


    def directions(
        group_ref,
        edges_ref,
        came_ref,
        grad_ref,
        hat_ref,
        basis_ref,
        send_ref,
        moment_ref,
        second_ref,
    ):
        unpack_columns(came_ref, owned_rows, second_ref, shards, rows, share)
        second_ref[...] = 0.95 * second_ref[...] + 0.05 * hat_ref[...] * hat_ref[...]
        unpack_columns(came_ref, owned_rows + tile_rows, moment_ref, shards, rows, share)
        masks = slot_masks(group_ref, edges_ref)
        moment = thirds_of(0.9 * moment_ref[...] + 0.1 * grad_ref[...])
        hat = jnp.zeros((width, wide), F32)
        for k, mask in enumerate(masks):
            hat = jnp.where(mask, fine_product(thirds_of(basis_ref[k].T), moment), hat)
        step = parts_of(adam_direction(hat, second_ref[...]))
        turned = jnp.zeros((width, wide), F32)
        for k, mask in enumerate(masks):
            turned = jnp.where(mask, product(parts_of(basis_ref[k]), step), turned)
        moment_ref[...] = turned
        pack_columns(moment_ref, send_ref, 0, shards, rows, share)
        pack_columns(second_ref, send_ref, tile_rows, shards, rows, share)

    send_five = call(
        directions,
        (shards, 2 * tile_rows, LANES),
        (group_arg, edge_table, came_two, grad_full, hat_full, basis_full),
        specs=[SMEM, SMEM] + [None] * 4,
        scratch=[pltpu.VMEM((width, wide), F32)] * 2,
    )
    came_four, send_five = together((came_four, send_five))
    came_five = exchange(send_five)


    gram_out, gram_half, gram_far = collect(came_four, 1)

    def refresh(
        rank_ref,
        basis_half_ref,
        basis_far_ref,
        gram_half_ref,
        gram_far_ref,
        weight_ref,
        mine_ref,
        other_ref,
        weight_out_ref,
        basis_ref,
        gram_ref,
        sem,
    ):
        fetch = pltpu.make_async_copy(weight_ref, weight_out_ref, sem)
        fetch.start()
        rank = rank_ref[0]
        first = rank < 2
        for out, half_ref, far_ref in (
            (basis_ref, basis_half_ref, basis_far_ref),
            (gram_ref, gram_half_ref, gram_far_ref),
        ):
            for group in range(shards):
                half = load_block(half_ref, group, 0, rows, owned)
                far = load_block(far_ref, group, 0, rows, owned)
                both = [jnp.where(first, half, far), jnp.where(first, far, half)]
                out[group * rows : (group + 1) * rows, :] = jnp.concatenate(both, axis=1)
        power = product(parts_of(basis_ref[...].T), parts_of(gram_ref[...]))
        frame = power / jnp.sqrt(jnp.sum(power * power) + 1e-06)
        for _ in range(NS_STEPS):
            pieces = parts_of(frame)
            square = product(pieces, pieces, (1, 1))
            frame = 1.5 * frame - 0.5 * product(parts_of(square), pieces)
        strips = [frame[r * columns : (r + 1) * columns] for r in range(ranks)]
        low = jnp.where(first, strips[0], strips[2])
        odd = jnp.where(first, strips[1], strips[3])
        even_core = rank % 2 == 0
        mine_ref[...] = jnp.where(even_core, low, odd)
        other_ref[...] = jnp.where(even_core, odd, low)
        fetch.wait()

    weight_dense = in_hbm(weight.reshape(dense))
    frame_mine, frame_other, weight_near = call(
        refresh,
        [(columns, width), (columns, width), dense],
        (rank_arg, basis_half, basis_far, gram_half, gram_far, weight_dense),
        specs=[SMEM] + [None] * 4 + [HBM],
        scratch=[pltpu.VMEM((width, width), F32)] * 2 + [pltpu.SemaphoreType.DMA(())],
    )
    frame_came = over_core(frame_other)
    pair_out = jnp.where(
        my_rank % 2 == 0,
        jnp.stack([frame_mine, frame_came]),
        jnp.stack([frame_came, frame_mine]),
    )
    came_five, pair_out, gram_out, first_out = together((came_five, pair_out, gram_out, first_out))


    def line_from(came_ref, base, line_ref):
        for group in range(shards):
            block = load_block(came_ref, group, base, rows, share)
            offset = 0
            for _, at, length in groups[group]:
                line_ref[:, at : at + length] = block[:, offset : offset + length]
                offset += length

    def take_back(came_ref, weight_ref, weight_out_ref, second_out_ref, line_ref):
        line_from(came_ref, 0, line_ref)
        close_line(line_ref, weight_out_ref)
        old = weight_ref[...]
        weight_out_ref[...] = old - 0.01 * (weight_out_ref[...] + 0.1 * old)
        line_from(came_ref, tile_rows, line_ref)
        close_line(line_ref, second_out_ref)

    weight_out, second_out = call(
        take_back, [dense, dense], (came_five, weight_near), scratch=[line_scratch]
    )

    bias_first_new = 0.9 * bias_first + 0.1 * bias_gradient
    bias_second_new = 0.95 * bias_second + 0.05 * bias_gradient * bias_gradient
    bias_updated = bias_weight - 0.01 * adam_direction(bias_first_new, bias_second_new)
    flat = (rows, 1, line)
    return (
        weight_out.reshape(flat),
        first_out.reshape(flat),
        second_out.reshape(flat),
        pair_out.transpose(0, 2, 1)[None],
        gram_out.transpose(0, 2, 1)[None],
        bias_updated,
        bias_first_new,
        bias_second_new,
    )


def solution(mesh):
    tiles = P("shard", "tensor", None)
    bias = P(("shard", "tensor"))
    owned = P("shard", None, None, "tensor")
    in_specs = (tiles,) * 6 + (P(),) + (bias,) * 4
    out_specs = (tiles,) * 3 + (owned,) * 2 + (bias,) * 3
    return jax.shard_map(body, mesh=mesh, in_specs=in_specs, out_specs=out_specs, check_vma=False)
```

```python
import functools

import jax
import jax.numpy as jnp
import numpy as np
from jax import lax
from jax.experimental import pallas as pl
from jax.experimental.pallas import tpu as pltpu
from jax.sharding import PartitionSpec as P

MCAP = 2
STEP = 10
NS_STEPS = 5
TYPE_TILES = (3, 1, 4, 4, 6)
LANES = 128
F32 = jnp.float32
BF16 = jnp.bfloat16
CORR_ONE = 1.0 - 0.9**STEP
CORR_TWO = 1.0 - 0.95**STEP


def adam_direction(moment_hat, second_new):
    return moment_hat / CORR_ONE / (jnp.sqrt(second_new / CORR_TWO) + 1e-08)


def place_columns(layer_total, shards, columns):
    sizes = [tiles * columns for tiles in TYPE_TILES] * layer_total
    starts = np.concatenate([[0], np.cumsum(sizes)]).tolist()
    share = starts[-1] // shards
    assert share * shards == starts[-1]
    small = [i for i, size in enumerate(sizes) if size <= share]
    groups = [[] for _ in range(shards)]
    room = [share] * shards
    if len(small) <= shards:
        for group, i in enumerate(small):
            groups[group].append((i, starts[i], sizes[i]))
            room[group] -= sizes[i]
        rest = [i for i in range(len(sizes)) if i not in small]
    else:
        rest = list(range(len(sizes)))
    group = 0
    for i in rest:
        at, left = starts[i], sizes[i]
        while left:
            while not room[group]:
                group += 1
            take = min(left, room[group])
            groups[group].append((i, at, take))
            room[group] -= take
            at += take
            left -= take
    return groups, share


def block_form(rows, width):
    full, rest = divmod(width, LANES)
    padded = -(-rows // 8) * 8
    halved = 0 < rest <= LANES // 2 and rows % 16 == 0
    total = full * padded + (0 if not rest else rows // 2 if halved else padded)
    return full, rest, padded, halved, total


def store_block(ref, index, base, value, rows, width):
    full, rest, padded, halved, _ = block_form(rows, width)
    for j in range(full):
        at = base + j * padded
        ref[index, at : at + rows, :] = value[:, j * LANES : (j + 1) * LANES]
    if rest:
        at = base + full * padded
        tail = value[:, full * LANES : width]
        if halved:
            half = rows // 2
            ref[index, at : at + half, 0:rest] = tail[:half]
            ref[index, at : at + half, LANES // 2 : LANES // 2 + rest] = tail[half:]
        else:
            ref[index, at : at + rows, 0:rest] = tail


def load_pieces(ref, index, base, rows, width):
    full, rest, padded, halved, _ = block_form(rows, width)
    pieces = []
    for j in range(full):
        at = base + j * padded
        pieces.append(ref[index, at : at + rows, :])
    if rest:
        at = base + full * padded
        if halved:
            half = rows // 2
            block = ref[index, at : at + half, :]
            pieces.append(
                jnp.concatenate(
                    [block[:, 0:rest], block[:, LANES // 2 : LANES // 2 + rest]], axis=0
                )
            )
        else:
            pieces.append(ref[index, at : at + rows, 0:rest])
    return pieces


def load_block(ref, index, base, rows, width):
    pieces = load_pieces(ref, index, base, rows, width)
    return pieces[0] if len(pieces) == 1 else jnp.concatenate(pieces, axis=1)


def unpack_columns(ref, base, out_ref, shards, rows, width):
    if width % LANES:
        tail = width // LANES * LANES
        out_ref[:, tail:] = jnp.zeros((out_ref.shape[0], LANES), F32)
    for source in range(shards):
        for j, piece in enumerate(load_pieces(ref, source, base, rows, width)):
            lanes = piece.shape[1]
            out_ref[source * rows : (source + 1) * rows, j * LANES : j * LANES + lanes] = piece


def pack_columns(value_ref, ref, base, shards, rows, width):
    for dest in range(shards):
        block = value_ref[dest * rows : (dest + 1) * rows, 0:width]
        store_block(ref, dest, base, block, rows, width)


def parts_of(value):
    high = value.astype(BF16)
    return high, (value - high.astype(F32)).astype(BF16)


def product(left, right, contract=(1, 0)):
    dims = (((contract[0],), (contract[1],)), ((), ()))
    dot = functools.partial(lax.dot_general, dimension_numbers=dims, preferred_element_type=F32)
    return dot(left[0], right[0]) + (dot(left[0], right[1]) + dot(left[1], right[0]))


def thirds_of(value):
    high = value.astype(BF16)
    rest = value - high.astype(F32)
    middle = rest.astype(BF16)
    return high, middle, (rest - middle.astype(F32)).astype(BF16)


def fine_product(left, right):
    dims = (((1,), (0,)), ((), ()))
    dot = functools.partial(lax.dot_general, dimension_numbers=dims, preferred_element_type=F32)
    small = dot(left[0], right[2]) + dot(left[1], right[1]) + dot(left[2], right[0])
    return dot(left[0], right[0]) + (dot(left[0], right[1]) + dot(left[1], right[0]) + small)


def call(kernel, outs, args, specs=None, out_specs=None, scratch=(), aliases=None, grid=()):
    single = isinstance(outs, tuple)
    shapes = [outs] if single else list(outs)
    shapes = [s if isinstance(s, jax.ShapeDtypeStruct) else jax.ShapeDtypeStruct(s, F32) for s in shapes]
    vmem = pl.BlockSpec(memory_space=pltpu.VMEM)
    specs = specs or [None] * len(args)
    result = pl.pallas_call(
        kernel,
        out_shape=shapes,
        grid=grid,
        in_specs=[s or vmem for s in specs],
        out_specs=out_specs or [vmem] * len(shapes),
        scratch_shapes=list(scratch),
        input_output_aliases=aliases or {},
        compiler_params=pltpu.CompilerParams(vmem_limit_bytes=16 * 2**20),
    )(*args)
    return result[0] if single else result


SMEM = pl.BlockSpec(memory_space=pltpu.SMEM)
ANY = pl.BlockSpec(memory_space=pl.ANY)
HBM = pl.BlockSpec(memory_space=pltpu.HBM)


def body(
    gradient,
    weight,
    first_moment,
    second_moment,
    left_basis,
    left_gram,
    owner_table,
    bias_gradient,
    bias_weight,
    bias_first,
    bias_second,
):
    shards = lax.axis_size("shard")
    ranks = lax.axis_size("tensor")
    assert ranks == 4 and MCAP == 2
    layer_total = owner_table.shape[0]
    matrix_total = 5 * layer_total
    rows = gradient.shape[0]
    line = gradient.shape[2]
    columns = line // (sum(TYPE_TILES) * layer_total)
    width = rows * shards
    assert columns * ranks == width and columns <= LANES
    groups, share = place_columns(layer_total, shards, columns)
    slots = max(len(group) for group in groups)
    wide = -(-share // LANES) * LANES
    strip = slots * columns
    owned = MCAP * columns
    tile_rows = block_form(rows, share)[4]
    strip_rows = block_form(rows, strip)[4]
    owned_rows = block_form(rows, owned)[4]
    slot_matrix = [[piece[0] for piece in group] for group in groups]
    edges = np.full((shards, slots + 1), share, np.int32)
    for group, pieces in enumerate(groups):
        edges[group, 0] = 0
        edges[group, 1 : len(pieces) + 1] = np.cumsum([piece[2] for piece in pieces])

    my_group = lax.axis_index("shard")
    my_rank = lax.axis_index("tensor").astype(jnp.int32)
    edge_table = jnp.asarray(edges.reshape(-1))
    group_arg = my_group.astype(jnp.int32).reshape(1)
    rank_arg = my_rank.reshape(1)
    owners = owner_table.reshape(-1)
    core_pairs = [(r, r ^ 1) for r in range(ranks)]
    chip_pairs = [(r, r ^ 2) for r in range(ranks)]

    def over_core(value):
        return lax.ppermute(value, "tensor", core_pairs)

    def over_chip(value):
        return lax.ppermute(value, "tensor", chip_pairs)

    def exchange(value):
        return lax.all_to_all(value, "shard", split_axis=0, concat_axis=0, tiled=True)

    together = lax.optimization_barrier

    def in_hbm(value):
        return pltpu.with_memory_space_constraint(value, pltpu.HBM)


    line_tiles = line // LANES
    assert line_tiles * LANES == line
    dense = (rows * line_tiles, LANES)
    line_scratch = pltpu.VMEM((rows, line), F32)

    def open_line(ref, line_ref):
        for j in range(line_tiles):
            line_ref[:, j * LANES : (j + 1) * LANES] = ref[pl.ds(j, rows, stride=line_tiles), :]

    def close_line(line_ref, ref):
        for j in range(line_tiles):
            ref[pl.ds(j, rows, stride=line_tiles), :] = line_ref[:, j * LANES : (j + 1) * LANES]

    def gather_line(ref, group):
        pieces = [ref[:, at : at + length] for _, at, length in groups[group]]
        return pieces[0] if len(pieces) == 1 else jnp.concatenate(pieces, axis=1)

    def send_tiles(ref, line_ref, out_ref, base):
        open_line(ref, line_ref)
        for group in range(shards):
            store_block(out_ref, group, base, gather_line(line_ref, group), rows, share)

    def fill_owned_table(owner_ref, table_ref, count_ref):
        for group in range(shards):
            count_ref[group] = 0
            for m in range(MCAP):
                table_ref[group * MCAP + m] = -1

        def take(i, carry):
            owner = owner_ref[i]
            rank = count_ref[owner]
            table_ref[owner * MCAP + rank] = i
            count_ref[owner] = rank + 1
            return carry

        lax.fori_loop(0, matrix_total, take, 0)

    def send_owned(stage_ref, table_ref, out_ref, base):
        for group in range(shards):
            held = []
            for m in range(MCAP):
                matrix = table_ref[group * MCAP + m]
                block = stage_ref[jnp.maximum(matrix, 0)]
                held.append(jnp.where(matrix >= 0, block, 0.0))
            store_block(out_ref, group, base, jnp.concatenate(held, axis=1), rows, owned)

    count_scratch = pltpu.SMEM((shards,), jnp.int32)
    stage_scratch = pltpu.VMEM((matrix_total, rows, columns), F32)

    def slot_masks(group_ref, edges_ref):
        lane = lax.broadcasted_iota(jnp.int32, (1, wide), 1)
        at = group_ref[0] * (slots + 1)
        return [(lane >= edges_ref[at + k]) & (lane < edges_ref[at + k + 1]) for k in range(slots)]


    def pack_gradient(grad_ref, basis_ref, out_ref, line_ref, dense_ref, near_ref, sems):
        step = pl.program_id(0)

        @pl.when(step == 0)
        def _():
            fetch_basis = pltpu.make_async_copy(basis_ref, near_ref, sems.at[0])
            fetch_basis.start()
            fetch = pltpu.make_async_copy(grad_ref, dense_ref, sems.at[1])
            fetch.start()
            fetch_basis.wait()
            fetch.wait()
            open_line(dense_ref, line_ref)

        for part in range(2):

            @pl.when(step == part)
            def _():
                basis = near_ref[:, 0, :]
                for place in range(shards // 2):
                    group = part * (shards // 2) + place
                    held = [
                        basis[:, matrix * columns : (matrix + 1) * columns]
                        for matrix in slot_matrix[group]
                    ]
                    held += [jnp.zeros((rows, columns), F32)] * (slots - len(held))
                    store_block(out_ref, place, 0, jnp.concatenate(held, axis=1), rows, strip)
                    block = gather_line(line_ref, group)
                    store_block(out_ref, place, strip_rows, block, rows, share)

    grad_dense = gradient.reshape(dense)
    send_one = call(
        pack_gradient,
        (shards, strip_rows + tile_rows, LANES),
        (in_hbm(grad_dense), in_hbm(left_basis)),
        specs=[HBM, HBM],
        out_specs=[pl.BlockSpec((shards // 2, strip_rows + tile_rows, LANES), lambda i: (i, 0, 0))],
        grid=(2,),
        scratch=[
            line_scratch,
            pltpu.VMEM(dense, F32),
            pltpu.VMEM(left_basis.shape, F32),
            pltpu.SemaphoreType.DMA((2,)),
        ],
    )
    came_one = exchange(send_one)


    half_groups = shards // 2
    half_total = matrix_total // 2
    assert half_groups * 2 == shards and shards & (shards - 1) == 0
    assert all(
        (matrix >= half_total) == (group >= half_groups)
        for group in range(shards)
        for matrix in slot_matrix[group]
    )
    slot_table = np.full((shards, slots), -1, np.int32)
    for group in range(shards):
        slot_table[group, : len(slot_matrix[group])] = slot_matrix[group]
    slot_table = jnp.asarray(slot_table.reshape(-1))


    def pack_moments(
        owner_ref,
        second_ref,
        first_ref,
        grad_ref,
        basis_ref,
        out_ref,
        new_ref,
        table_ref,
        count_ref,
        stage_ref,
        line_ref,
    ):
        fill_owned_table(owner_ref, table_ref, count_ref)
        basis = basis_ref[:, 0, :]
        for matrix in range(matrix_total):
            stage_ref[matrix] = basis[:, matrix * columns : (matrix + 1) * columns]
        send_owned(stage_ref, table_ref, out_ref, 0)
        send_tiles(second_ref, line_ref, out_ref, owned_rows)
        send_tiles(first_ref, line_ref, out_ref, owned_rows + tile_rows)
        new_ref[...] = 0.9 * first_ref[...] + 0.1 * grad_ref[...]

    vmem = pl.BlockSpec(memory_space=pltpu.VMEM)
    send_two, first_out, owned_table = call(
        pack_moments,
        [
            (shards, owned_rows + 2 * tile_rows, LANES),
            dense,
            jax.ShapeDtypeStruct((shards * MCAP,), jnp.int32),
        ],
        (
            owners,
            second_moment.reshape(dense),
            first_moment.reshape(dense),
            grad_dense,
            left_basis,
        ),
        specs=[SMEM, None, None, None, None],
        out_specs=[vmem, vmem, SMEM],
        scratch=[count_scratch, stage_scratch, line_scratch],
    )
    came_one, send_two = together((came_one, send_two))
    came_two = exchange(send_two)


    def gram_partials(
        group_ref, rank_ref, edges_ref, came_ref, grad_ref, strips_ref, kept_ref, core_ref, turned_ref
    ):
        unpack_columns(came_ref, strip_rows, grad_ref, shards, rows, share)
        for source in range(shards):
            strips_ref[source] = came_ref[source, 0:strip_rows, :]
        turned_ref[...] = jnp.zeros_like(turned_ref)
        for rank in range(ranks):
            turned_ref[rank * LANES : rank * LANES + columns, :] = grad_ref[
                rank * columns : (rank + 1) * columns, :
            ]
        right = parts_of(turned_ref[...])
        grams = []
        for mask in slot_masks(group_ref, edges_ref):
            left = parts_of(jnp.where(mask, grad_ref[...], 0.0))
            grams.append(product(left, right, (1, 1)))
        odd = rank_ref[0] % 2 == 1
        for chip in range(2):
            for group in range(shards):
                at = slice(group * rows, (group + 1) * rows)
                low = [g[at, 2 * chip * LANES : 2 * chip * LANES + columns] for g in grams]
                high = [g[at, (2 * chip + 1) * LANES : (2 * chip + 1) * LANES + columns] for g in grams]
                low, high = jnp.concatenate(low, axis=1), jnp.concatenate(high, axis=1)
                mine, other = jnp.where(odd, high, low), jnp.where(odd, low, high)
                store_block(kept_ref.at[chip], group, 0, mine, rows, strip)
                store_block(core_ref.at[chip], group, 0, other, rows, strip)

    strip_shape = (shards, strip_rows, LANES)
    grad_full, strips_own, kept, for_core = call(
        gram_partials,
        [(width, wide), strip_shape, (2,) + strip_shape, (2,) + strip_shape],
        (group_arg, rank_arg, edge_table, came_one),
        specs=[SMEM, SMEM, SMEM, None],
        scratch=[pltpu.VMEM((ranks * LANES, wide), F32)],
    )


    def add_core(rank_ref, kept_ref, came_ref, mine_ref, far_ref):
        chip = rank_ref[0] // 2
        mine_ref[...] = kept_ref[chip] + came_ref[chip]
        far_ref[...] = kept_ref[1 - chip] + came_ref[1 - chip]

    gram_mine, for_chip = call(
        add_core,
        [strip_shape, strip_shape],
        (rank_arg, kept, over_core(for_core)),
        specs=[SMEM, None, None],
    )
    came_chip = over_chip(for_chip)


    def sum_strips(group_ref, mine_ref, came_ref, *out_refs):
        place = group_ref[0] % half_groups
        for k, out_ref in enumerate(out_refs):
            for j in range(2):
                at = (place ^ k) + j * half_groups
                out_ref[j] = mine_ref[at] + came_ref[at]

    gram_blocks = call(
        sum_strips,
        [(2, strip_rows, LANES)] * half_groups,
        (group_arg, gram_mine, came_chip),
        specs=[SMEM, None, None],
    )
    *gram_blocks, strips_own = together((*gram_blocks, strips_own))
    gram_blocks = [gram_blocks[0]] + [
        lax.ppermute(gram_blocks[k], "shard", [(s, s ^ k) for s in range(shards)])
        for k in range(1, half_groups)
    ]


    strips_chip = over_chip(strips_own)
    *late, strips_chip = together((*gram_blocks[half_groups // 2 :], strips_chip))
    gram_blocks = gram_blocks[: half_groups // 2] + late


    def split_owned(rank_ref, came_ref, *refs):
        spread = len(refs) == 4
        mine_ref, other_ref = refs[-3:-1] if spread else refs
        odd = rank_ref[0] % 2 == 1
        for block_at in range(shards):
            at = slice(block_at * rows, (block_at + 1) * rows)
            if spread:
                place, base = block_at % half_groups, block_at // half_groups * owned_rows
                block = load_block(came_ref, place, base, rows, owned) + load_block(
                    came_ref, half_groups + place, base, rows, owned
                )
            else:
                block = load_block(came_ref, block_at, 0, rows, owned)
            strips = [block[:, m * columns : (m + 1) * columns] for m in range(MCAP)]
            mine_ref[at, 0:columns] = jnp.where(odd, strips[1], strips[0])
            other_ref[at, 0:columns] = jnp.where(odd, strips[0], strips[1])
            if spread:
                for m in range(MCAP):
                    refs[-1][m, at, 0:columns] = strips[m]
        if spread:
            for m in range(MCAP):
                refs[0][m] = refs[-1][m].T[0:columns]

    def join_half(rank_ref, mine_ref, other_ref, half_ref):
        odd = rank_ref[0] % 2 == 1
        for group in range(shards):
            at = slice(group * rows, (group + 1) * rows)
            mine, other = mine_ref[at, 0:columns], other_ref[at, 0:columns]
            both = [jnp.where(odd, other, mine), jnp.where(odd, mine, other)]
            store_block(half_ref, group, 0, jnp.concatenate(both, axis=1), rows, owned)

    def collect(came, spread):
        *strips, mine, other = call(
            split_owned,
            [(MCAP, columns, width)] * spread + [(width, LANES), (width, LANES)],
            (rank_arg, came),
            specs=[SMEM, None],
            scratch=[pltpu.VMEM((MCAP, width, LANES), F32)] * spread,
        )
        half = call(
            join_half,
            (shards, owned_rows, LANES),
            (rank_arg, mine, over_core(other)),
            specs=[SMEM, None, None],
        )
        return *strips, half, over_chip(half)


    def add_blocks(group_ref, slot_ref, came, first, stage_ref):
        for k, came_ref in enumerate(came):
            for j in range(2):
                block = load_block(came_ref, j, 0, rows, strip)
                for m in range(slots):
                    matrix = slot_ref[(group_ref[0] ^ (first + k)) * slots + m]
                    at = jnp.where(matrix >= 0, matrix, matrix_total)
                    part = block[:, m * columns : (m + 1) * columns]
                    stage_ref[j, at] = stage_ref[j, at] + 0.05 * part

    def early_grams(group_ref, slot_ref, gram_ref, *refs):
        came, stage_ref = refs[:-1], refs[-1]
        half = group_ref[0] // half_groups
        stage_ref[...] = jnp.zeros_like(stage_ref)
        old = 0.95 * gram_ref[:, 0, :]
        for matrix in range(matrix_total):
            stage_ref[half, matrix] = old[:, matrix * columns : (matrix + 1) * columns]
        add_blocks(group_ref, slot_ref, came, 0, stage_ref)

    early_blocks = half_groups // 2
    stage_shape = (2, matrix_total + 1, rows, columns)
    early_stage = call(
        early_grams,
        stage_shape,
        (group_arg, slot_table, left_gram, *gram_blocks[:early_blocks]),
        specs=[SMEM, SMEM] + [None] * (1 + early_blocks),
    )

    def new_grams(group_ref, table_ref, slot_ref, *refs):
        early_ref, *came, out_ref, stage_ref = refs
        stage_ref[...] = early_ref[...]
        add_blocks(group_ref, slot_ref, came, early_blocks, stage_ref)
        for dest in range(shards):
            for j in range(2):
                held = []
                for m in range(MCAP):
                    matrix = table_ref[dest * MCAP + m]
                    block = stage_ref[j, jnp.maximum(matrix, 0)]
                    held.append(jnp.where(matrix >= 0, block, 0.0))
                block = jnp.concatenate(held, axis=1)
                store_block(out_ref, dest, j * owned_rows, block, rows, owned)

    send_four = call(
        new_grams,
        (shards, 2 * owned_rows, LANES),
        (group_arg, owned_table, slot_table, early_stage, *gram_blocks[early_blocks:]),
        specs=[SMEM, SMEM, SMEM] + [None] * (1 + half_groups - early_blocks),
        scratch=[pltpu.VMEM(stage_shape, F32)],
    )
    send_four = in_hbm(send_four)
    came_two, send_four = together((came_two, send_four))
    came_four = in_hbm(exchange(send_four))
    pair = over_core(jnp.stack([strips_own, strips_chip]))


    def rotate_gradient(
        group_ref,
        rank_ref,
        edges_ref,
        own_ref,
        chip_ref,
        pair_ref,
        grad_ref,
        basis_ref,
        hat_ref,
    ):
        rank = rank_ref[0]
        for group in range(shards):
            blocks = [
                load_block(ref, group, 0, rows, strip)
                for ref in (own_ref, pair_ref.at[0], chip_ref, pair_ref.at[1])
            ]
            at = slice(group * rows, (group + 1) * rows)
            for k in range(slots):
                cut = [block[:, k * columns : (k + 1) * columns] for block in blocks]
                low = [jnp.where(rank % 2 == 0, cut[0 + h], cut[1 + h]) for h in (0, 2)]
                odd = [jnp.where(rank % 2 == 0, cut[1 + h], cut[0 + h]) for h in (0, 2)]
                first = rank < 2
                ordered = [
                    jnp.where(first, low[0], low[1]),
                    jnp.where(first, odd[0], odd[1]),
                    jnp.where(first, low[1], low[0]),
                    jnp.where(first, odd[1], odd[0]),
                ]
                basis_ref[k, at, :] = jnp.concatenate(ordered, axis=1)
        grad = thirds_of(grad_ref[...])
        hat = jnp.zeros((width, wide), F32)
        for k, mask in enumerate(slot_masks(group_ref, edges_ref)):
            hat = jnp.where(mask, fine_product(thirds_of(basis_ref[k].T), grad), hat)
        hat_ref[...] = hat

    basis_full, hat_full = call(
        rotate_gradient,
        [(slots, width, width), (width, wide)],
        (group_arg, rank_arg, edge_table, strips_own, strips_chip, pair, grad_full),
        specs=[SMEM, SMEM, SMEM] + [None] * 4,
    )

    basis_half, basis_far = collect(came_two, 0)


    def directions(
        group_ref,
        edges_ref,
        came_ref,
        grad_ref,
        hat_ref,
        basis_ref,
        send_ref,
        moment_ref,
        second_ref,
    ):
        unpack_columns(came_ref, owned_rows, second_ref, shards, rows, share)
        second_ref[...] = 0.95 * second_ref[...] + 0.05 * hat_ref[...] * hat_ref[...]
        unpack_columns(came_ref, owned_rows + tile_rows, moment_ref, shards, rows, share)
        masks = slot_masks(group_ref, edges_ref)
        moment = thirds_of(0.9 * moment_ref[...] + 0.1 * grad_ref[...])
        hat = jnp.zeros((width, wide), F32)
        for k, mask in enumerate(masks):
            hat = jnp.where(mask, fine_product(thirds_of(basis_ref[k].T), moment), hat)
        step = parts_of(adam_direction(hat, second_ref[...]))
        turned = jnp.zeros((width, wide), F32)
        for k, mask in enumerate(masks):
            turned = jnp.where(mask, product(parts_of(basis_ref[k]), step), turned)
        moment_ref[...] = turned
        pack_columns(moment_ref, send_ref, 0, shards, rows, share)
        pack_columns(second_ref, send_ref, tile_rows, shards, rows, share)

    send_five = call(
        directions,
        (shards, 2 * tile_rows, LANES),
        (group_arg, edge_table, came_two, grad_full, hat_full, basis_full),
        specs=[SMEM, SMEM] + [None] * 4,
        scratch=[pltpu.VMEM((width, wide), F32)] * 2,
    )
    came_four, send_five = together((came_four, send_five))
    came_five = exchange(send_five)


    gram_out, gram_half, gram_far = collect(came_four, 1)

    def refresh(
        rank_ref,
        basis_half_ref,
        basis_far_ref,
        gram_half_ref,
        gram_far_ref,
        weight_ref,
        mine_ref,
        other_ref,
        weight_out_ref,
        basis_ref,
        gram_ref,
        sem,
    ):
        fetch = pltpu.make_async_copy(weight_ref, weight_out_ref, sem)
        fetch.start()
        rank = rank_ref[0]
        first = rank < 2
        for out, half_ref, far_ref in (
            (basis_ref, basis_half_ref, basis_far_ref),
            (gram_ref, gram_half_ref, gram_far_ref),
        ):
            for group in range(shards):
                half = load_block(half_ref, group, 0, rows, owned)
                far = load_block(far_ref, group, 0, rows, owned)
                both = [jnp.where(first, half, far), jnp.where(first, far, half)]
                out[group * rows : (group + 1) * rows, :] = jnp.concatenate(both, axis=1)
        power = product(parts_of(basis_ref[...].T), parts_of(gram_ref[...]))
        frame = power / jnp.sqrt(jnp.sum(power * power) + 1e-06)
        for _ in range(NS_STEPS):
            pieces = parts_of(frame)
            square = product(pieces, pieces, (1, 1))
            frame = 1.5 * frame - 0.5 * product(parts_of(square), pieces)
        strips = [frame[r * columns : (r + 1) * columns] for r in range(ranks)]
        low = jnp.where(first, strips[0], strips[2])
        odd = jnp.where(first, strips[1], strips[3])
        even_core = rank % 2 == 0
        mine_ref[...] = jnp.where(even_core, low, odd)
        other_ref[...] = jnp.where(even_core, odd, low)
        fetch.wait()

    weight_dense = in_hbm(weight.reshape(dense))
    frame_mine, frame_other, weight_near = call(
        refresh,
        [(columns, width), (columns, width), dense],
        (rank_arg, basis_half, basis_far, gram_half, gram_far, weight_dense),
        specs=[SMEM] + [None] * 4 + [HBM],
        scratch=[pltpu.VMEM((width, width), F32)] * 2 + [pltpu.SemaphoreType.DMA(())],
    )
    frame_came = over_core(frame_other)
    pair_out = jnp.where(
        my_rank % 2 == 0,
        jnp.stack([frame_mine, frame_came]),
        jnp.stack([frame_came, frame_mine]),
    )
    came_five, pair_out, gram_out, first_out = together((came_five, pair_out, gram_out, first_out))


    steps = 2 if rows % 16 == 0 else 1
    step_rows = rows // steps
    step_dense = (step_rows * line_tiles, LANES)

    def line_from(came_ref, base, part, line_ref, ref):
        for group in range(shards):
            block = load_block(came_ref, group, base, rows, share)
            block = block[part * step_rows : (part + 1) * step_rows]
            offset = 0
            for _, at, length in groups[group]:
                line_ref[:, at : at + length] = block[:, offset : offset + length]
                offset += length
        for j in range(line_tiles):
            ref[pl.ds(j, step_rows, stride=line_tiles), :] = line_ref[:, j * LANES : (j + 1) * LANES]

    def take_back(came_ref, weight_ref, weight_out_ref, second_out_ref, line_ref):
        for part in range(steps):

            @pl.when(pl.program_id(0) == part)
            def _():
                line_from(came_ref, 0, part, line_ref, weight_out_ref)
                old = weight_ref[...]
                weight_out_ref[...] = old - 0.01 * (weight_out_ref[...] + 0.1 * old)
                line_from(came_ref, tile_rows, part, line_ref, second_out_ref)

    part_spec = pl.BlockSpec(step_dense, lambda i: (i, 0))
    weight_out, second_out = call(
        take_back,
        [dense, dense],
        (came_five, weight_near),
        specs=[None, part_spec],
        out_specs=[part_spec, part_spec],
        grid=(steps,),
        scratch=[pltpu.VMEM((step_rows, line), F32)],
    )

    bias_first_new = 0.9 * bias_first + 0.1 * bias_gradient
    bias_second_new = 0.95 * bias_second + 0.05 * bias_gradient * bias_gradient
    bias_updated = bias_weight - 0.01 * adam_direction(bias_first_new, bias_second_new)
    flat = (rows, 1, line)
    return (
        weight_out.reshape(flat),
        first_out.reshape(flat),
        second_out.reshape(flat),
        pair_out.transpose(0, 2, 1)[None],
        gram_out.transpose(0, 2, 1)[None],
        bias_updated,
        bias_first_new,
        bias_second_new,
    )


def solution(mesh):
    tiles = P("shard", "tensor", None)
    bias = P(("shard", "tensor"))
    owned = P("shard", None, None, "tensor")
    in_specs = (tiles,) * 6 + (P(),) + (bias,) * 4
    out_specs = (tiles,) * 3 + (owned,) * 2 + (bias,) * 3
    return jax.shard_map(body, mesh=mesh, in_specs=in_specs, out_specs=out_specs, check_vma=False)
```

```python
import functools

import jax
import jax.numpy as jnp
import numpy as np
from jax import lax
from jax.experimental import pallas as pl
from jax.experimental.pallas import tpu as pltpu
from jax.sharding import PartitionSpec as P

MCAP = 2
STEP = 10
NS_STEPS = 5
TYPE_TILES = (3, 1, 4, 4, 6)
LANES = 128
F32 = jnp.float32
BF16 = jnp.bfloat16
CORR_ONE = 1.0 - 0.9**STEP
CORR_TWO = 1.0 - 0.95**STEP


def adam_direction(moment_hat, second_new):
    return moment_hat / CORR_ONE / (jnp.sqrt(second_new / CORR_TWO) + 1e-08)


def place_columns(layer_total, shards, columns):
    sizes = [tiles * columns for tiles in TYPE_TILES] * layer_total
    starts = np.concatenate([[0], np.cumsum(sizes)]).tolist()
    share = starts[-1] // shards
    assert share * shards == starts[-1]
    small = [i for i, size in enumerate(sizes) if size <= share]
    groups = [[] for _ in range(shards)]
    room = [share] * shards
    if len(small) <= shards:
        for group, i in enumerate(small):
            groups[group].append((i, starts[i], sizes[i]))
            room[group] -= sizes[i]
        rest = [i for i in range(len(sizes)) if i not in small]
    else:
        rest = list(range(len(sizes)))
    group = 0
    for i in rest:
        at, left = starts[i], sizes[i]
        while left:
            while not room[group]:
                group += 1
            take = min(left, room[group])
            groups[group].append((i, at, take))
            room[group] -= take
            at += take
            left -= take
    return groups, share


def block_form(rows, width):
    full, rest = divmod(width, LANES)
    padded = -(-rows // 8) * 8
    halved = 0 < rest <= LANES // 2 and rows % 16 == 0
    total = full * padded + (0 if not rest else rows // 2 if halved else padded)
    return full, rest, padded, halved, total


def store_block(ref, index, base, value, rows, width):
    full, rest, padded, halved, _ = block_form(rows, width)
    for j in range(full):
        at = base + j * padded
        ref[index, at : at + rows, :] = value[:, j * LANES : (j + 1) * LANES]
    if rest:
        at = base + full * padded
        tail = value[:, full * LANES : width]
        if halved:
            half = rows // 2
            ref[index, at : at + half, 0:rest] = tail[:half]
            ref[index, at : at + half, LANES // 2 : LANES // 2 + rest] = tail[half:]
        else:
            ref[index, at : at + rows, 0:rest] = tail


def load_pieces(ref, index, base, rows, width):
    full, rest, padded, halved, _ = block_form(rows, width)
    pieces = []
    for j in range(full):
        at = base + j * padded
        pieces.append(ref[index, at : at + rows, :])
    if rest:
        at = base + full * padded
        if halved:
            half = rows // 2
            block = ref[index, at : at + half, :]
            pieces.append(
                jnp.concatenate(
                    [block[:, 0:rest], block[:, LANES // 2 : LANES // 2 + rest]], axis=0
                )
            )
        else:
            pieces.append(ref[index, at : at + rows, 0:rest])
    return pieces


def load_block(ref, index, base, rows, width):
    pieces = load_pieces(ref, index, base, rows, width)
    return pieces[0] if len(pieces) == 1 else jnp.concatenate(pieces, axis=1)


def unpack_columns(ref, base, out_ref, shards, rows, width):
    if width % LANES:
        tail = width // LANES * LANES
        out_ref[:, tail:] = jnp.zeros((out_ref.shape[0], LANES), F32)
    for source in range(shards):
        for j, piece in enumerate(load_pieces(ref, source, base, rows, width)):
            lanes = piece.shape[1]
            out_ref[source * rows : (source + 1) * rows, j * LANES : j * LANES + lanes] = piece


def pack_columns(value_ref, ref, base, shards, rows, width):
    for dest in range(shards):
        block = value_ref[dest * rows : (dest + 1) * rows, 0:width]
        store_block(ref, dest, base, block, rows, width)


def parts_of(value):
    high = value.astype(BF16)
    return high, (value - high.astype(F32)).astype(BF16)


def product(left, right, contract=(1, 0)):
    dims = (((contract[0],), (contract[1],)), ((), ()))
    dot = functools.partial(lax.dot_general, dimension_numbers=dims, preferred_element_type=F32)
    return dot(left[0], right[0]) + (dot(left[0], right[1]) + dot(left[1], right[0]))


def thirds_of(value):
    high = value.astype(BF16)
    rest = value - high.astype(F32)
    middle = rest.astype(BF16)
    return high, middle, (rest - middle.astype(F32)).astype(BF16)


def fine_product(left, right):
    dims = (((1,), (0,)), ((), ()))
    dot = functools.partial(lax.dot_general, dimension_numbers=dims, preferred_element_type=F32)
    small = dot(left[0], right[2]) + dot(left[1], right[1]) + dot(left[2], right[0])
    return dot(left[0], right[0]) + (dot(left[0], right[1]) + dot(left[1], right[0]) + small)


def call(kernel, outs, args, specs=None, out_specs=None, scratch=(), aliases=None, grid=()):
    single = isinstance(outs, tuple)
    shapes = [outs] if single else list(outs)
    shapes = [s if isinstance(s, jax.ShapeDtypeStruct) else jax.ShapeDtypeStruct(s, F32) for s in shapes]
    vmem = pl.BlockSpec(memory_space=pltpu.VMEM)
    specs = specs or [None] * len(args)
    result = pl.pallas_call(
        kernel,
        out_shape=shapes,
        grid=grid,
        in_specs=[s or vmem for s in specs],
        out_specs=out_specs or [vmem] * len(shapes),
        scratch_shapes=list(scratch),
        input_output_aliases=aliases or {},
        compiler_params=pltpu.CompilerParams(vmem_limit_bytes=16 * 2**20),
    )(*args)
    return result[0] if single else result


SMEM = pl.BlockSpec(memory_space=pltpu.SMEM)
ANY = pl.BlockSpec(memory_space=pl.ANY)
HBM = pl.BlockSpec(memory_space=pltpu.HBM)


def body(
    gradient,
    weight,
    first_moment,
    second_moment,
    left_basis,
    left_gram,
    owner_table,
    bias_gradient,
    bias_weight,
    bias_first,
    bias_second,
):
    shards = lax.axis_size("shard")
    ranks = lax.axis_size("tensor")
    assert ranks == 4 and MCAP == 2
    layer_total = owner_table.shape[0]
    matrix_total = 5 * layer_total
    rows = gradient.shape[0]
    line = gradient.shape[2]
    columns = line // (sum(TYPE_TILES) * layer_total)
    width = rows * shards
    assert columns * ranks == width and columns <= LANES
    groups, share = place_columns(layer_total, shards, columns)
    slots = max(len(group) for group in groups)
    wide = -(-share // LANES) * LANES
    strip = slots * columns
    owned = MCAP * columns
    tile_rows = block_form(rows, share)[4]
    strip_rows = block_form(rows, strip)[4]
    owned_rows = block_form(rows, owned)[4]
    slot_matrix = [[piece[0] for piece in group] for group in groups]
    edges = np.full((shards, slots + 1), share, np.int32)
    for group, pieces in enumerate(groups):
        edges[group, 0] = 0
        edges[group, 1 : len(pieces) + 1] = np.cumsum([piece[2] for piece in pieces])

    my_group = lax.axis_index("shard")
    my_rank = lax.axis_index("tensor").astype(jnp.int32)
    edge_table = jnp.asarray(edges.reshape(-1))
    group_arg = my_group.astype(jnp.int32).reshape(1)
    rank_arg = my_rank.reshape(1)
    owners = owner_table.reshape(-1)
    core_pairs = [(r, r ^ 1) for r in range(ranks)]
    chip_pairs = [(r, r ^ 2) for r in range(ranks)]

    def over_core(value):
        return lax.ppermute(value, "tensor", core_pairs)

    def over_chip(value):
        return lax.ppermute(value, "tensor", chip_pairs)

    def exchange(value):
        return lax.all_to_all(value, "shard", split_axis=0, concat_axis=0, tiled=True)

    together = lax.optimization_barrier

    def in_hbm(value):
        return pltpu.with_memory_space_constraint(value, pltpu.HBM)


    line_tiles = line // LANES
    assert line_tiles * LANES == line
    dense = (rows * line_tiles, LANES)
    line_scratch = pltpu.VMEM((rows, line), F32)

    def open_line(ref, line_ref):
        for j in range(line_tiles):
            line_ref[:, j * LANES : (j + 1) * LANES] = ref[pl.ds(j, rows, stride=line_tiles), :]

    def close_line(line_ref, ref):
        for j in range(line_tiles):
            ref[pl.ds(j, rows, stride=line_tiles), :] = line_ref[:, j * LANES : (j + 1) * LANES]

    def gather_line(ref, group):
        pieces = [ref[:, at : at + length] for _, at, length in groups[group]]
        return pieces[0] if len(pieces) == 1 else jnp.concatenate(pieces, axis=1)

    def send_tiles(ref, line_ref, out_ref, base):
        open_line(ref, line_ref)
        for group in range(shards):
            store_block(out_ref, group, base, gather_line(line_ref, group), rows, share)

    def fill_owned_table(owner_ref, table_ref, count_ref):
        for group in range(shards):
            count_ref[group] = 0
            for m in range(MCAP):
                table_ref[group * MCAP + m] = -1

        def take(i, carry):
            owner = owner_ref[i]
            rank = count_ref[owner]
            table_ref[owner * MCAP + rank] = i
            count_ref[owner] = rank + 1
            return carry

        lax.fori_loop(0, matrix_total, take, 0)

    def send_owned(stage_ref, table_ref, out_ref, base):
        for group in range(shards):
            held = []
            for m in range(MCAP):
                matrix = table_ref[group * MCAP + m]
                block = stage_ref[jnp.maximum(matrix, 0)]
                held.append(jnp.where(matrix >= 0, block, 0.0))
            store_block(out_ref, group, base, jnp.concatenate(held, axis=1), rows, owned)

    count_scratch = pltpu.SMEM((shards,), jnp.int32)
    stage_scratch = pltpu.VMEM((matrix_total, rows, columns), F32)

    def slot_masks(group_ref, edges_ref):
        lane = lax.broadcasted_iota(jnp.int32, (1, wide), 1)
        at = group_ref[0] * (slots + 1)
        return [(lane >= edges_ref[at + k]) & (lane < edges_ref[at + k + 1]) for k in range(slots)]


    def pack_gradient(grad_ref, basis_ref, out_ref, line_ref, dense_ref, near_ref, sems):
        step = pl.program_id(0)

        @pl.when(step == 0)
        def _():
            fetch_basis = pltpu.make_async_copy(basis_ref, near_ref, sems.at[0])
            fetch_basis.start()
            fetch = pltpu.make_async_copy(grad_ref, dense_ref, sems.at[1])
            fetch.start()
            fetch_basis.wait()
            fetch.wait()
            open_line(dense_ref, line_ref)

        for part in range(2):

            @pl.when(step == part)
            def _():
                basis = near_ref[:, 0, :]
                for place in range(shards // 2):
                    group = part * (shards // 2) + place
                    held = [
                        basis[:, matrix * columns : (matrix + 1) * columns]
                        for matrix in slot_matrix[group]
                    ]
                    held += [jnp.zeros((rows, columns), F32)] * (slots - len(held))
                    store_block(out_ref, place, 0, jnp.concatenate(held, axis=1), rows, strip)
                    block = gather_line(line_ref, group)
                    store_block(out_ref, place, strip_rows, block, rows, share)

    grad_dense = gradient.reshape(dense)
    send_one = call(
        pack_gradient,
        (shards, strip_rows + tile_rows, LANES),
        (in_hbm(grad_dense), in_hbm(left_basis)),
        specs=[HBM, HBM],
        out_specs=[pl.BlockSpec((shards // 2, strip_rows + tile_rows, LANES), lambda i: (i, 0, 0))],
        grid=(2,),
        scratch=[
            line_scratch,
            pltpu.VMEM(dense, F32),
            pltpu.VMEM(left_basis.shape, F32),
            pltpu.SemaphoreType.DMA((2,)),
        ],
    )
    came_one = exchange(send_one)


    half_groups = shards // 2
    half_total = matrix_total // 2
    assert half_groups * 2 == shards and shards & (shards - 1) == 0
    assert all(
        (matrix >= half_total) == (group >= half_groups)
        for group in range(shards)
        for matrix in slot_matrix[group]
    )
    slot_table = np.full((shards, slots), -1, np.int32)
    for group in range(shards):
        slot_table[group, : len(slot_matrix[group])] = slot_matrix[group]
    slot_table = jnp.asarray(slot_table.reshape(-1))


    def pack_moments(
        owner_ref,
        second_ref,
        first_ref,
        grad_ref,
        basis_ref,
        out_ref,
        new_ref,
        table_ref,
        count_ref,
        stage_ref,
        line_ref,
    ):
        fill_owned_table(owner_ref, table_ref, count_ref)
        basis = basis_ref[:, 0, :]
        for matrix in range(matrix_total):
            stage_ref[matrix] = basis[:, matrix * columns : (matrix + 1) * columns]
        send_owned(stage_ref, table_ref, out_ref, 0)
        send_tiles(second_ref, line_ref, out_ref, owned_rows)
        send_tiles(first_ref, line_ref, out_ref, owned_rows + tile_rows)
        new_ref[...] = 0.9 * first_ref[...] + 0.1 * grad_ref[...]

    vmem = pl.BlockSpec(memory_space=pltpu.VMEM)
    send_two, first_out, owned_table = call(
        pack_moments,
        [
            (shards, owned_rows + 2 * tile_rows, LANES),
            dense,
            jax.ShapeDtypeStruct((shards * MCAP,), jnp.int32),
        ],
        (
            owners,
            second_moment.reshape(dense),
            first_moment.reshape(dense),
            grad_dense,
            left_basis,
        ),
        specs=[SMEM, None, None, None, None],
        out_specs=[vmem, vmem, SMEM],
        scratch=[count_scratch, stage_scratch, line_scratch],
    )
    came_one, send_two = together((came_one, send_two))
    came_two = exchange(send_two)


    def gram_partials(
        group_ref, rank_ref, edges_ref, came_ref, grad_ref, strips_ref, kept_ref, core_ref, turned_ref
    ):
        unpack_columns(came_ref, strip_rows, grad_ref, shards, rows, share)
        for source in range(shards):
            strips_ref[source] = came_ref[source, 0:strip_rows, :]
        turned_ref[...] = jnp.zeros_like(turned_ref)
        for rank in range(ranks):
            turned_ref[rank * LANES : rank * LANES + columns, :] = grad_ref[
                rank * columns : (rank + 1) * columns, :
            ]
        right = parts_of(turned_ref[...])
        grams = []
        for mask in slot_masks(group_ref, edges_ref):
            left = parts_of(jnp.where(mask, grad_ref[...], 0.0))
            grams.append(product(left, right, (1, 1)))
        odd = rank_ref[0] % 2 == 1
        for chip in range(2):
            for group in range(shards):
                at = slice(group * rows, (group + 1) * rows)
                low = [g[at, 2 * chip * LANES : 2 * chip * LANES + columns] for g in grams]
                high = [g[at, (2 * chip + 1) * LANES : (2 * chip + 1) * LANES + columns] for g in grams]
                low, high = jnp.concatenate(low, axis=1), jnp.concatenate(high, axis=1)
                mine, other = jnp.where(odd, high, low), jnp.where(odd, low, high)
                store_block(kept_ref.at[chip], group, 0, mine, rows, strip)
                store_block(core_ref.at[chip], group, 0, other, rows, strip)

    strip_shape = (shards, strip_rows, LANES)
    grad_full, strips_own, kept, for_core = call(
        gram_partials,
        [(width, wide), strip_shape, (2,) + strip_shape, (2,) + strip_shape],
        (group_arg, rank_arg, edge_table, came_one),
        specs=[SMEM, SMEM, SMEM, None],
        scratch=[pltpu.VMEM((ranks * LANES, wide), F32)],
    )


    def add_core(rank_ref, kept_ref, came_ref, mine_ref, far_ref):
        chip = rank_ref[0] // 2
        mine_ref[...] = kept_ref[chip] + came_ref[chip]
        far_ref[...] = kept_ref[1 - chip] + came_ref[1 - chip]

    gram_mine, for_chip = call(
        add_core,
        [strip_shape, strip_shape],
        (rank_arg, kept, over_core(for_core)),
        specs=[SMEM, None, None],
    )
    came_chip = over_chip(for_chip)


    def sum_strips(group_ref, mine_ref, came_ref, *out_refs):
        place = group_ref[0] % half_groups
        for k, out_ref in enumerate(out_refs):
            for j in range(2):
                at = (place ^ k) + j * half_groups
                out_ref[j] = mine_ref[at] + came_ref[at]

    gram_blocks = call(
        sum_strips,
        [(2, strip_rows, LANES)] * half_groups,
        (group_arg, gram_mine, came_chip),
        specs=[SMEM, None, None],
    )
    *gram_blocks, strips_own = together((*gram_blocks, strips_own))
    gram_blocks = [gram_blocks[0]] + [
        lax.ppermute(gram_blocks[k], "shard", [(s, s ^ k) for s in range(shards)])
        for k in range(1, half_groups)
    ]


    strips_chip = over_chip(strips_own)
    *late, strips_chip = together((*gram_blocks[half_groups // 2 :], strips_chip))
    gram_blocks = gram_blocks[: half_groups // 2] + late


    def split_owned(rank_ref, came_ref, *refs):
        spread = len(refs) == 3
        mine_ref, other_ref = refs[-2:]
        odd = rank_ref[0] % 2 == 1
        for block_at in range(shards):
            at = slice(block_at * rows, (block_at + 1) * rows)
            if spread:
                place, base = block_at % half_groups, block_at // half_groups * owned_rows
                block = load_block(came_ref, place, base, rows, owned) + load_block(
                    came_ref, half_groups + place, base, rows, owned
                )
            else:
                block = load_block(came_ref, block_at, 0, rows, owned)
            strips = [block[:, m * columns : (m + 1) * columns] for m in range(MCAP)]
            mine_ref[at, 0:columns] = jnp.where(odd, strips[1], strips[0])
            other_ref[at, 0:columns] = jnp.where(odd, strips[0], strips[1])
            if spread:
                for m in range(MCAP):
                    refs[0][m, at, 0:columns] = strips[m]

    def join_half(rank_ref, mine_ref, other_ref, half_ref):
        odd = rank_ref[0] % 2 == 1
        for group in range(shards):
            at = slice(group * rows, (group + 1) * rows)
            mine, other = mine_ref[at, 0:columns], other_ref[at, 0:columns]
            both = [jnp.where(odd, other, mine), jnp.where(odd, mine, other)]
            store_block(half_ref, group, 0, jnp.concatenate(both, axis=1), rows, owned)

    def collect(came, spread):
        *strips, mine, other = call(
            split_owned,
            [(MCAP, width, LANES)] * spread + [(width, LANES), (width, LANES)],
            (rank_arg, came),
            specs=[SMEM, None],
        )
        half = call(
            join_half,
            (shards, owned_rows, LANES),
            (rank_arg, mine, over_core(other)),
            specs=[SMEM, None, None],
        )
        return *strips, half, over_chip(half)


    def add_blocks(group_ref, slot_ref, came, first, stage_ref):
        for k, came_ref in enumerate(came):
            for j in range(2):
                block = load_block(came_ref, j, 0, rows, strip)
                for m in range(slots):
                    matrix = slot_ref[(group_ref[0] ^ (first + k)) * slots + m]
                    at = jnp.where(matrix >= 0, matrix, matrix_total)
                    part = block[:, m * columns : (m + 1) * columns]
                    stage_ref[j, at] = stage_ref[j, at] + 0.05 * part

    def early_grams(group_ref, slot_ref, gram_ref, *refs):
        came, stage_ref = refs[:-1], refs[-1]
        half = group_ref[0] // half_groups
        stage_ref[...] = jnp.zeros_like(stage_ref)
        old = 0.95 * gram_ref[:, 0, :]
        for matrix in range(matrix_total):
            stage_ref[half, matrix] = old[:, matrix * columns : (matrix + 1) * columns]
        add_blocks(group_ref, slot_ref, came, 0, stage_ref)

    early_blocks = half_groups // 2
    stage_shape = (2, matrix_total + 1, rows, columns)
    early_stage = call(
        early_grams,
        stage_shape,
        (group_arg, slot_table, left_gram, *gram_blocks[:early_blocks]),
        specs=[SMEM, SMEM] + [None] * (1 + early_blocks),
    )

    def new_grams(group_ref, table_ref, slot_ref, *refs):
        early_ref, *came, out_ref, stage_ref = refs
        stage_ref[...] = early_ref[...]
        add_blocks(group_ref, slot_ref, came, early_blocks, stage_ref)
        for dest in range(shards):
            for j in range(2):
                held = []
                for m in range(MCAP):
                    matrix = table_ref[dest * MCAP + m]
                    block = stage_ref[j, jnp.maximum(matrix, 0)]
                    held.append(jnp.where(matrix >= 0, block, 0.0))
                block = jnp.concatenate(held, axis=1)
                store_block(out_ref, dest, j * owned_rows, block, rows, owned)

    send_four = call(
        new_grams,
        (shards, 2 * owned_rows, LANES),
        (group_arg, owned_table, slot_table, early_stage, *gram_blocks[early_blocks:]),
        specs=[SMEM, SMEM, SMEM] + [None] * (1 + half_groups - early_blocks),
        scratch=[pltpu.VMEM(stage_shape, F32)],
    )
    send_four = in_hbm(send_four)
    came_two, send_four = together((came_two, send_four))
    came_four = in_hbm(exchange(send_four))
    pair = over_core(jnp.stack([strips_own, strips_chip]))


    def rotate_gradient(
        group_ref,
        rank_ref,
        edges_ref,
        own_ref,
        chip_ref,
        pair_ref,
        grad_ref,
        basis_ref,
        hat_ref,
    ):
        rank = rank_ref[0]
        for group in range(shards):
            blocks = [
                load_block(ref, group, 0, rows, strip)
                for ref in (own_ref, pair_ref.at[0], chip_ref, pair_ref.at[1])
            ]
            at = slice(group * rows, (group + 1) * rows)
            for k in range(slots):
                cut = [block[:, k * columns : (k + 1) * columns] for block in blocks]
                low = [jnp.where(rank % 2 == 0, cut[0 + h], cut[1 + h]) for h in (0, 2)]
                odd = [jnp.where(rank % 2 == 0, cut[1 + h], cut[0 + h]) for h in (0, 2)]
                first = rank < 2
                ordered = [
                    jnp.where(first, low[0], low[1]),
                    jnp.where(first, odd[0], odd[1]),
                    jnp.where(first, low[1], low[0]),
                    jnp.where(first, odd[1], odd[0]),
                ]
                basis_ref[k, at, :] = jnp.concatenate(ordered, axis=1)
        grad = thirds_of(grad_ref[...])
        hat = jnp.zeros((width, wide), F32)
        for k, mask in enumerate(slot_masks(group_ref, edges_ref)):
            hat = jnp.where(mask, fine_product(thirds_of(basis_ref[k].T), grad), hat)
        hat_ref[...] = hat

    basis_full, hat_full = call(
        rotate_gradient,
        [(slots, width, width), (width, wide)],
        (group_arg, rank_arg, edge_table, strips_own, strips_chip, pair, grad_full),
        specs=[SMEM, SMEM, SMEM] + [None] * 4,
    )

    basis_half, basis_far = collect(came_two, 0)


    def directions(
        group_ref,
        edges_ref,
        came_ref,
        grad_ref,
        hat_ref,
        basis_ref,
        send_ref,
        moment_ref,
        second_ref,
    ):
        unpack_columns(came_ref, owned_rows, second_ref, shards, rows, share)
        second_ref[...] = 0.95 * second_ref[...] + 0.05 * hat_ref[...] * hat_ref[...]
        unpack_columns(came_ref, owned_rows + tile_rows, moment_ref, shards, rows, share)
        masks = slot_masks(group_ref, edges_ref)
        moment = thirds_of(0.9 * moment_ref[...] + 0.1 * grad_ref[...])
        hat = jnp.zeros((width, wide), F32)
        for k, mask in enumerate(masks):
            hat = jnp.where(mask, fine_product(thirds_of(basis_ref[k].T), moment), hat)
        step = parts_of(adam_direction(hat, second_ref[...]))
        turned = jnp.zeros((width, wide), F32)
        for k, mask in enumerate(masks):
            turned = jnp.where(mask, product(parts_of(basis_ref[k]), step), turned)
        moment_ref[...] = turned
        pack_columns(moment_ref, send_ref, 0, shards, rows, share)
        pack_columns(second_ref, send_ref, tile_rows, shards, rows, share)

    send_five = call(
        directions,
        (shards, 2 * tile_rows, LANES),
        (group_arg, edge_table, came_two, grad_full, hat_full, basis_full),
        specs=[SMEM, SMEM] + [None] * 4,
        scratch=[pltpu.VMEM((width, wide), F32)] * 2,
    )
    came_four, send_five = together((came_four, send_five))
    came_five = exchange(send_five)


    gram_strips, gram_half, gram_far = collect(came_four, 1)

    def turn_strips(strips_ref, out_ref):
        for m in range(MCAP):
            out_ref[m] = strips_ref[m].T[0:columns]

    gram_out = call(turn_strips, (MCAP, columns, width), (gram_strips,))

    def refresh(
        rank_ref,
        basis_half_ref,
        basis_far_ref,
        gram_half_ref,
        gram_far_ref,
        weight_ref,
        mine_ref,
        other_ref,
        weight_out_ref,
        basis_ref,
        gram_ref,
        sem,
    ):
        fetch = pltpu.make_async_copy(weight_ref, weight_out_ref, sem)
        fetch.start()
        rank = rank_ref[0]
        first = rank < 2
        for out, half_ref, far_ref in (
            (basis_ref, basis_half_ref, basis_far_ref),
            (gram_ref, gram_half_ref, gram_far_ref),
        ):
            for group in range(shards):
                half = load_block(half_ref, group, 0, rows, owned)
                far = load_block(far_ref, group, 0, rows, owned)
                both = [jnp.where(first, half, far), jnp.where(first, far, half)]
                out[group * rows : (group + 1) * rows, :] = jnp.concatenate(both, axis=1)
        power = product(parts_of(basis_ref[...].T), parts_of(gram_ref[...]))
        frame = power / jnp.sqrt(jnp.sum(power * power) + 1e-06)
        for _ in range(NS_STEPS):
            pieces = parts_of(frame)
            square = product(pieces, pieces, (1, 1))
            frame = 1.5 * frame - 0.5 * product(parts_of(square), pieces)
        strips = [frame[r * columns : (r + 1) * columns] for r in range(ranks)]
        low = jnp.where(first, strips[0], strips[2])
        odd = jnp.where(first, strips[1], strips[3])
        even_core = rank % 2 == 0
        mine_ref[...] = jnp.where(even_core, low, odd)
        other_ref[...] = jnp.where(even_core, odd, low)
        fetch.wait()

    weight_dense = in_hbm(weight.reshape(dense))
    frame_mine, frame_other, weight_near = call(
        refresh,
        [(columns, width), (columns, width), dense],
        (rank_arg, basis_half, basis_far, gram_half, gram_far, weight_dense),
        specs=[SMEM] + [None] * 4 + [HBM],
        scratch=[pltpu.VMEM((width, width), F32)] * 2 + [pltpu.SemaphoreType.DMA(())],
    )
    frame_came = over_core(frame_other)
    pair_out = jnp.where(
        my_rank % 2 == 0,
        jnp.stack([frame_mine, frame_came]),
        jnp.stack([frame_came, frame_mine]),
    )
    came_five, pair_out, gram_out, first_out = together((came_five, pair_out, gram_out, first_out))


    steps = 2 if rows % 16 == 0 else 1
    step_rows = rows // steps
    step_dense = (step_rows * line_tiles, LANES)

    def line_from(came_ref, base, part, line_ref, ref):
        for group in range(shards):
            block = load_block(came_ref, group, base, rows, share)
            block = block[part * step_rows : (part + 1) * step_rows]
            offset = 0
            for _, at, length in groups[group]:
                line_ref[:, at : at + length] = block[:, offset : offset + length]
                offset += length
        for j in range(line_tiles):
            ref[pl.ds(j, step_rows, stride=line_tiles), :] = line_ref[:, j * LANES : (j + 1) * LANES]

    def take_back(came_ref, weight_ref, weight_out_ref, second_out_ref, line_ref):
        for part in range(steps):

            @pl.when(pl.program_id(0) == part)
            def _():
                line_from(came_ref, 0, part, line_ref, weight_out_ref)
                old = weight_ref[...]
                weight_out_ref[...] = old - 0.01 * (weight_out_ref[...] + 0.1 * old)
                line_from(came_ref, tile_rows, part, line_ref, second_out_ref)

    part_spec = pl.BlockSpec(step_dense, lambda i: (i, 0))
    weight_out, second_out = call(
        take_back,
        [dense, dense],
        (came_five, weight_near),
        specs=[None, part_spec],
        out_specs=[part_spec, part_spec],
        grid=(steps,),
        scratch=[pltpu.VMEM((step_rows, line), F32)],
    )

    bias_first_new = 0.9 * bias_first + 0.1 * bias_gradient
    bias_second_new = 0.95 * bias_second + 0.05 * bias_gradient * bias_gradient
    bias_updated = bias_weight - 0.01 * adam_direction(bias_first_new, bias_second_new)
    flat = (rows, 1, line)
    return (
        weight_out.reshape(flat),
        first_out.reshape(flat),
        second_out.reshape(flat),
        pair_out.transpose(0, 2, 1)[None],
        gram_out.transpose(0, 2, 1)[None],
        bias_updated,
        bias_first_new,
        bias_second_new,
    )


def solution(mesh):
    tiles = P("shard", "tensor", None)
    bias = P(("shard", "tensor"))
    owned = P("shard", None, None, "tensor")
    in_specs = (tiles,) * 6 + (P(),) + (bias,) * 4
    out_specs = (tiles,) * 3 + (owned,) * 2 + (bias,) * 3
    return jax.shard_map(body, mesh=mesh, in_specs=in_specs, out_specs=out_specs, check_vma=False)
```
